32 devices in a mesh: narrow: 4 (over z), wide: 8 (over y, x, core).
Axes of the slice: x: 2, y: 2, z: 4, core: 2. Of those that a mesh axis runs over, the one named last changes fastest.
Arguments:
- pixels: int32 [12, 262144], P(None, ('narrow', 'wide')), may hold values from 0 to 255
- noise: float32 [12, 262144], P(None, ('narrow', 'wide')), may hold values from 0 to 1
- depth: int32 [1024], P(('narrow', 'wide')), may hold values from 5 to 8, as said below
- step_count: int32 [], replicated, may hold values from 2 to 20
- conv_in: float32 [2, 512, 54], P(None, 'wide'), may hold values from -0.4082483 to 0.4082483
- conv_mid: float32 [2, 512, 512], P(None, 'wide'), may hold values from -0.13258252 to 0.13258252
- conv_out: float32 [2, 108, 512], P(None, None, 'wide'), may hold values from -0.044194174 to 0.044194174
- hidden_bias: float32 [2, 2, 512], P(None, None, 'wide'), may hold values from -1.5 to 1.5
- flow_small: float32 [2, 12, 15], replicated, may hold values from -0.3 to 0.3
- prior_conv: float32 [12, 55], replicated, may hold values from -0.12 to 0.12
- mean_in: float32 [2, 512, 54], P(None, 'wide'), may hold values from -3.8146973e-06 to 3.8146973e-06
- mean_mid: float32 [2, 512, 512], P(None, 'wide'), may hold values from -6.67572e-06 to 6.67572e-06
- mean_out: float32 [2, 108, 512], P(None, None, 'wide'), may hold values from -7.6293945e-05 to 7.6293945e-05
- mean_bias: float32 [2, 2, 512], P(None, None, 'wide'), may hold values from -9.536743e-06 to 9.536743e-06
- mean_small: float32 [2, 12, 15], replicated, may hold values from -0.0625 to 0.0625
- mean_prior: float32 [12, 55], replicated, may hold values from -0.03125 to 0.03125
- square_in: float32 [2, 512, 54], P(None, 'wide'), may hold values from 1.953125e-14 to 3.125e-13
- square_mid: float32 [2, 512, 512], P(None, 'wide'), may hold values from 4.3945313e-14 to 7.03125e-13
- square_out: float32 [2, 108, 512], P(None, None, 'wide'), may hold values from 7.8125e-12 to 1.25e-10
- square_bias: float32 [2, 2, 512], P(None, None, 'wide'), may hold values from 1.2207031e-13 to 1.953125e-12
- square_small: float32 [2, 12, 15], replicated, may hold values from 5e-06 to 8e-05
- square_prior: float32 [12, 55], replicated, may hold values from 1.25e-06 to 2e-05
Outputs:
- loss: float32 [], replicated
- new_conv_in: float32 [2, 512, 54], P(None, 'wide')
- new_mean_in: float32 [2, 512, 54], P(None, 'wide')
- new_square_in: float32 [2, 512, 54], P(None, 'wide')
- new_conv_mid: float32 [2, 512, 512], P(None, 'wide')
- new_mean_mid: float32 [2, 512, 512], P(None, 'wide')
- new_square_mid: float32 [2, 512, 512], P(None, 'wide')
- new_conv_out: float32 [2, 108, 512], P(None, None, 'wide')
- new_mean_out: float32 [2, 108, 512], P(None, None, 'wide')
- new_square_out: float32 [2, 108, 512], P(None, None, 'wide')
- new_hidden_bias: float32 [2, 2, 512], P(None, None, 'wide')
- new_mean_bias: float32 [2, 2, 512], P(None, None, 'wide')
- new_square_bias: float32 [2, 2, 512], P(None, None, 'wide')
- new_flow_small: float32 [2, 12, 15], replicated
- new_mean_small: float32 [2, 12, 15], replicated
- new_square_small: float32 [2, 12, 15], replicated
- new_prior_conv: float32 [12, 55], replicated
- new_mean_prior: float32 [12, 55], replicated
- new_square_prior: float32 [12, 55], replicated
The draws below stay inside these ranges and needn't reach their ends.
Inputs may be any that keep to these rules, and one draw needn't show every extreme that they name: `depth`: each entry is 5 or 8; the share of 5 rises with the image index from about a tenth to about nine tenths; the first image has 8, the last 5.
All inputs are finite; a program needn't handle non-finite values.
Results may differ from the reference program's by a relative error of at most 0.00085.
The reference program's roundings to bfloat16 on the way count: a program that leaves them out, or rounds other values in their place, can miss the bound.
Values may be sent and summed in bfloat16 or wider, within the bound.
A program may use at most 192 MiB of HBM per device.

```python
import math
import jax
import jax.numpy as jnp
from jax import lax

HID = 512
LAYERS = 2
IMAGES = 1024
PIXELS = 262144


def draw_pixels(key, part):
    key = jax.random.fold_in(key, 5)
    image = jnp.arange(PIXELS, dtype=jnp.int32) // 256
    reach = (40 + 88 * image // (IMAGES - 1)).astype(jnp.int32)
    offsets = jax.random.randint(key, (12, PIXELS), -reach[None, :], reach[None, :] + 1)
    values = jnp.clip(128 + offsets, 0, 255).astype(jnp.int32)
    values = values.at[0, PIXELS - 1].set(0)
    values = values.at[1, PIXELS - 1].set(255)
    return values.astype(jnp.int32)


def draw_depth(key, part):
    key = jax.random.fold_in(key, 7)
    index = jnp.arange(IMAGES, dtype=jnp.int32)
    limit = 100 + 800 * index // (IMAGES - 1)
    rolls = jax.random.randint(key, (IMAGES,), 0, 1000)
    values = jnp.where(rolls < limit, 5, 8).astype(jnp.int32)
    values = values.at[0].set(8)
    values = values.at[IMAGES - 1].set(5)
    return values.astype(jnp.int32)


def bounded_normal(key, shape, scale):
    values = jax.random.truncated_normal(key, -3.0, 3.0, shape, jnp.float32)
    return (values * scale).astype(jnp.float32)


def draw_conv_in(key, part):
    key = jax.random.fold_in(key, 11)
    return bounded_normal(key, (LAYERS, HID, 54), 54.0 ** (-0.5))


def draw_conv_mid(key, part):
    key = jax.random.fold_in(key, 12)
    return bounded_normal(key, (LAYERS, HID, HID), float(HID) ** (-0.5))


def draw_conv_out(key, part):
    key = jax.random.fold_in(key, 13)
    return bounded_normal(key, (LAYERS, 108, HID), float(9 * HID) ** (-0.5))


def draw_hidden_bias(key, part):
    key = jax.random.fold_in(key, 14)
    return bounded_normal(key, (LAYERS, 2, HID), 0.5)


def draw_prior_conv(key, part):
    key = jax.random.fold_in(key, 15)
    return bounded_normal(key, (12, 55), 0.04)


def steps_of(stream_key, extent, cuts, smallest, top_value):
    def one(dim, shards_of):
        heights = jax.random.uniform(jax.random.fold_in(jax.random.fold_in(stream_key, 6), dim), (shards_of,), jnp.float32, smallest / len(cuts), top_value / len(cuts))
        return jnp.repeat(jnp.exp(heights), extent[dim] // shards_of).reshape((-1,) + (1,) * (len(extent) - dim - 1))

    loudness = one(*cuts[0])
    for cut in cuts[1:]:
        loudness = loudness * one(*cut)
    return loudness


def centred(key, shape, spread, most, pieces=(), kind=jnp.bfloat16):
    result = spread * jax.random.normal(key, shape, jnp.float32)
    if pieces:
        result = result * steps_of(key, shape, pieces, -0.22, 0.18)
    return jnp.clip(result, -most, most).astype(kind)


def setup_inputs(seed: int = 0) -> dict:
    key_of = jax.random.split(jax.random.key(seed), 23)
    return {
        "pixels": draw_pixels(jax.random.fold_in(key_of[22], 71), 0),
        "noise": jnp.clip(1.0 * jax.random.uniform(key_of[1], (12, PIXELS), jnp.float32) ** steps_of(key_of[1], (12, PIXELS), ((1, 32),), -0.2, 0.2), 0.0, 1.0),
        "depth": draw_depth(jax.random.fold_in(key_of[22], 71), 0),
        "step_count": jax.random.randint(key_of[3], (), 2, 21).astype(jnp.int32),
        "conv_in": draw_conv_in(jax.random.fold_in(key_of[22], 71), 0),
        "conv_mid": draw_conv_mid(jax.random.fold_in(key_of[22], 71), 0),
        "conv_out": draw_conv_out(jax.random.fold_in(key_of[22], 71), 0),
        "hidden_bias": draw_hidden_bias(jax.random.fold_in(key_of[22], 71), 0),
        "flow_small": jnp.clip(jax.random.uniform(key_of[8], (LAYERS, 12, 15), jnp.float32, -0.3, 0.3), -0.3, 0.3),
        "prior_conv": draw_prior_conv(jax.random.fold_in(key_of[22], 71), 0),
        "mean_in": centred(key_of[10], (LAYERS, HID, 54), (0.000022 / IMAGES ** 0.5), 3.814697265625e-06, ((1, 8),), jnp.float32),
        "mean_mid": centred(key_of[11], (LAYERS, HID, HID), (0.000033 / IMAGES ** 0.5), 6.67572021484375e-06, ((1, 8),), jnp.float32),
        "mean_out": centred(key_of[12], (LAYERS, 108, HID), (0.00044 / IMAGES ** 0.5), 7.62939453125e-05, ((2, 8),), jnp.float32),
        "mean_bias": centred(key_of[13], (LAYERS, 2, HID), (0.000055 / IMAGES ** 0.5), 9.5367431640625e-06, ((2, 8),), jnp.float32),
        "mean_small": centred(key_of[14], (LAYERS, 12, 15), 0.011, 0.0625, (), jnp.float32),
        "mean_prior": centred(key_of[15], (12, 55), 0.0055, 0.03125, (), jnp.float32),
        "square_in": jnp.clip(jnp.exp(math.log(3.124999987513116e-13) - 2.7725887 * jax.random.uniform(key_of[16], (LAYERS, HID, 54), jnp.float32) ** steps_of(key_of[16], (LAYERS, HID, 54), ((1, 8),), -0.2, 0.2)), 1.9531249921956977e-14, 3.124999987513116e-13),
        "square_mid": jnp.clip(jnp.exp(math.log(7.031250039667147e-13) - 2.7725887 * jax.random.uniform(key_of[17], (LAYERS, HID, HID), jnp.float32) ** steps_of(key_of[17], (LAYERS, HID, HID), ((1, 8),), -0.2, 0.2)), 4.394531274791967e-14, 7.031250039667147e-13),
        "square_out": jnp.clip(jnp.exp(math.log(1.2499999646475857e-10) - 2.7725887 * jax.random.uniform(key_of[18], (LAYERS, 108, HID), jnp.float32) ** steps_of(key_of[18], (LAYERS, 108, HID), ((2, 8),), -0.2, 0.2)), 7.81249977904741e-12, 1.2499999646475857e-10),
        "square_bias": jnp.clip(jnp.exp(math.log(1.9531249447618526e-12) - 2.7725887 * jax.random.uniform(key_of[19], (LAYERS, 2, HID), jnp.float32) ** steps_of(key_of[19], (LAYERS, 2, HID), ((2, 8),), -0.2, 0.2)), 1.220703090476158e-13, 1.9531249447618526e-12),
        "square_small": jnp.clip(jnp.exp(jax.random.uniform(key_of[20], (LAYERS, 12, 15), jnp.float32, math.log(4.999999873689376e-06), math.log(7.999999797903001e-05))), 4.999999873689376e-06, 7.999999797903001e-05),
        "square_prior": jnp.clip(jnp.exp(jax.random.uniform(key_of[21], (12, 55), jnp.float32, math.log(1.249999968422344e-06), math.log(1.9999999494757503e-05))), 1.249999968422344e-06, 1.9999999494757503e-05),
    }


@jax.custom_vjp
def low(v):
    return lax.optimization_barrier(v.astype(jnp.bfloat16)).astype(jnp.float32)

@jax.custom_vjp
def low_back(v):
    return v

def low_keep(v):
    return (low(v), None)

def low_pass(kept, grad):
    return (grad,)

def back_keep(v):
    return (v, None)

def back_low(kept, grad):
    return (low(grad),)
low.defvjp(low_keep, low_pass)
low_back.defvjp(back_keep, back_low)
highest = lax.Precision.HIGHEST
learn_rate = 0.02
beta_one = 0.9
beta_two = 0.999
epsilon = 1e-08
decay_rate = 0.01
penalty_weight = 0.5
tap_offsets = [(row_step, col_step) for row_step in (-1, 0, 1) for col_step in (-1, 0, 1)]

def tap_mask(count, row_step, col_step):
    index = jnp.arange(count, dtype=jnp.int32)
    row = index // 16 % 16
    column = index % 16
    return (row + row_step >= 0) & (row + row_step < 16) & (column + col_step >= 0) & (column + col_step < 16)

def shifted(values, row_step, col_step):
    moved = jnp.roll(values, -(16 * row_step + col_step), axis=1)
    return jnp.where(tap_mask(values.shape[1], row_step, col_step)[None, :], moved, jnp.zeros_like(moved))

def all_taps(values):
    return jnp.concatenate([shifted(values, row_step, col_step) for row_step, col_step in tap_offsets], axis=0)

def dequantize(pixels, noise, depth):
    coarse = jnp.repeat(depth, 256) == 5
    divisor = jnp.where(coarse, 8, 1).astype(jnp.int32)
    levels = jnp.where(coarse, 32.0, 256.0).astype(jnp.float32)
    quant = (pixels // divisor[None, :]).astype(jnp.float32)
    return (quant + noise) / levels[None, :] - 0.5

def mixing_matrix(lu_part):
    lower = jnp.tril(lu_part, -1) + jnp.eye(12, dtype=lu_part.dtype)
    upper = jnp.triu(lu_part, 1) + jnp.diag(jnp.exp(jnp.diag(lu_part)))
    return jnp.dot(lower, upper, precision=highest)[::-1]

def prepare(state, small):
    lu_part = small[:, 0:12]
    moved = (state + small[:, 12:13]) * jnp.exp(small[:, 13:14])
    mixed = jnp.dot(mixing_matrix(lu_part), moved, precision=highest)
    logdet = state.shape[1] * (jnp.sum(small[:, 13]) + jnp.sum(jnp.diag(lu_part)))
    return (mixed, logdet)

def prior_logp(latent, prior):
    first = latent[0:6]
    rest = latent[6:12]
    stats = jnp.dot(prior[:, 0:54], all_taps(first), precision=highest) + prior[:, 54:55]
    centre = stats[0:6]
    log_sd = stats[6:12]
    gauss = -0.5 * first * first - 0.5 * jnp.square((rest - centre) * jnp.exp(-log_sd)) - log_sd
    return jnp.sum(gauss) - latent.shape[1] * 6.0 * math.log(2.0 * math.pi)

def flow_layer(state, small, conv_first, conv_second, conv_third, biases):
    mixed, logdet = prepare(state, small)
    kept = mixed[0:6]
    other = mixed[6:12]
    stacked = all_taps(low(kept))
    first = low_back(jnp.dot(low(conv_first), stacked, precision=highest) + low(biases[0])[:, None])
    hidden_one = low(jax.nn.relu(first))
    second = low_back(jnp.dot(low(conv_second), hidden_one, precision=highest) + low(biases[1])[:, None])
    hidden_two = low(jax.nn.relu(second))
    taps_out = jnp.dot(low(conv_third), hidden_two, precision=highest)
    summed = shifted(taps_out[0:12], tap_offsets[0][0], tap_offsets[0][1])
    for index in range(1, 9):
        summed = summed + shifted(taps_out[12 * index:12 * index + 12], tap_offsets[index][0], tap_offsets[index][1])
    output = low_back(summed) + small[:, 14:15]
    scale = jax.nn.sigmoid(output[6:12] + 2.0)
    other_new = (other + output[0:6]) * scale
    logdet = logdet + jnp.sum(jnp.log(scale))
    return (jnp.concatenate([kept, other_new], axis=0), logdet)

def total_loss(params, blocks):
    conv_in, conv_mid, conv_out, hidden_bias, flow_small, prior_conv = params

    def block_fn(carry, state):
        logdet = jnp.zeros((), jnp.float32)
        for layer in range(LAYERS):
            state, term = flow_layer(state, flow_small[layer], conv_in[layer], conv_mid[layer], conv_out[layer], hidden_bias[layer])
            logdet = logdet + term
        likely = prior_logp(state, prior_conv) + logdet
        return ((carry[0] + likely, carry[1] + lax.optimization_barrier(jnp.sum(state, axis=1)), carry[2] + lax.optimization_barrier(jnp.sum(state * state, axis=1))), None)
    start = (jnp.zeros((), jnp.float32), jnp.zeros((12,), jnp.float32), jnp.zeros((12,), jnp.float32))
    (likely, first_sum, square_sum), _ = lax.scan(jax.checkpoint(block_fn), start, blocks)
    total = blocks.shape[0] * blocks.shape[2]
    mean = first_sum / total
    var = square_sum / total - mean * mean
    penalty = penalty_weight * jnp.sum(mean * mean + jnp.square(var - 1.0))
    return -likely / (total * 12 * math.log(2.0)) + penalty

def adamw(weight, grad, first, second, step):
    first_new = beta_one * first + (1.0 - beta_one) * grad
    second_new = beta_two * second + (1.0 - beta_two) * grad * grad
    fix_one = 1.0 - jnp.power(beta_one, step)
    fix_two = 1.0 - jnp.power(beta_two, step)
    update = first_new / fix_one / (jnp.sqrt(second_new / fix_two) + epsilon) + decay_rate * weight
    return (weight - learn_rate * update, first_new, second_new)

def reference(pixels, noise, depth, step_count, conv_in, conv_mid, conv_out, hidden_bias, flow_small, prior_conv, mean_in, mean_mid, mean_out, mean_bias, mean_small, mean_prior, square_in, square_mid, square_out, square_bias, square_small, square_prior):
    state = dequantize(pixels, noise, depth)
    count = IMAGES // 16
    blocks = state.reshape(12, count, 4096).transpose(1, 0, 2)
    params = (conv_in, conv_mid, conv_out, hidden_bias, flow_small, prior_conv)
    value, pull = jax.vjp(lambda items: total_loss(items, blocks), params)
    grads = pull(jnp.ones((), value.dtype))[0]
    loss = value + jnp.mean(depth.astype(jnp.float32))
    step = step_count.astype(jnp.float32)
    firsts = (mean_in, mean_mid, mean_out, mean_bias, mean_small, mean_prior)
    seconds = (square_in, square_mid, square_out, square_bias, square_small, square_prior)
    results = [loss]
    for index in range(6):
        results.extend(adamw(params[index], grads[index], firsts[index], seconds[index], step))
    return tuple(results)
```

```python
import functools
import math

import jax
import jax.numpy as jnp
from jax import lax
from jax.experimental import pallas as pl
from jax.experimental.pallas import tpu as pltpu
from jax.sharding import PartitionSpec as P

f32 = jnp.float32
bf16 = jnp.bfloat16
highest = lax.Precision.HIGHEST
MESH = pl.DeviceIdType.MESH
learn_rate = 0.02
beta_one = 0.9
beta_two = 0.999
epsilon = 1e-08
decay_rate = 0.01
penalty_weight = 0.5
tap_offsets = [(r, c) for r in (-1, 0, 1) for c in (-1, 0, 1)]
TILE = 512
BACK = 512
OUT = 144
SMALL = 256
VMEM = pl.BlockSpec(memory_space=pltpu.VMEM)
SMEM = pl.BlockSpec(memory_space=pltpu.SMEM)


def dot(a, b, precision=None):
    return lax.dot_general(
        a, b, (((1,), (0,)), ((), ())), preferred_element_type=f32, precision=precision
    )


def dot_nt(a, b, precision=None):
    return lax.dot_general(
        a, b, (((1,), (1,)), ((), ())), preferred_element_type=f32, precision=precision
    )


def dot_tn(a, b, precision=None):
    return lax.dot_general(
        a, b, (((0,), (0,)), ((), ())), preferred_element_type=f32, precision=precision
    )


def iota(shape, axis):
    return lax.broadcasted_iota(jnp.int32, shape, axis)


def slot(s):
    return s + 2 * ((s * 10923) >> 16)


def spread(count, width, first=0):
    return jnp.where(slot(iota((count, width), 0) + first) == iota((count, width), 1), 1.0, 0.0)


def spread_rows(height, count):
    return jnp.where(slot(iota((height, count), 1)) == iota((height, count), 0), 1.0, 0.0)


def split_three(v):
    high = v.astype(bf16).astype(f32)
    rest = v - high
    middle = rest.astype(bf16).astype(f32)
    return high, middle, rest - middle


def as_row(column):
    n = column.shape[0]
    eye = iota((n, n), 0) == iota((n, n), 1)
    return jnp.sum(jnp.where(eye, column, 0.0), axis=0, keepdims=True)


def mixing_parts(lu):
    n = lu.shape[0]
    row, col = iota((n, n), 0), iota((n, n), 1)
    lower = jnp.where(row > col, lu, 0.0) + jnp.where(row == col, 1.0, 0.0)
    upper = jnp.where(row < col, lu, 0.0) + jnp.where(row == col, jnp.exp(lu), 0.0)
    return lower, upper


def wide_rows(v, lanes):
    return jnp.concatenate([v] * (lanes // 128), axis=1)


class Shifts:
    def __init__(self, mask_ref, lanes):
        self.lanes = lanes
        self.masks = mask_ref

    def mask(self, which, rows):
        m = self.masks[which, :, 0 : self.lanes]
        return jnp.concatenate([m] * (rows // 8), axis=0) if rows > 8 else m

    def col(self, v, c):
        if c == 0:
            return v
        moved = pltpu.roll(v, (-c) % self.lanes, 1)
        return moved * self.mask(0 if c > 0 else 1, v.shape[0])

    def row(self, v, r):
        if r == 0:
            return v
        moved = pltpu.roll(v, (-16 * r) % self.lanes, 1)
        return moved * self.mask(2 if r > 0 else 3, v.shape[0])

    def taps(self, v, sign=1):
        by_col = {c: self.col(v, c) for c in (-1, 0, 1)}
        return [self.row(by_col[sign * c], sign * r) for r, c in tap_offsets]

    def fold(self, pieces, sign=1):
        total = None
        for c in (-1, 0, 1):
            part = None
            for r in (-1, 0, 1):
                piece = self.row(pieces[3 * (r + 1) + (c + 1)], sign * r)
                part = piece if part is None else part + piece
            part = self.col(part, sign * c)
            total = part if total is None else total + part
        return total


def fill_masks(mask_ref):
    lanes = mask_ref.shape[2]
    pos = iota((8, lanes), 1)
    row, col = (pos >> 4) & 15, pos & 15
    for which, keep in enumerate((col < 15, col > 0, row < 15, row > 0)):
        mask_ref[which] = jnp.where(keep, 1.0, 0.0)


def flow_kernel(
    wide,
    narrow,
    pixels_ref,
    noise_ref,
    depth_ref,
    small_ref,
    prior_ref,
    in_ref,
    mid_ref,
    out_ref,
    bias_ref,
    grad_ref,
    sums_ref,
    wall,
    wmt,
    wst,
    win,
    bone,
    mixes,
    mixes_back,
    prior_fwd,
    prior_back,
    masks,
    states,
    keep,
    taps_in,
    hidden_one,
    hidden_two,
    gz,
    stat_acc,
    like_acc,
    prior_acc,
    small_acc,
    bone_acc,
    gst,
    gall,
    rs_buf,
    nr_buf,
    st_wide,
    st_narrow,
    sm_wide,
    sm_narrow,
    ga_send,
    ga_recv,
    rs_send,
    rs_recv,
    nr_send,
    nr_recv,
    st_send,
    st_recv,
    sn_send,
    sn_recv,
    sw_send,
    sw_recv,
    so_send,
    so_recv,
):
    layers, share, hid = mid_ref.shape
    count = pixels_ref.shape[1]
    total = count * wide * narrow
    coeff = -1.0 / (total * 12 * math.log(2.0))
    me_w = lax.axis_index("wide") if wide > 1 else 0
    me_n = lax.axis_index("narrow") if narrow > 1 else 0

    def block(index):
        return pl.ds(pl.multiple_of(index * share, share), share)

    def peer(axis, size, me, d):
        return {axis: lax.rem(me + d, size)}

    def source(size, me, d):
        return lax.rem(me + size - d, size)

    def each(size, fn):
        if size > 1:
            lax.fori_loop(1, size, lambda d, c: (fn(d), c)[1], 0)

    def remote(src, dst, send, recv, device):
        return pltpu.make_async_remote_copy(
            src_ref=src, dst_ref=dst, send_sem=send, recv_sem=recv, device_id=device, device_id_type=MESH
        )

    if wide > 1:
        barrier = pltpu.get_barrier_semaphore()
        each(
            wide,
            lambda d: pl.semaphore_signal(
                barrier, inc=1, device_id=peer("wide", wide, me_w, d), device_id_type=MESH
            ),
        )
        each(
            narrow,
            lambda d: pl.semaphore_signal(
                barrier, inc=1, device_id=peer("narrow", narrow, me_n, d), device_id_type=MESH
            ),
        )

    place = spread(164, SMALL).astype(bf16)
    for layer in range(layers):
        small_part = (
            dot_tn(out_ref[layer].astype(bf16), place[0:108])
            + dot(in_ref[layer].astype(bf16), place[108:162])
            + dot_tn(bias_ref[layer].astype(bf16), place[162:164])
        )
        wall[layer, block(me_w), 0:hid] = mid_ref[layer].astype(bf16)
        wall[layer, block(me_w), hid : hid + SMALL] = small_part.astype(bf16)

    def gather(layer, d):
        mine = wall.at[layer, block(me_w)]
        return remote(
            mine, mine, ga_send.at[layer, d], ga_recv.at[layer, d], peer("wide", wide, me_w, d)
        )

    def gathered(layer, d):
        theirs = wall.at[layer, block(source(wide, me_w, d))]
        return remote(
            theirs, theirs, ga_send.at[layer, d], ga_recv.at[layer, d], peer("wide", wide, me_w, d)
        )

    if wide > 1:
        pl.semaphore_wait(barrier, wide + narrow - 2)
        for layer in range(layers):
            each(wide, lambda d: gather(layer, d).start())

    fill_masks(masks)
    to_slots = spread_rows(16, 12)
    reverse = jnp.where(slot(11 - iota((16, 12), 1)) == iota((16, 12), 0), 1.0, 0.0)
    for layer in range(layers):
        small = small_ref[layer]
        lower, upper = mixing_parts(small[:, 0:12])
        scale = jnp.exp(small[:, 13:14])
        mixed = dot(reverse, dot(lower, upper, highest), highest) * as_row(scale)
        const = jnp.sum(mixed * as_row(small[:, 12:13]), axis=1, keepdims=True)
        back = dot_nt(to_slots, mixed, highest)
        cb = jnp.sum(to_slots * as_row(small[:, 14:15]), axis=1, keepdims=True)
        for c in range(12):
            mixes[layer, c] = jnp.broadcast_to(mixed[:, c : c + 1], (16, 128))
            at = c + 2 * (c // 6)
            mixes_back[layer, c] = jnp.broadcast_to(back[:, at : at + 1], (16, 128))
        mixes[layer, 12] = jnp.broadcast_to(const, (16, 128))
        mixes[layer, 13] = jnp.broadcast_to(cb, (16, 128))

    prior = prior_ref[...]
    s = iota((55, 256), 0)
    at = iota((55, 256), 1)
    hit = (slot(s) == at) | (slot(s) + 72 == at) | (slot(s) + 144 == at)
    to_taps = jnp.where(((s < 54) & hit) | ((s == 54) & (at == 216)), 1.0, 0.0)
    prior_slots = dot(to_slots, prior, highest)
    parts = split_three(dot(prior_slots, to_taps, highest))
    prior_fwd[...] = jnp.concatenate(parts, axis=0).astype(bf16)
    turned = dot_nt(spread_rows(72, 55), prior_slots, highest)
    stacked = jnp.concatenate(list(split_three(turned)) + [jnp.zeros((8, 16), f32)], axis=0)
    again = jnp.where((iota((16, 48), 1) & 15) == iota((16, 48), 0), 1.0, 0.0)
    prior_back[...] = dot(stacked.astype(bf16), again.astype(bf16)).astype(bf16)

    stat_acc[...] = jnp.zeros_like(stat_acc)
    like_acc[...] = jnp.zeros_like(like_acc)
    prior_acc[...] = jnp.zeros_like(prior_acc)
    small_acc[...] = jnp.zeros_like(small_acc)
    bone_acc[...] = jnp.zeros_like(bone_acc)
    gst[...] = jnp.zeros_like(gst)
    gall[...] = jnp.zeros_like(gall)

    def land(size, fn_send, fn_recv):
        def one(d):
            fn_send(d).wait_send()
            fn_recv(d).wait_recv()

        each(size, one)

    pick = jnp.where(iota((SMALL, 128), 0) == iota((SMALL, 128), 1) + OUT, 1.0, 0.0).astype(bf16)
    for layer in range(layers):
        land(wide, functools.partial(gather, layer), functools.partial(gathered, layer))
        wmt[layer] = wall[layer, :, 0:hid].T
        wsm = wall[layer, :, hid : hid + SMALL]
        wst[layer] = wsm.T
        win[layer] = dot(wsm, pick).astype(bf16)
        bone[layer] = jnp.broadcast_to(wsm[:, 217:218].astype(f32), (hid, 128))

    def by_lanes(v):
        total_lanes = v[:, 0:128]
        for k in range(1, v.shape[1] // 128):
            total_lanes = total_lanes + v[:, 128 * k : 128 * k + 128]
        return total_lanes

    real = jnp.where(iota((8, 128), 0) < 6, 1.0, 0.0)

    def forward(t, carry):
        here = pl.ds(pl.multiple_of(t * TILE, TILE), TILE)
        shifts = Shifts(masks, TILE)
        images = TILE // 256
        blank = jnp.zeros((2, 256), f32)
        chunks = []
        for k in range(images):
            coarse = depth_ref[t * images + k] == 5
            by = jnp.where(coarse, 3, 0)
            level = jnp.where(coarse, 1.0 / 32.0, 1.0 / 256.0).astype(f32)
            at_image = pl.ds(pl.multiple_of(t * TILE + k * 256, 256), 256)
            quant = lax.shift_right_logical(pixels_ref[:, at_image], jnp.broadcast_to(by, (12, 256)))
            x = (quant.astype(f32) + noise_ref[:, at_image]) * level - 0.5
            chunks.append(jnp.concatenate([x[0:6], blank, x[6:12], blank], axis=0))
        x = jnp.concatenate(chunks, axis=1)
        states[0, :, here] = x
        logs = None
        for layer in range(layers):
            y = wide_rows(mixes[layer, 12], TILE)
            for c in range(12):
                at = c + 2 * (c // 6)
                y = y + wide_rows(mixes[layer, c], TILE) * x[at : at + 1, :]
            kept, other = y[0:8], y[8:16]
            ones = jnp.where(iota((8, TILE), 0) == 0, 1.0, 0.0)
            s0 = jnp.concatenate(shifts.taps(kept) + [ones], axis=0).astype(bf16)
            taps_in[layer, :, here] = s0
            h1 = jnp.maximum(dot(win[layer, :, 0:80], s0), 0.0).astype(bf16)
            hidden_one[layer, :, here] = h1
            second = dot(wall[layer, :, 0:hid], h1) + wide_rows(bone[layer], TILE)
            h2 = jnp.maximum(second, 0.0).astype(bf16)
            hidden_two[layer, :, here] = h2
            taps_out = dot(wst[layer, 0:OUT, :], h2)
            o = shifts.fold([taps_out[16 * k : 16 * k + 16] for k in range(9)])
            o = o + wide_rows(mixes[layer, 13], TILE)
            v = other + o[0:8]
            decay = 1.0 + jnp.exp(-(o[8:16] + 2.0))
            q = 1.0 / decay
            term = by_lanes(jnp.log(decay))
            logs = term if logs is None else logs + term
            keep[layer, 0:8, here] = v
            keep[layer, 8:16, here] = q
            x = jnp.concatenate([kept, v * q], axis=0)
            states[layer + 1, :, here] = x
        stat_acc[0] += by_lanes(x)
        stat_acc[1] += by_lanes(x * x)
        like_acc[...] -= logs * real
        return carry

    lax.fori_loop(0, count // TILE, forward, 0)

    lane = iota((16, 128), 1)
    stats = jnp.where(lane == 0, jnp.sum(stat_acc[0], axis=1, keepdims=True), 0.0) + jnp.where(
        lane == 1, jnp.sum(stat_acc[1], axis=1, keepdims=True), 0.0
    )
    st_wide[me_w] = stats

    def stat_send(d):
        mine = st_wide.at[me_w]
        return remote(mine, mine, st_send.at[d], st_recv.at[d], peer("wide", wide, me_w, d))

    def stat_recv(d):
        theirs = st_wide.at[source(wide, me_w, d)]
        return remote(theirs, theirs, st_send.at[d], st_recv.at[d], peer("wide", wide, me_w, d))

    each(wide, lambda d: stat_send(d).start())

    def prior_tile(t, carry):
        here = pl.ds(pl.multiple_of(t * TILE, TILE), TILE)
        shifts = Shifts(masks, TILE)
        z1 = states[layers, 0:8, here]
        z2 = states[layers, 8:16, here]
        ones = jnp.where(iota((8, TILE), 0) == 0, 1.0, 0.0)
        pieces = [split_three(v) for v in shifts.taps(z1)]
        tz = jnp.concatenate(
            [p[0] for p in pieces] + [p[1] for p in pieces] + [p[2] for p in pieces] + [ones], axis=0
        ).astype(bf16)
        three = dot(prior_fwd[:, 0:224], tz)
        stat = three[0:16] + three[16:32] + three[32:48]
        centre, log_sd = stat[0:8], stat[8:16]
        inverse = jnp.exp(-log_sd)
        ratio = (z2 - centre) * inverse
        like_acc[...] += by_lanes(-0.5 * z1 * z1 - 0.5 * ratio * ratio - log_sd)
        d_centre = ratio * inverse
        d_stat = jnp.concatenate([d_centre, ratio * ratio - 1.0], axis=0)
        ds = jnp.concatenate(split_three(d_stat), axis=0).astype(bf16)
        prior_acc[:, 0:224] += dot_nt(ds, tz)
        dt = dot(prior_back[...], ds)
        dt = dt[0:72] + dt[72:144] + dt[144:216]
        folded = shifts.fold([dt[8 * k : 8 * k + 8] for k in range(9)], -1)
        gz[0:8, here] = coeff * (folded - z1)
        gz[8:16, here] = -coeff * d_centre
        return carry

    lax.fori_loop(0, count // TILE, prior_tile, 0)

    land(wide, stat_send, stat_recv)
    stats = st_wide[0]
    for k in range(1, wide):
        stats = stats + st_wide[k]
    st_narrow[me_n] = stats

    def stat_send_n(d):
        mine = st_narrow.at[me_n]
        return remote(mine, mine, sn_send.at[d], sn_recv.at[d], peer("narrow", narrow, me_n, d))

    def stat_recv_n(d):
        theirs = st_narrow.at[source(narrow, me_n, d)]
        return remote(theirs, theirs, sn_send.at[d], sn_recv.at[d], peer("narrow", narrow, me_n, d))

    each(narrow, lambda d: stat_send_n(d).start())
    land(narrow, stat_send_n, stat_recv_n)
    stats = st_narrow[0]
    for k in range(1, narrow):
        stats = stats + st_narrow[k]
    mean = stats[:, 0:1] / total
    var = stats[:, 1:2] / total - mean * mean
    from_first = penalty_weight * (2.0 * mean - 4.0 * (var - 1.0) * mean) / total
    from_square = penalty_weight * 2.0 * (var - 1.0) / total
    ones_rows = jnp.where((iota((16, 1), 0) & 7) < 6, 1.0, 0.0)
    penalty = penalty_weight * jnp.sum(
        ones_rows * (mean * mean + (var - 1.0) * (var - 1.0)), axis=0, keepdims=True
    )

    def backward(layer):
        def tile(t, carry):
            here = pl.ds(pl.multiple_of(t * BACK, BACK), BACK)
            shifts = Shifts(masks, BACK)
            g = gz[:, here]
            if layer == layers - 1:
                g = g + from_first + 2.0 * states[layers, :, here] * from_square
            ga, gb = g[0:8], g[8:16]
            v = keep[layer, 0:8, here]
            q = keep[layer, 8:16, here]
            gbq = gb * q
            do = jnp.concatenate([gbq, (gbq * v + coeff) * (1.0 - q)], axis=0)
            rounded = do.astype(bf16).astype(f32)
            d3 = jnp.concatenate(shifts.taps(rounded, -1), axis=0).astype(bf16)
            h2 = hidden_two[layer, :, here]
            gst[layer, 0:OUT, :] += dot_nt(d3, h2)
            dd2 = dot(wall[layer, :, hid : hid + OUT], d3)
            masked = jnp.where(h2 > 0, dd2, 0.0)
            bone_acc[layer] += by_lanes(masked)
            d2 = masked.astype(bf16)
            h1 = hidden_one[layer, :, here]
            gall[layer, :, 0:hid] += dot_nt(d2, h1)
            dd1 = dot(wmt[layer], d2)
            d1 = jnp.where(h1 > 0, dd1, 0.0).astype(bf16)
            s0 = taps_in[layer, :, here]
            gst[layer, OUT : OUT + 80, :] += dot_nt(s0, d1)
            dt = dot(wst[layer, OUT : OUT + 80, :], d1)
            gya = ga + shifts.fold([dt[8 * k : 8 * k + 8] for k in range(9)], -1)
            gy = jnp.concatenate([gya, gbq], axis=0)
            x = states[layer, :, here]
            ones = jnp.where(iota((16, BACK), 0) == 0, 1.0, 0.0)
            left = jnp.concatenate(split_three(gy) + split_three(do), axis=0).astype(bf16)
            right = jnp.concatenate(split_three(x) + (ones,), axis=0).astype(bf16)
            small_acc[layer, :, 0:64] += dot_nt(left, right)
            if layer:
                gx = wide_rows(mixes_back[layer, 0], BACK) * gy[0:1, :]
                for c in range(1, 12):
                    at = c + 2 * (c // 6)
                    gx = gx + wide_rows(mixes_back[layer, c], BACK) * gy[at : at + 1, :]
                gz[:, here] = gx
            return carry

        lax.fori_loop(0, count // BACK, tile, 0)
        column = jnp.sum(bone_acc[layer], axis=1, keepdims=True)
        gall[layer, :, hid : hid + SMALL] = gst[layer].T + jnp.where(
            iota((hid, SMALL), 1) == 217, column, 0.0
        )

    def rs_go(layer, d):
        to = lax.rem(me_w + d, wide)
        return remote(
            gall.at[layer, block(to)],
            rs_buf.at[layer, d],
            rs_send.at[layer, d],
            rs_recv.at[layer, d],
            {"wide": to},
        )

    def nr_go(layer, d):
        mine = nr_buf.at[layer, me_n]
        return remote(
            mine, mine, nr_send.at[layer, d], nr_recv.at[layer, d], peer("narrow", narrow, me_n, d)
        )

    def nr_come(layer, d):
        theirs = nr_buf.at[layer, source(narrow, me_n, d)]
        return remote(
            theirs, theirs, nr_send.at[layer, d], nr_recv.at[layer, d], peer("narrow", narrow, me_n, d)
        )

    def rs_end(layer):
        land(wide, functools.partial(rs_go, layer), functools.partial(rs_go, layer))
        nr_buf[layer, me_n] = gall[layer, block(me_w), :]

        def add(d):
            nr_buf[layer, me_n] += rs_buf[layer, d]

        each(wide, add)
        each(narrow, lambda d: nr_go(layer, d).start())

    def nr_end(layer):
        land(narrow, functools.partial(nr_go, layer), functools.partial(nr_come, layer))
        whole = nr_buf[layer, 0]
        for k in range(1, narrow):
            whole = whole + nr_buf[layer, k]
        grad_ref[layer] = whole

    for layer in reversed(range(layers)):
        backward(layer)
        each(wide, lambda d: rs_go(layer, d).start())

    pieces = []
    for layer in range(layers):
        acc = small_acc[layer]
        gy_part = acc[0:16] + acc[16:32] + acc[32:48]
        do_part = acc[48:64] + acc[64:80] + acc[80:96]
        moment = gy_part + pltpu.roll(gy_part, 112, 1) + pltpu.roll(gy_part, 96, 1)
        moment = jnp.where(lane < 16, moment, 0.0)
        moment = moment + jnp.where(lane == 16, pltpu.roll(gy_part, 96, 1), 0.0)
        moment = moment + jnp.where(lane == 17, pltpu.roll(do_part, 97, 1), 0.0)
        pieces.append(moment)
    acc = prior_acc[0:16] + prior_acc[16:32] + prior_acc[32:48]
    taps_part = (
        acc + pltpu.roll(acc, 256 - 72, 1) + pltpu.roll(acc, 256 - 144, 1)
    )[:, 0:128]
    ones_part = pltpu.roll(acc, 256 - 144, 1)[:, 0:128]
    pieces.append(jnp.where(lane < 72, taps_part, 0.0) + jnp.where(lane == 72, ones_part, 0.0))
    depths = lax.fori_loop(0, depth_ref.shape[0], lambda k, c: c + depth_ref[k], jnp.int32(0))
    depths = jnp.broadcast_to(depths, (8, 128)).astype(f32)
    row8 = iota((8, 128), 0)
    logs = jnp.sum(like_acc[...], axis=0, keepdims=True)
    pieces.append(jnp.where(row8 == 0, logs, 0.0) + jnp.where(row8 == 1, depths, 0.0))
    sm_wide[me_w] = jnp.concatenate(pieces, axis=0)

    def sw_go(d):
        mine = sm_wide.at[me_w]
        return remote(mine, mine, sw_send.at[d], sw_recv.at[d], peer("wide", wide, me_w, d))

    def sw_come(d):
        theirs = sm_wide.at[source(wide, me_w, d)]
        return remote(theirs, theirs, sw_send.at[d], sw_recv.at[d], peer("wide", wide, me_w, d))

    def so_go(d):
        mine = sm_narrow.at[me_n]
        return remote(mine, mine, so_send.at[d], so_recv.at[d], peer("narrow", narrow, me_n, d))

    def so_come(d):
        theirs = sm_narrow.at[source(narrow, me_n, d)]
        return remote(theirs, theirs, so_send.at[d], so_recv.at[d], peer("narrow", narrow, me_n, d))

    each(wide, lambda d: sw_go(d).start())
    land(wide, sw_go, sw_come)
    whole = sm_wide[0]
    for k in range(1, wide):
        whole = whole + sm_wide[k]
    sm_narrow[me_n] = whole
    each(narrow, lambda d: so_go(d).start())
    for layer in reversed(range(layers)):
        rs_end(layer)
    land(narrow, so_go, so_come)
    whole = sm_narrow[0]
    for k in range(1, narrow):
        whole = whole + sm_narrow[k]
    rows = whole.shape[0]
    sums_ref[...] = whole + jnp.where(iota((rows, 128), 0) == rows - 8 + 2, penalty, 0.0)
    for layer in reversed(range(layers)):
        nr_end(layer)


def adamw(weight, grad, first, second, fixes):
    first_new = beta_one * first + (1.0 - beta_one) * grad
    second_new = beta_two * second + (1.0 - beta_two) * grad * grad
    update = first_new / fixes[0] / (jnp.sqrt(second_new / fixes[1]) + epsilon) + decay_rate * weight
    return (weight - learn_rate * update, first_new, second_new)


def update_kernel(total, images, step_ref, grad_ref, sums_ref, *refs):
    weights, firsts, seconds, loss_ref, outs = refs[0:6], refs[6:12], refs[12:18], refs[18], refs[19:]
    layers, share, _ = grad_ref.shape
    hid = weights[1].shape[2]
    coeff = -1.0 / (total * 12 * math.log(2.0))
    power = iota((8, 128), 1)
    used = power < jnp.broadcast_to(step_ref[0], (8, 128))
    fixes = tuple(
        (1.0 - beta)
        * jnp.sum(
            jnp.where(used, jnp.exp(power.astype(f32) * math.log(beta)), 0.0), axis=1, keepdims=True
        )[0:1]
        for beta in (beta_one, beta_two)
    )

    def write(which, at, grad):
        new = adamw(weights[which][at], grad, firsts[which][at], seconds[which][at], fixes)
        for k in range(3):
            outs[3 * which + k][at] = new[k]

    place = spread(164, SMALL)
    to_slots = spread_rows(16, 12)
    reverse = jnp.where(slot(11 - iota((16, 12), 1)) == iota((16, 12), 0), 1.0, 0.0)
    row, col = iota((12, 12), 0), iota((12, 12), 1)
    eye = row == col
    logdet = jnp.zeros((1, 1), f32)
    for layer in range(layers):
        write(1, layer, grad_ref[layer, :, 0:hid])
        part = grad_ref[layer, :, hid : hid + SMALL]
        write(0, layer, dot_nt(part, place[108:162], highest))
        write(2, layer, dot_nt(place[0:108], part, highest))
        write(3, layer, dot_nt(place[162:164], part, highest))
        small = weights[4][layer]
        lu = small[:, 0:12]
        lower, upper = mixing_parts(lu)
        scale = jnp.exp(small[:, 13:14])
        scale_row = as_row(scale)
        sums = sums_ref[16 * layer : 16 * layer + 16]
        turned = dot_tn(reverse, sums, highest)
        moment = dot(turned[:, 0:16], to_slots, highest)
        ones = turned[:, 16:17]
        g_mix = (moment + ones * as_row(small[:, 12:13])) * scale_row
        mix = dot(lower, upper, highest)
        g_bias = scale * dot_tn(mix, ones, highest)
        g_scale = as_column(jnp.sum(mix * g_mix, axis=0, keepdims=True)) + coeff * total
        g_lower = dot_nt(g_mix, upper, highest)
        g_upper = dot_tn(lower, g_mix, highest)
        g_lu = jnp.where(row > col, g_lower, jnp.where(eye, g_upper * jnp.exp(lu) + coeff * total, g_upper))
        g_cb = dot_tn(to_slots, sums, highest)[:, 17:18]
        wide15 = iota((12, 15), 1)
        grad = dot(g_lu, jnp.where(iota((12, 15), 0) == wide15, 1.0, 0.0), highest)
        grad = jnp.where(wide15 == 12, g_bias, grad)
        grad = jnp.where(wide15 == 13, g_scale, grad)
        grad = jnp.where(wide15 == 14, g_cb, grad)
        write(4, layer, grad)
        diag = jnp.sum(jnp.where(eye, lu, 0.0), axis=0, keepdims=True) + as_row(small[:, 13:14])
        logdet = logdet + jnp.sum(diag, axis=1, keepdims=True)
    sums = sums_ref[16 * layers : 16 * layers + 16]
    grad = coeff * dot_nt(
        dot_tn(to_slots, sums, highest), spread(55, 128), highest
    )
    write(5, Ellipsis, grad)
    tail = sums_ref[16 * layers + 16 :]
    likely = jnp.sum(tail[0:1], axis=1, keepdims=True)
    likely = likely - total * 6.0 * math.log(2.0 * math.pi) + total * logdet
    loss_ref[...] = coeff * likely + tail[1:2, 0:1] / images + tail[2:3, 0:1]


def as_column(row):
    n = row.shape[1]
    eye = iota((n, n), 0) == iota((n, n), 1)
    return jnp.sum(jnp.where(eye, row, 0.0), axis=1, keepdims=True)


def shards(*args, wide, narrow):
    pixels, noise, depth, step_count = args[0:4]
    params, firsts, seconds = args[4:10], args[10:16], args[16:22]
    layers, share, hid = params[1].shape
    count = pixels.shape[1]
    width = hid + SMALL
    rows = 16 * layers + 16 + 8
    dma = pltpu.SemaphoreType.DMA
    big = functools.partial(pltpu.VMEM)
    scratch = [
        big((layers, hid, width), bf16),
        big((layers, hid, hid), bf16),
        big((layers, SMALL, hid), bf16),
        big((layers, hid, 128), bf16),
        big((layers, hid, 128), f32),
        big((layers, 14, 16, 128), f32),
        big((layers, 12, 16, 128), f32),
        big((48, 256), bf16),
        big((224, 48), bf16),
        big((4, 8, max(TILE, BACK)), f32),
        big((layers + 1, 16, count), f32),
        big((layers, 16, count), f32),
        big((layers, 80, count), bf16),
        big((layers, hid, count), bf16),
        big((layers, hid, count), bf16),
        big((16, count), f32),
        big((2, 16, 128), f32),
        big((8, 128), f32),
        big((48, 256), f32),
        big((layers, 96, 128), f32),
        big((layers, hid, 128), f32),
        big((layers, SMALL, hid), f32),
        big((layers, hid, width), f32),
        big((layers, wide, share, width), f32),
        big((layers, narrow, share, width), f32),
        big((wide, 16, 128), f32),
        big((narrow, 16, 128), f32),
        big((wide, rows, 128), f32),
        big((narrow, rows, 128), f32),
        dma((layers, wide)),
        dma((layers, wide)),
        dma((layers, wide)),
        dma((layers, wide)),
        dma((layers, narrow)),
        dma((layers, narrow)),
        dma((wide,)),
        dma((wide,)),
        dma((narrow,)),
        dma((narrow,)),
        dma((wide,)),
        dma((wide,)),
        dma((narrow,)),
        dma((narrow,)),
    ]
    remote = {"collective_id": 0, "has_side_effects": True} if wide > 1 else {}
    grads, sums = pl.pallas_call(
        functools.partial(flow_kernel, wide, narrow),
        out_shape=(
            jax.ShapeDtypeStruct((layers, share, width), f32),
            jax.ShapeDtypeStruct((rows, 128), f32),
        ),
        in_specs=[VMEM, VMEM, SMEM] + [VMEM] * 6,
        out_specs=(VMEM, VMEM),
        scratch_shapes=scratch,
        compiler_params=pltpu.CompilerParams(vmem_limit_bytes=63 * 1024 * 1024, **remote),
        name="flow",
    )(pixels, noise, depth, params[4], params[5], params[0], params[1], params[2], params[3])
    total = count * wide * narrow
    shapes = [jax.ShapeDtypeStruct((1, 1), f32)]
    for p in params:
        shapes += [jax.ShapeDtypeStruct(p.shape, f32)] * 3
    results = pl.pallas_call(
        functools.partial(update_kernel, total, total // 256),
        out_shape=tuple(shapes),
        in_specs=[SMEM] + [VMEM] * 20,
        out_specs=(VMEM,) * 19,
        compiler_params=pltpu.CompilerParams(vmem_limit_bytes=32 * 1024 * 1024),
        name="update",
    )(step_count.reshape(1), grads, sums, *params, *firsts, *seconds)
    return (results[0].reshape(()),) + tuple(results[1:])


def solution(mesh):
    weights = (P(None, "wide", None), P(None, "wide", None), P(None, None, "wide"), P(None, None, "wide"), P(), P())
    return jax.shard_map(
        functools.partial(shards, wide=mesh.shape["wide"], narrow=mesh.shape["narrow"]),
        mesh=mesh,
        in_specs=(
            P(None, ("narrow", "wide")),
            P(None, ("narrow", "wide")),
            P(("narrow", "wide")),
            P(),
        )
        + weights * 3,
        out_specs=(P(),) + tuple(w for w in weights for _ in range(3)),
        check_vma=False,
    )
```

```python
import functools
import math

import jax
import jax.numpy as jnp
from jax import lax
from jax.experimental import pallas as pl
from jax.experimental.pallas import tpu as pltpu
from jax.sharding import PartitionSpec as P

f32 = jnp.float32
bf16 = jnp.bfloat16
highest = lax.Precision.HIGHEST
MESH = pl.DeviceIdType.MESH
learn_rate = 0.02
beta_one = 0.9
beta_two = 0.999
epsilon = 1e-08
decay_rate = 0.01
penalty_weight = 0.5
tap_offsets = [(r, c) for r in (-1, 0, 1) for c in (-1, 0, 1)]
TILE = 2048
FLOW_VMEM = 60 * 1024 * 1024
UPDATE_VMEM = 60 * 1024 * 1024
OUT = 144
SMALL = 256
VMEM = pl.BlockSpec(memory_space=pltpu.VMEM)
SMEM = pl.BlockSpec(memory_space=pltpu.SMEM)


def dot(a, b, precision=None):
    return lax.dot_general(
        a, b, (((1,), (0,)), ((), ())), preferred_element_type=f32, precision=precision
    )


def dot_nt(a, b, precision=None):
    return lax.dot_general(
        a, b, (((1,), (1,)), ((), ())), preferred_element_type=f32, precision=precision
    )


def dot_tn(a, b, precision=None):
    return lax.dot_general(
        a, b, (((0,), (0,)), ((), ())), preferred_element_type=f32, precision=precision
    )


def iota(shape, axis):
    return lax.broadcasted_iota(jnp.int32, shape, axis)


def slot(s):
    return s + 2 * ((s * 10923) >> 16)


def spread(count, width, first=0):
    return jnp.where(slot(iota((count, width), 0) + first) == iota((count, width), 1), 1.0, 0.0)


def spread_rows(height, count):
    return jnp.where(slot(iota((height, count), 1)) == iota((height, count), 0), 1.0, 0.0)


def split_three(v):
    high = v.astype(bf16).astype(f32)
    rest = v - high
    middle = rest.astype(bf16).astype(f32)
    return high, middle, rest - middle


def as_row(column):
    n = column.shape[0]
    eye = iota((n, n), 0) == iota((n, n), 1)
    return jnp.sum(jnp.where(eye, column, 0.0), axis=0, keepdims=True)


def mixing_parts(lu):
    n = lu.shape[0]
    row, col = iota((n, n), 0), iota((n, n), 1)
    lower = jnp.where(row > col, lu, 0.0) + jnp.where(row == col, 1.0, 0.0)
    upper = jnp.where(row < col, lu, 0.0) + jnp.where(row == col, jnp.exp(lu), 0.0)
    return lower, upper


def wide_rows(v, lanes):
    return jnp.concatenate([v] * (lanes // 128), axis=1)


class Shifts:
    def __init__(self, mask_ref, lanes):
        self.lanes = lanes
        self.masks = mask_ref

    def mask(self, which, rows):
        m = self.masks[which, :, 0 : self.lanes]
        return jnp.concatenate([m] * (rows // 8), axis=0) if rows > 8 else m

    def col(self, v, c):
        if c == 0:
            return v
        moved = pltpu.roll(v, (-c) % self.lanes, 1)
        return moved * self.mask(0 if c > 0 else 1, v.shape[0])

    def row(self, v, r):
        if r == 0:
            return v
        moved = pltpu.roll(v, (-16 * r) % self.lanes, 1)
        return moved * self.mask(2 if r > 0 else 3, v.shape[0])

    def taps(self, v, sign=1):
        by_col = {c: self.col(v, c) for c in (-1, 0, 1)}
        return [self.row(by_col[sign * c], sign * r) for r, c in tap_offsets]

    def fold(self, pieces, sign=1):
        total = None
        for c in (-1, 0, 1):
            part = None
            for r in (-1, 0, 1):
                piece = self.row(pieces[3 * (r + 1) + (c + 1)], sign * r)
                part = piece if part is None else part + piece
            part = self.col(part, sign * c)
            total = part if total is None else total + part
        return total


def fill_masks(mask_ref):
    lanes = mask_ref.shape[2]
    pos = iota((8, lanes), 1)
    row, col = (pos >> 4) & 15, pos & 15
    for which, keep in enumerate((col < 15, col > 0, row < 15, row > 0)):
        mask_ref[which] = jnp.where(keep, 1.0, 0.0)


def flow_kernel(wide, narrow, layout, *refs):
    names, groups = layout
    at = dict(zip(names, refs))
    pixels_ref, noise_ref, depth_ref = at["pixels"], at["noise"], at["depth"]
    wall, wmt, wst, win, bone = at["wall"], at["wmt"], at["wst"], at["win"], at["bone"]
    mixes, mixes_back = at["mixes"], at["mixes_back"]
    states, keep, taps_in, gz = at["states"], at["keep"], at["taps_in"], at["gz"]
    hidden_one, hidden_two = at["hidden_one"], at["hidden_two"]
    layers, share, hid = at["mid"].shape
    count = pixels_ref.shape[1]
    total = count * wide * narrow
    coeff = -1.0 / (total * 12 * math.log(2.0))
    chips = max(wide // 2, 1)
    me_w = lax.axis_index("wide") if wide > 1 else 0
    me_n = lax.axis_index("narrow") if narrow > 1 else 0
    chip, core = (me_w // 2, lax.rem(me_w, 2)) if wide > 1 else (0, 0)
    shifts = Shifts(at["masks"], TILE)

    def block(index):
        return pl.ds(pl.multiple_of(index * share, share), share)

    def tile_at(t):
        return pl.ds(pl.multiple_of(t * TILE, TILE), TILE)

    def ahead(size, me, d):
        return lax.rem(me + d, size)

    def behind(size, me, d):
        return lax.rem(me + size - d, size)

    def each(first, size, fn):
        if wide > 1 and size > first:
            lax.fori_loop(first, size, lambda d, c: (fn(d), c)[1], 0)

    def remote(src, dst, sems, index, device):
        send, recv = at[sems + "_send"], at[sems + "_recv"]
        return pltpu.make_async_remote_copy(
            src_ref=src,
            dst_ref=dst,
            send_sem=send.at[index],
            recv_sem=recv.at[index],
            device_id=device,
            device_id_type=MESH,
        )

    class Exchange:
        def __init__(self, name):
            self.name, self.bufs = name, (at[name + "_w"], at[name + "_n"])

        def copy(self, phase, d, coming):
            axis, size, me = (("wide", wide, me_w), ("narrow", narrow, me_n))[phase]
            row = self.bufs[phase].at[behind(size, me, d) if coming else me]
            sems = self.name + ("_sw", "_sn")[phase]
            return remote(row, row, sems, d, {axis: ahead(size, me, d)})

        def start(self, phase, value):
            me, size = ((me_w, wide), (me_n, narrow))[phase]
            self.bufs[phase][me] = value
            each(1, size, lambda d: self.copy(phase, d, False).start())

        def finish(self, phase):
            size = (wide, narrow)[phase]

            def one(d):
                self.copy(phase, d, False).wait_send()
                self.copy(phase, d, True).wait_recv()

            each(1, size, one)
            value = self.bufs[phase][0]
            for k in range(1, size):
                value = value + self.bufs[phase][k]
            return value

        def hop(self):
            self.start(1, self.finish(0))

    stat, early, late = Exchange("stat"), Exchange("early"), Exchange("late")

    class Group:
        def __init__(self, name):
            self.name = name
            self.full, self.pair, self.chip = at[name], at[name + "_p"], at[name + "_c"]
            self.part, self.out = at[name + "_n"], at[name + "_out"]
            self.scatter = share % (8 * narrow) == 0
            self.piece = share // narrow if self.scatter else share
            self.stage = 0

        def rows(self, index):
            return pl.ds(pl.multiple_of(index * self.piece, 8), self.piece)

        def copies(self, stage):
            if stage == 0:
                go = lambda d: remote(
                    self.full.at[block(2 * d + 1 - core)],
                    self.pair.at[d],
                    self.name + "_s0",
                    d,
                    {"wide": me_w + 1 - 2 * core},
                )
                return 0, chips, go, go
            if stage == 1:

                def go(d):
                    to = 2 * ahead(chips, chip, d) + core
                    return remote(
                        self.full.at[block(to)], self.chip.at[d], self.name + "_s1", d, {"wide": to}
                    )

                return 1, chips, go, go
            if stage == 2 and self.scatter:

                def go(d):
                    to = ahead(narrow, me_n, d)
                    mine = pl.ds(pl.multiple_of(me_w * share + to * self.piece, 8), self.piece)
                    return remote(
                        self.full.at[mine], self.part.at[d], self.name + "_s2", d, {"narrow": to}
                    )

                return 1, narrow, go, go
            if stage == 2:
                go = lambda d: remote(
                    self.part.at[me_n],
                    self.part.at[me_n],
                    self.name + "_s2",
                    d,
                    {"narrow": ahead(narrow, me_n, d)},
                )
                come = lambda d: remote(
                    self.part.at[behind(narrow, me_n, d)],
                    self.part.at[behind(narrow, me_n, d)],
                    self.name + "_s2",
                    d,
                    {"narrow": ahead(narrow, me_n, d)},
                )
                return 1, narrow, go, come
            go = lambda d: remote(
                self.out.at[self.rows(me_n)],
                self.out.at[self.rows(me_n)],
                self.name + "_s3",
                d,
                {"narrow": ahead(narrow, me_n, d)},
            )
            come = lambda d: remote(
                self.out.at[self.rows(behind(narrow, me_n, d))],
                self.out.at[self.rows(behind(narrow, me_n, d))],
                self.name + "_s3",
                d,
                {"narrow": ahead(narrow, me_n, d)},
            )
            return 1, narrow if self.scatter else 1, go, come

        def start(self):
            first, end, go, _ = self.copies(self.stage)
            each(first, end, lambda d: go(d).start())

        def finish(self):
            first, end, go, come = self.copies(self.stage)

            def one(d):
                go(d).wait_send()
                come(d).wait_recv()

            each(first, end, one)
            own = block(me_w)
            if self.stage == 0:

                def add(d):
                    mine = block(2 * d + core)
                    self.full[mine, :] += self.pair[d]

                each(0, chips, add)
            if self.stage == 1:

                def add(d):
                    self.full[own, :] += self.chip[d]

                each(1, chips, add)
                if not self.scatter:
                    self.part[me_n] = self.full[own, :]
            if self.stage == 2 and self.scatter:
                mine = pl.ds(pl.multiple_of(me_w * share + me_n * self.piece, 8), self.piece)
                value = self.full[mine, :]
                for d in range(1, narrow):
                    value = value + self.part[d]
                self.out[self.rows(me_n), :] = value
            elif self.stage == 2:
                value = self.part[0]
                for d in range(1, narrow):
                    value = value + self.part[d]
                self.out[...] = value
            self.stage += 1

        def advance(self):
            if self.stage < 4:
                self.finish()
                if self.stage < 4:
                    self.start()

    made = {name: Group(name) for name in groups}

    if wide > 1:
        barrier = pltpu.get_barrier_semaphore()
        for axis, size, me in (("wide", wide, me_w), ("narrow", narrow, me_n)):
            each(
                1,
                size,
                lambda d: pl.semaphore_signal(
                    barrier, inc=1, device_id={axis: ahead(size, me, d)}, device_id_type=MESH
                ),
            )

    place = spread(164, SMALL).astype(bf16)
    for layer in range(layers):
        small_part = (
            dot(at["out"][layer].astype(bf16), place[0:108])
            + dot_tn(at["in"][:, layer, :].astype(bf16), place[108:162])
            + dot_tn(at["bias"][layer].astype(bf16), place[162:164])
        )
        wall[layer, block(me_w), 0:hid] = at["mid"][layer].astype(bf16)
        wall[layer, block(me_w), hid : hid + SMALL] = small_part.astype(bf16)

    def weights_of(index):
        return wall.at[0, block(index)]

    def to_chip(d, coming=False):
        index = 2 * (behind(chips, chip, d) if coming else chip) + core
        to = 2 * ahead(chips, chip, d) + core
        return remote(weights_of(index), weights_of(index), "ga", d, {"wide": to})

    def to_core(d, coming=False):
        index = 2 * behind(chips, chip, d) + (1 - core if coming else core)
        to = me_w + 1 - 2 * core
        return remote(weights_of(index), weights_of(index), "ga", chips + d, {"wide": to})

    def to_all(layer, d, coming=False):
        mine = wall.at[layer, block(behind(wide, me_w, d) if coming else me_w)]
        return remote(mine, mine, "gb", (layer, d), {"wide": ahead(wide, me_w, d)})

    if wide > 1:
        pl.semaphore_wait(barrier, wide + narrow - 2)
        each(1, chips, lambda d: to_chip(d).start())
        to_core(0).start()

    fill_masks(at["masks"])
    to_slots = spread_rows(16, 12)
    reverse = jnp.where(slot(11 - iota((16, 12), 1)) == iota((16, 12), 0), 1.0, 0.0)
    for layer in range(layers):
        small = at["small"][:, layer, :]
        lower, upper = mixing_parts(small[:, 0:12])
        scale = jnp.exp(small[:, 13:14])
        mixed = dot(reverse, dot(lower, upper, highest), highest) * as_row(scale)
        const = jnp.sum(mixed * as_row(small[:, 12:13]), axis=1, keepdims=True)
        cb = jnp.sum(to_slots * as_row(small[:, 14:15]), axis=1, keepdims=True)
        for c in range(12):
            mixes[layer, c] = jnp.broadcast_to(mixed[:, c : c + 1], (16, 128))
        mixes[layer, 12] = jnp.broadcast_to(const, (16, 128))
        mixes[layer, 13] = jnp.broadcast_to(cb, (16, 128))
        if layer:
            back = dot_nt(to_slots, mixed, highest)
            for c in range(12):
                s = c + 2 * (c // 6)
                mixes_back[layer, c] = jnp.broadcast_to(back[:, s : s + 1], (16, 128))

    def by_lanes(v):
        parts = [v[:, 128 * k : 128 * k + 128] for k in range(v.shape[1] // 128)]
        while len(parts) > 1:
            parts = [a + b for a, b in zip(parts[0::2], parts[1::2])]
        return parts[0]

    real = jnp.where(iota((8, 128), 0) < 6, 1.0, 0.0)

    def enter(layer, here, x):
        states[layer, :, here] = x
        y = wide_rows(mixes[layer, 12], TILE)
        for c in range(12):
            s = c + 2 * (c // 6)
            y = y + wide_rows(mixes[layer, c], TILE) * x[s : s + 1, :]
        ones = jnp.where(iota((8, TILE), 0) == 0, 1.0, 0.0)
        taps_in[layer, :, here] = jnp.concatenate(shifts.taps(y[0:8]) + [ones], axis=0).astype(bf16)
        states[layer + 1, 0:8, here] = y[0:8]
        keep[layer, 0:8, here] = y[8:16]

    def pixels_in(t, carry):
        images = TILE // 256
        blank = jnp.zeros((2, 256), f32)
        chunks = []
        for k in range(images):
            coarse = depth_ref[t * images + k] == 5
            by = jnp.where(coarse, 3, 0)
            level = jnp.where(coarse, 1.0 / 32.0, 1.0 / 256.0).astype(f32)
            at_image = pl.ds(pl.multiple_of(t * TILE + k * 256, 256), 256)
            quant = lax.shift_right_logical(pixels_ref[:, at_image], jnp.broadcast_to(by, (12, 256)))
            x = (quant.astype(f32) + noise_ref[:, at_image]) * level - 0.5
            chunks.append(jnp.concatenate([x[0:6], blank, x[6:12], blank], axis=0))
        enter(0, tile_at(t), jnp.concatenate(chunks, axis=1))
        return carry

    lax.fori_loop(0, count // TILE, pixels_in, 0)

    if wide > 1:

        def pass_on(d):
            to_chip(d).wait_send()
            to_chip(d, True).wait_recv()
            to_core(d).start()

        each(1, chips, pass_on)

    prior = at["prior"][...]
    s = iota((55, 256), 0)
    lane = iota((55, 256), 1)
    hit = (slot(s) == lane) | (slot(s) + 72 == lane) | (slot(s) + 144 == lane)
    to_taps = jnp.where(((s < 54) & hit) | ((s == 54) & (lane == 216)), 1.0, 0.0)
    prior_slots = dot(to_slots, prior, highest)
    parts = split_three(dot(prior_slots, to_taps, highest))
    at["prior_fwd"][...] = jnp.concatenate(parts, axis=0).astype(bf16)
    turned = dot_nt(spread_rows(72, 55), prior_slots, highest)
    stacked = jnp.concatenate(list(split_three(turned)) + [jnp.zeros((8, 16), f32)], axis=0)
    again = jnp.where((iota((16, 48), 1) & 15) == iota((16, 48), 0), 1.0, 0.0)
    at["prior_back"][...] = dot(stacked.astype(bf16), again.astype(bf16)).astype(bf16)

    for name in ("stat_acc", "like_acc", "prior_acc", "small_acc", "sum_acc", "bone_acc", "gst"):
        at[name][...] = jnp.zeros_like(at[name])
    for layer in range(layers):
        at[f"mid{layer}"][...] = jnp.zeros_like(at[f"mid{layer}"])

    pick = jnp.where(iota((SMALL, 128), 0) == iota((SMALL, 128), 1) + OUT, 1.0, 0.0).astype(bf16)

    def derive(layer):
        wsm = wall[layer, :, hid : hid + SMALL]
        win[layer] = dot(wsm, pick).astype(bf16)
        wst[layer] = wsm.T
        bone[layer] = jnp.broadcast_to(wsm[:, 217:218].astype(f32), (hid, 128))

    if wide > 1:

        def landed(d):
            to_core(d).wait_send()
            to_core(d, True).wait_recv()

        each(0, chips, landed)
        for layer in range(1, layers):
            each(1, wide, lambda d: to_all(layer, d).start())

    for layer in range(layers):
        if layer and wide > 1:

            def arrived(d):
                to_all(layer, d).wait_send()
                to_all(layer, d, True).wait_recv()

            each(1, wide, arrived)
        derive(layer)

        def forward(t, carry):
            here = tile_at(t)
            first = dot(win[layer, :, 0:80], taps_in[layer, :, here]).astype(bf16)
            h1 = jnp.maximum(first, jnp.zeros_like(first))
            hidden_one[layer, :, here] = h1
            second = dot(wall[layer, :, 0:hid], h1) + wide_rows(bone[layer], TILE)
            h2 = jnp.maximum(second, 0.0).astype(bf16)
            hidden_two[layer, :, here] = h2
            taps_out = dot(wst[layer, 0:OUT, :], h2)
            o = shifts.fold([taps_out[16 * k : 16 * k + 16] for k in range(9)])
            o = o + wide_rows(mixes[layer, 13], TILE)
            v = keep[layer, 0:8, here] + o[0:8]
            decay = 1.0 + jnp.exp(-(o[8:16] + 2.0))
            q = 1.0 / decay
            at["like_acc"][...] -= by_lanes(jnp.log(decay)) * real
            keep[layer, 0:8, here] = v
            keep[layer, 8:16, here] = q
            x = jnp.concatenate([states[layer + 1, 0:8, here], v * q], axis=0)
            if layer < layers - 1:
                enter(layer + 1, here, x)
            else:
                states[layer + 1, 8:16, here] = x[8:16]
                at["stat_acc"][0] += by_lanes(x)
                at["stat_acc"][1] += by_lanes(x * x)
            return carry

        lax.fori_loop(0, count // TILE, forward, 0)

    lane = iota((16, 128), 1)

    def columns(*parts):
        value = jnp.zeros((16, 128), f32)
        for k, part in enumerate(parts):
            value = jnp.where(lane == k, jnp.sum(part, axis=1, keepdims=True), value)
        return value

    stat.start(0, columns(at["stat_acc"][0], at["stat_acc"][1]))

    def prior_tile(t, carry):
        here = tile_at(t)
        z1 = states[layers, 0:8, here]
        z2 = states[layers, 8:16, here]
        ones = jnp.where(iota((8, TILE), 0) == 0, 1.0, 0.0)
        pieces = [split_three(v) for v in shifts.taps(z1)]
        tz = jnp.concatenate(
            [p[0] for p in pieces] + [p[1] for p in pieces] + [p[2] for p in pieces] + [ones], axis=0
        ).astype(bf16)
        three = dot(at["prior_fwd"][:, 0:224], tz)
        value = three[0:16] + three[16:32] + three[32:48]
        centre, log_sd = value[0:8], value[8:16]
        inverse = jnp.exp(-log_sd)
        ratio = (z2 - centre) * inverse
        at["like_acc"][...] += by_lanes(-0.5 * z1 * z1 - 0.5 * ratio * ratio - log_sd)
        d_centre = ratio * inverse
        d_stat = jnp.concatenate([d_centre, ratio * ratio - 1.0], axis=0)
        ds = jnp.concatenate(split_three(d_stat), axis=0).astype(bf16)
        at["prior_acc"][:, 0:224] += dot_nt(ds, tz)
        dt = dot(at["prior_back"][...], ds)
        dt = dt[0:72] + dt[72:144] + dt[144:216]
        folded = shifts.fold([dt[8 * k : 8 * k + 8] for k in range(9)], -1)
        gz[0:8, here] = coeff * (folded - z1)
        gz[8:16, here] = -coeff * d_centre
        return carry

    tiles = count // TILE
    lax.fori_loop(0, tiles // 2, prior_tile, 0)
    stat.hop()
    lax.fori_loop(tiles // 2, tiles, prior_tile, 0)
    for layer in range(layers):
        wmt[layer] = wall[layer, :, 0:hid].T
    stats = stat.finish(1)
    mean = stats[:, 0:1] / total
    var = stats[:, 1:2] / total - mean * mean
    from_first = penalty_weight * (2.0 * mean - 4.0 * (var - 1.0) * mean) / total
    from_square = penalty_weight * 2.0 * (var - 1.0) / total
    ones_rows = jnp.where((iota((16, 1), 0) & 7) < 6, 1.0, 0.0)
    penalty = penalty_weight * jnp.sum(
        ones_rows * (mean * mean + (var - 1.0) * (var - 1.0)), axis=0, keepdims=True
    )

    def back_a(layer, t, carry):
        here = tile_at(t)
        g = gz[:, here]
        if layer == layers - 1:
            g = g + from_first + 2.0 * states[layers, :, here] * from_square
            gz[0:8, here] = g[0:8]
        v = keep[layer, 0:8, here]
        q = keep[layer, 8:16, here]
        gbq = g[8:16] * q
        gz[8:16, here] = gbq
        do = jnp.concatenate([gbq, (gbq * v + coeff) * (1.0 - q)], axis=0)
        at["sum_acc"][layer, 1] += by_lanes(do)
        rounded = do.astype(bf16).astype(f32)
        d3 = jnp.concatenate(shifts.taps(rounded, -1), axis=0).astype(bf16)
        h2 = hidden_two[layer, :, here]
        at["gst"][0:OUT, :] += dot_nt(d3, h2)
        dd2 = dot(wall[layer, :, hid : hid + OUT], d3).astype(bf16)
        hidden_two[layer, :, here] = jnp.where(h2 > 0, dd2, jnp.zeros_like(dd2))
        return carry

    def back_b(layer, t, carry):
        here = tile_at(t)
        d2 = hidden_two[layer, :, here]
        at[f"mid{layer}"][...] += dot_nt(d2, hidden_one[layer, :, here])
        at["bone_acc"][...] += by_lanes(d2.astype(f32))
        return carry

    def back_c(layer, t, carry):
        here = tile_at(t)
        dd1 = dot(wmt[layer], hidden_two[layer, :, here]).astype(bf16)
        d1 = jnp.where(hidden_one[layer, :, here] > 0, dd1, jnp.zeros_like(dd1))
        at["gst"][OUT : OUT + 80, :] += dot_nt(taps_in[layer, :, here], d1)
        dt = dot(wst[layer, OUT : OUT + 80, :], d1)
        g = gz[:, here]
        gya = g[0:8] + shifts.fold([dt[8 * k : 8 * k + 8] for k in range(9)], -1)
        gy = jnp.concatenate([gya, g[8:16]], axis=0)
        at["sum_acc"][layer, 0] += by_lanes(gy)
        left = jnp.concatenate(split_three(gy), axis=0).astype(bf16)
        right = jnp.concatenate(split_three(states[layer, :, here]), axis=0).astype(bf16)
        at["small_acc"][layer, :, 0:48] += dot_nt(left, right)
        if layer:
            gx = wide_rows(mixes_back[layer, 0], TILE) * gy[0:1, :]
            for c in range(1, 12):
                s = c + 2 * (c // 6)
                gx = gx + wide_rows(mixes_back[layer, c], TILE) * gy[s : s + 1, :]
            gz[:, here] = gx
        return carry

    def moments(layer):
        acc = at["small_acc"][layer]
        part = acc[0:16] + acc[16:32] + acc[32:48]
        moment = part + pltpu.roll(part, 112, 1) + pltpu.roll(part, 96, 1)
        moment = jnp.where(lane < 16, moment, 0.0)
        for k in range(2):
            line = jnp.sum(at["sum_acc"][layer, k], axis=1, keepdims=True)
            moment = moment + jnp.where(lane == 16 + k, line, 0.0)
        return moment

    def early_sums():
        acc = at["prior_acc"][0:16] + at["prior_acc"][16:32] + at["prior_acc"][32:48]
        last = pltpu.roll(acc, 256 - 144, 1)
        taps_part = (acc + pltpu.roll(acc, 256 - 72, 1) + last)[:, 0:128]
        pieces = [moments(layer) for layer in range(1, layers)]
        pieces.append(
            jnp.where(lane < 72, taps_part, 0.0) + jnp.where(lane == 72, last[:, 0:128], 0.0)
        )
        depths = lax.fori_loop(0, depth_ref.shape[0], lambda k, c: c + depth_ref[k], jnp.int32(0))
        depths = jnp.broadcast_to(depths, (8, 128)).astype(f32)
        row8 = iota((8, 128), 0)
        logs = jnp.sum(at["like_acc"][...], axis=0, keepdims=True)
        pieces.append(jnp.where(row8 == 0, logs, 0.0) + jnp.where(row8 == 1, depths, 0.0))
        return jnp.concatenate(pieces, axis=0)

    running = []

    def advance_all():
        for group in running:
            group.advance()

    def launch(name):
        made[name].start()
        running.append(made[name])

    half = tiles // 2
    for layer in reversed(range(layers)):
        lax.fori_loop(0, tiles, functools.partial(back_a, layer), 0)
        at[f"out{layer}"][...] = at["gst"][0:128, :].T
        advance_all()
        launch(f"out{layer}")
        if not layer:
            early.hop()
        lax.fori_loop(0, tiles, functools.partial(back_b, layer), 0)
        advance_all()
        launch(f"mid{layer}")
        if not layer:
            early_total = early.finish(1)
        lax.fori_loop(0, half, functools.partial(back_c, layer), 0)
        advance_all()
        lax.fori_loop(half, tiles, functools.partial(back_c, layer), 0)
        column = jnp.sum(at["bone_acc"][...], axis=1, keepdims=True)
        at[f"inn{layer}"][...] = jnp.where(
            iota((hid, 128), 1) == 217 - 128, column, at["gst"][128:SMALL, :].T
        )
        if layer:
            advance_all()
            launch(f"inn{layer}")
            at["gst"][...] = jnp.zeros_like(at["gst"])
            at["bone_acc"][...] = jnp.zeros_like(at["bone_acc"])
            if layer == 1:
                early.start(0, early_sums())
        else:
            late.start(0, moments(0))
            launch("inn0")
    advance_all()
    late.hop()
    while any(group.stage < 4 for group in running):
        advance_all()
    late_total = late.finish(1)
    for layer in range(layers):
        at["grad"][layer, :, 0:hid] = made[f"mid{layer}"].out[...]
        at["grad"][layer, :, hid : hid + 128] = made[f"out{layer}"].out[...]
        at["grad"][layer, :, hid + 128 : hid + SMALL] = made[f"inn{layer}"].out[...]
    whole = jnp.concatenate([late_total, early_total], axis=0)
    rows = whole.shape[0]
    at["sums"][...] = whole + jnp.where(iota((rows, 128), 0) == rows - 8 + 2, penalty, 0.0)


def adamw(weight, grad, first, second, fixes):
    first_new = beta_one * first + (1.0 - beta_one) * grad
    second_new = beta_two * second + (1.0 - beta_two) * grad * grad
    update = first_new / fixes[0] / (jnp.sqrt(second_new / fixes[1]) + epsilon) + decay_rate * weight
    return (weight - learn_rate * update, first_new, second_new)


def update_kernel(total, images, step_ref, grad_ref, sums_ref, *refs):
    weights, firsts, seconds, loss_ref, outs = refs[0:6], refs[6:12], refs[12:18], refs[18], refs[19:]
    layers, share, _ = grad_ref.shape
    hid = weights[1].shape[2]
    coeff = -1.0 / (total * 12 * math.log(2.0))
    power = iota((8, 128), 1)
    used = power < jnp.broadcast_to(step_ref[0], (8, 128))
    fixes = tuple(
        (1.0 - beta)
        * jnp.sum(
            jnp.where(used, jnp.exp(power.astype(f32) * math.log(beta)), 0.0), axis=1, keepdims=True
        )[0:1]
        for beta in (beta_one, beta_two)
    )

    def write(which, at, grad):
        new = adamw(weights[which][at], grad, firsts[which][at], seconds[which][at], fixes)
        for k in range(3):
            outs[3 * which + k][at] = new[k]

    def column(layer):
        return (slice(None), layer, slice(None))

    place = spread(164, SMALL)
    to_slots = spread_rows(16, 12)
    reverse = jnp.where(slot(11 - iota((16, 12), 1)) == iota((16, 12), 0), 1.0, 0.0)
    row, col = iota((12, 12), 0), iota((12, 12), 1)
    eye = row == col
    logdet = jnp.zeros((1, 1), f32)
    for layer in range(layers):
        write(1, layer, grad_ref[layer, :, 0:hid])
        part = grad_ref[layer, :, hid : hid + SMALL]
        write(0, column(layer), dot_nt(place[108:162], part, highest))
        write(2, layer, dot_nt(part, place[0:108], highest))
        write(3, layer, dot_nt(place[162:164], part, highest))
        small = weights[4][column(layer)]
        lu = small[:, 0:12]
        lower, upper = mixing_parts(lu)
        scale = jnp.exp(small[:, 13:14])
        scale_row = as_row(scale)
        sums = sums_ref[16 * layer : 16 * layer + 16]
        turned = dot_tn(reverse, sums, highest)
        moment = dot(turned[:, 0:16], to_slots, highest)
        ones = turned[:, 16:17]
        g_mix = (moment + ones * as_row(small[:, 12:13])) * scale_row
        mix = dot(lower, upper, highest)
        g_bias = scale * dot_tn(mix, ones, highest)
        g_scale = as_column(jnp.sum(mix * g_mix, axis=0, keepdims=True)) + coeff * total
        g_lower = dot_nt(g_mix, upper, highest)
        g_upper = dot_tn(lower, g_mix, highest)
        g_lu = jnp.where(row > col, g_lower, jnp.where(eye, g_upper * jnp.exp(lu) + coeff * total, g_upper))
        g_cb = dot_tn(to_slots, sums, highest)[:, 17:18]
        wide15 = iota((12, 15), 1)
        grad = dot(g_lu, jnp.where(iota((12, 15), 0) == wide15, 1.0, 0.0), highest)
        grad = jnp.where(wide15 == 12, g_bias, grad)
        grad = jnp.where(wide15 == 13, g_scale, grad)
        grad = jnp.where(wide15 == 14, g_cb, grad)
        write(4, column(layer), grad)
        diag = jnp.sum(jnp.where(eye, lu, 0.0), axis=0, keepdims=True) + as_row(small[:, 13:14])
        logdet = logdet + jnp.sum(diag, axis=1, keepdims=True)
    sums = sums_ref[16 * layers : 16 * layers + 16]
    grad = coeff * dot_nt(
        dot_tn(to_slots, sums, highest), spread(55, 128), highest
    )
    write(5, Ellipsis, grad)
    tail = sums_ref[16 * layers + 16 :]
    likely = jnp.sum(tail[0:1], axis=1, keepdims=True)
    likely = likely - total * 6.0 * math.log(2.0 * math.pi) + total * logdet
    loss_ref[...] = coeff * likely + tail[1:2, 0:1] / images + tail[2:3, 0:1]


def as_column(row):
    n = row.shape[1]
    eye = iota((n, n), 0) == iota((n, n), 1)
    return jnp.sum(jnp.where(eye, row, 0.0), axis=1, keepdims=True)


def turn(arrays, back=False):
    orders = ((1, 2, 0) if back else (2, 0, 1), None, (0, 2, 1), None, (1, 0, 2), None)
    return tuple(a if o is None else jnp.transpose(a, o) for a, o in zip(arrays, orders))


def shards(*args, wide, narrow):
    pixels, noise, depth, step_count = args[0:4]
    params, firsts, seconds = turn(args[4:10]), turn(args[10:16]), turn(args[16:22])
    layers, share, hid = params[1].shape
    count = pixels.shape[1]
    chips = max(wide // 2, 1)
    width = hid + SMALL
    early = 16 * layers + 8
    rows = early + 16
    dma = pltpu.SemaphoreType.DMA
    names = ["pixels", "noise", "depth", "small", "prior", "in", "mid", "out", "bias", "grad", "sums"]
    scratch = []

    def add(name, kind):
        names.append(name)
        scratch.append(kind)

    def sems(name, shape):
        add(name + "_send", dma(shape))
        add(name + "_recv", dma(shape))

    for name, shape, dtype in (
        ("wall", (layers, hid, width), bf16),
        ("wmt", (layers, hid, hid), bf16),
        ("wst", (layers, SMALL, hid), bf16),
        ("win", (layers, hid, 128), bf16),
        ("bone", (layers, hid, 128), f32),
        ("mixes", (layers, 14, 16, 128), f32),
        ("mixes_back", (layers, 12, 16, 128), f32),
        ("prior_fwd", (48, 256), bf16),
        ("prior_back", (224, 48), bf16),
        ("masks", (4, 8, TILE), f32),
        ("states", (layers + 1, 16, count), f32),
        ("keep", (layers, 16, count), f32),
        ("taps_in", (layers, 80, count), bf16),
        ("hidden_one", (layers, hid, count), bf16),
        ("hidden_two", (layers, hid, count), bf16),
        ("gz", (16, count), f32),
        ("stat_acc", (2, 16, 128), f32),
        ("like_acc", (8, 128), f32),
        ("prior_acc", (48, 256), f32),
        ("small_acc", (layers, 48, 128), f32),
        ("sum_acc", (layers, 2, 16, 128), f32),
        ("bone_acc", (hid, 128), f32),
        ("gst", (SMALL, hid), f32),
    ):
        add(name, pltpu.VMEM(shape, dtype))
    for name, height in (("stat", 16), ("early", early), ("late", 16)):
        add(name + "_w", pltpu.VMEM((wide, height, 128), f32))
        add(name + "_n", pltpu.VMEM((narrow, height, 128), f32))
        sems(name + "_sw", (wide,))
        sems(name + "_sn", (narrow,))
    groups = []
    piece = share // narrow if share % (8 * narrow) == 0 else share
    for layer in range(layers):
        for kind, across in (("mid", hid), ("out", 128), ("inn", 128)):
            name = f"{kind}{layer}"
            groups.append(name)
            add(name, pltpu.VMEM((hid, across), f32))
            add(name + "_p", pltpu.VMEM((chips, share, across), f32))
            add(name + "_c", pltpu.VMEM((chips, share, across), f32))
            add(name + "_n", pltpu.VMEM((narrow, piece, across), f32))
            add(name + "_out", pltpu.VMEM((share, across), f32))
            for stage, size in enumerate((chips, chips, narrow, narrow)):
                sems(f"{name}_s{stage}", (size,))
    sems("ga", (2 * chips,))
    sems("gb", (layers, wide))
    remote = {"collective_id": 0, "has_side_effects": True} if wide > 1 else {}
    grads, sums = pl.pallas_call(
        functools.partial(flow_kernel, wide, narrow, (names, groups)),
        out_shape=(
            jax.ShapeDtypeStruct((layers, share, width), f32),
            jax.ShapeDtypeStruct((rows, 128), f32),
        ),
        in_specs=[VMEM, VMEM, SMEM] + [VMEM] * 6,
        out_specs=(VMEM, VMEM),
        scratch_shapes=scratch,
        compiler_params=pltpu.CompilerParams(vmem_limit_bytes=FLOW_VMEM, **remote),
        name="flow",
    )(pixels, noise, depth, params[4], params[5], *params[0:4])
    total = count * wide * narrow
    shapes = [jax.ShapeDtypeStruct((1, 1), f32)]
    for p in params:
        shapes += [jax.ShapeDtypeStruct(p.shape, f32)] * 3
    results = pl.pallas_call(
        functools.partial(update_kernel, total, total // 256),
        out_shape=tuple(shapes),
        in_specs=[SMEM] + [VMEM] * 20,
        out_specs=(VMEM,) * 19,
        compiler_params=pltpu.CompilerParams(vmem_limit_bytes=UPDATE_VMEM),
        name="update",
    )(step_count.reshape(1), grads, sums, *params, *firsts, *seconds)
    updated = [turn(results[1 + k :: 3], True) for k in range(3)]
    return (results[0].reshape(()),) + tuple(updated[k][p] for p in range(6) for k in range(3))


def solution(mesh):
    weights = (P(None, "wide", None), P(None, "wide", None), P(None, None, "wide"), P(None, None, "wide"), P(), P())
    return jax.shard_map(
        functools.partial(shards, wide=mesh.shape["wide"], narrow=mesh.shape["narrow"]),
        mesh=mesh,
        in_specs=(
            P(None, ("narrow", "wide")),
            P(None, ("narrow", "wide")),
            P(("narrow", "wide")),
            P(),
        )
        + weights * 3,
        out_specs=(P(),) + tuple(w for w in weights for _ in range(3)),
        check_vma=False,
    )
```

```python
import functools
import math
from types import SimpleNamespace

import jax
import jax.numpy as jnp
from jax import lax
from jax.experimental import pallas as pl
from jax.experimental.pallas import tpu as pltpu
from jax.sharding import PartitionSpec as P

f32 = jnp.float32
bf16 = jnp.bfloat16
highest = lax.Precision.HIGHEST
MESH = pl.DeviceIdType.MESH
learn_rate = 0.02
beta_one = 0.9
beta_two = 0.999
epsilon = 1e-08
decay_rate = 0.01
penalty_weight = 0.5
tap_offsets = [(r, c) for r in (-1, 0, 1) for c in (-1, 0, 1)]
TILE = 2048
FLOW_VMEM = 62 * 1024 * 1024
UPDATE_VMEM = 60 * 1024 * 1024
OUT = 144
SMALL = 256
VMEM = pl.BlockSpec(memory_space=pltpu.VMEM)
SMEM = pl.BlockSpec(memory_space=pltpu.SMEM)
HBM = pl.BlockSpec(memory_space=pl.ANY)
WIDE, NARROW = "wide", "narrow"


def dot(a, b, precision=None):
    return lax.dot_general(
        a, b, (((1,), (0,)), ((), ())), preferred_element_type=f32, precision=precision
    )


def dot_nt(a, b, precision=None):
    return lax.dot_general(
        a, b, (((1,), (1,)), ((), ())), preferred_element_type=f32, precision=precision
    )


def dot_tn(a, b, precision=None):
    return lax.dot_general(
        a, b, (((0,), (0,)), ((), ())), preferred_element_type=f32, precision=precision
    )


def iota(shape, axis):
    return lax.broadcasted_iota(jnp.int32, shape, axis)


def slot(s):
    return s + 2 * ((s * 10923) >> 16)


def spread(count, width, first=0):
    return jnp.where(slot(iota((count, width), 0) + first) == iota((count, width), 1), 1.0, 0.0)


def spread_rows(height, count):
    return jnp.where(slot(iota((height, count), 1)) == iota((height, count), 0), 1.0, 0.0)


def split_two(v):
    high = v.astype(bf16).astype(f32)
    return high, v - high


def as_row(column):
    n = column.shape[0]
    eye = iota((n, n), 0) == iota((n, n), 1)
    return jnp.sum(jnp.where(eye, column, 0.0), axis=0, keepdims=True)


def as_column(row):
    n = row.shape[1]
    eye = iota((n, n), 0) == iota((n, n), 1)
    return jnp.sum(jnp.where(eye, row, 0.0), axis=1, keepdims=True)


def mixing_parts(lu):
    n = lu.shape[0]
    row, col = iota((n, n), 0), iota((n, n), 1)
    lower = jnp.where(row > col, lu, 0.0) + jnp.where(row == col, 1.0, 0.0)
    upper = jnp.where(row < col, lu, 0.0) + jnp.where(row == col, jnp.exp(lu), 0.0)
    return lower, upper


def wide_rows(v, lanes):
    return jnp.concatenate([v] * (lanes // 128), axis=1)


class Shifts:
    def __init__(self, mask_ref, lanes):
        self.lanes = lanes
        self.masks = mask_ref

    def mask(self, which, rows):
        m = self.masks[which, :, 0 : self.lanes]
        return jnp.concatenate([m] * (rows // 8), axis=0) if rows > 8 else m

    def col(self, v, c):
        if c == 0:
            return v
        moved = pltpu.roll(v, (-c) % self.lanes, 1)
        return moved * self.mask(0 if c > 0 else 1, v.shape[0])

    def row(self, v, r):
        if r == 0:
            return v
        moved = pltpu.roll(v, (-16 * r) % self.lanes, 1)
        return moved * self.mask(2 if r > 0 else 3, v.shape[0])

    def taps(self, v, sign=1):
        by_col = {c: self.col(v, c) for c in (-1, 0, 1)}
        return [self.row(by_col[sign * c], sign * r) for r, c in tap_offsets]

    def fold(self, pieces, sign=1):
        total = None
        for c in (-1, 0, 1):
            part = None
            for r in (-1, 0, 1):
                piece = self.row(pieces[3 * (r + 1) + (c + 1)], sign * r)
                part = piece if part is None else part + piece
            part = self.col(part, sign * c)
            total = part if total is None else total + part
        return total


def fill_masks(mask_ref):
    lanes = mask_ref.shape[2]
    pos = iota((8, lanes), 1)
    row, col = (pos >> 4) & 15, pos & 15
    for which, keep in enumerate((col < 15, col > 0, row < 15, row > 0)):
        mask_ref[which] = jnp.where(keep, 1.0, 0.0)


def flow_kernel(wide, narrow, tree, *refs):
    hbm, grads, at = (SimpleNamespace(**part) for part in jax.tree.unflatten(tree, refs))
    wmid, wsmall, wmt, wst, win = at.wmid, at.wsmall, at.wmt, at.wst, at.win
    bone, mixes, mixes_back = at.bone, at.mixes, at.mixes_back
    gz, gy_ref, d3, tbuf = at.gz, at.gy, at.d3, at.tbuf
    given = SimpleNamespace(**at.given)
    layers, share, hid = given.mid.shape
    count = given.pixels.shape[1]
    total = count * wide * narrow
    coeff = -1.0 / (total * 12 * math.log(2.0))
    chips = max(wide // 2, 1)
    me_w = lax.axis_index(WIDE) if wide > 1 else 0
    me_n = lax.axis_index(NARROW) if narrow > 1 else 0
    chip, core = (me_w // 2, lax.rem(me_w, 2)) if wide > 1 else (0, 0)
    shifts = Shifts(at.masks, TILE)

    def block(index):
        return pl.ds(pl.multiple_of(index * share, share), share)

    def tile_at(t):
        return pl.ds(pl.multiple_of(t * TILE, TILE), TILE)

    def ahead(size, me, d):
        return lax.rem(me + d, size)

    def behind(size, me, d):
        return lax.rem(me + size - d, size)

    def each(first, size, fn):
        if wide > 1 and size > first:
            lax.fori_loop(first, size, lambda d, c: (fn(d), c)[1], 0)

    def remote(src, dst, sems, index, device):
        return pltpu.make_async_remote_copy(
            src_ref=src,
            dst_ref=dst,
            send_sem=sems[0].at[index],
            recv_sem=sems[1].at[index],
            device_id=device,
            device_id_type=MESH,
        )

    def drain(ref, sem):
        if wide > 1:
            pltpu.make_async_copy(ref, ref, sem.at[0]).wait()

    class Exchange:
        def __init__(self, bufs, sems):
            self.bufs, self.sems = bufs, sems

        def copy(self, phase, d):
            axis, size, me = ((WIDE, wide, me_w), (NARROW, narrow, me_n))[phase]
            row = self.bufs[phase].at[me]
            return remote(row, row, self.sems[phase], 0, {axis: ahead(size, me, d)})

        def start(self, phase, value):
            me, size = ((me_w, wide), (me_n, narrow))[phase]
            self.bufs[phase][me] = value
            each(1, size, lambda d: self.copy(phase, d).start())

        def finish(self, phase):
            size = (wide, narrow)[phase]
            if size > 1:
                for sem in self.sems[phase]:
                    drain(self.bufs[phase].at[1:size], sem)
            value = self.bufs[phase][0]
            for k in range(1, size):
                value = value + self.bufs[phase][k]
            return value

        def hop(self):
            self.start(1, self.finish(0))

    class OneShot:
        def __init__(self, rows, sems):
            self.rows, self.sems = rows, sems

        def copy(self, d):
            by_n, by_w = d // wide, lax.rem(d, wide)
            row = self.rows.at[me_n * wide + me_w]
            device = {NARROW: ahead(narrow, me_n, by_n), WIDE: ahead(wide, me_w, by_w)}
            return remote(row, row, self.sems, 0, device)

        def start(self, value):
            self.rows[me_n * wide + me_w] = value
            each(1, wide * narrow, lambda d: self.copy(d).start())

        def finish(self):
            if wide > 1:
                for sem in self.sems:
                    drain(self.rows.at[1 : wide * narrow], sem)
            return lax.fori_loop(
                0, wide * narrow, lambda k, c: c + self.rows[k], jnp.zeros(self.rows.shape[1:], f32)
            )

    stat, late = OneShot(*at.stat), OneShot(*at.late)
    early = Exchange(*at.early)

    class Group:
        def __init__(self, refs):
            self.full, self.pair, self.chip, self.part, self.out = refs[0:5]
            self.sems = refs[5]
            self.piece = self.part.shape[1]
            self.scatter = self.piece < share
            self.stage = 0
            self.last = 3 if self.scatter else 2

        def mine(self, index):
            return pl.ds(pl.multiple_of(index * self.piece, 8), self.piece)

        def start(self):
            sems = self.sems[self.stage]
            if self.stage == 0:
                if wide > 1:
                    theirs = self.full.at[:, 1 - core]
                    remote(theirs, self.pair, sems, 0, {WIDE: me_w + 1 - 2 * core}).start()
                return

            def go(d):
                if self.stage == 1:
                    to = ahead(chips, chip, d)
                    remote(self.full.at[to, core], self.chip.at[d - 1], sems, 0, {WIDE: 2 * to + core}).start()
                    return
                to = ahead(narrow, me_n, d)
                if self.stage == 2 and self.scatter:
                    rows = self.full.at[chip, core, self.mine(to)]
                    remote(rows, self.part.at[d - 1], sems, 0, {NARROW: to}).start()
                    return
                ref = self.part.at[me_n] if self.stage == 2 else self.out.at[self.mine(me_n)]
                remote(ref, ref, sems, 0, {NARROW: to}).start()

            each(1, chips if self.stage == 1 else narrow, go)

        def finish(self):
            if self.stage == 0:
                come = self.pair
            elif self.stage == 1:
                come = self.chip.at[0 : chips - 1] if chips > 1 else None
            elif self.stage == 2:
                come = self.part.at[0 : narrow - 1] if narrow > 1 else None
            else:
                come = self.out.at[0 : (narrow - 1) * self.piece] if narrow > 1 else None
            if come is not None:
                for sem in self.sems[self.stage]:
                    drain(come, sem)
            own = (chip, core)
            if self.stage == 0:

                def add(d):
                    self.full[d, core] += self.pair[d]

                each(0, chips, add)
            if self.stage == 1:
                value = self.full[own]
                for d in range(chips - 1):
                    value = value + self.chip[d]
                if self.scatter:
                    self.full[own] = value
                else:
                    self.part[me_n] = value
            if self.stage == 2:
                value = self.full[chip, core, self.mine(me_n)] if self.scatter else self.part[0]
                for d in range(0 if self.scatter else 1, narrow - 1 if self.scatter else narrow):
                    value = value + self.part[d]
                self.out[self.mine(me_n) if self.scatter else slice(None)] = value
            self.stage += 1

        def put(self, value):
            self.full[...] = value.reshape(self.full.shape)

        def add(self, value):
            self.full[...] += value.reshape(self.full.shape)

        def advance(self):
            self.finish()
            if self.stage <= self.last:
                self.start()

    mid, out, inn = ([Group(refs) for refs in kind] for kind in (at.mid, at.out, at.inn))

    if wide > 1:
        barrier = pltpu.get_barrier_semaphore()
        each(
            1,
            wide * narrow,
            lambda d: pl.semaphore_signal(
                barrier,
                inc=1,
                device_id={
                    NARROW: ahead(narrow, me_n, d // wide),
                    WIDE: ahead(wide, me_w, lax.rem(d, wide)),
                },
                device_id_type=MESH,
            ),
        )
    loads = {
        name: pltpu.make_async_copy(source_ref, at.given[name], at.load.at[k])
        for k, (name, source_ref) in enumerate(vars(hbm).items())
    }
    for copy in loads.values():
        copy.start()
    loads = SimpleNamespace(**loads)

    place = spread(164, SMALL).astype(bf16)
    for copy in (loads.mid, loads.first, loads.out, loads.bias):
        copy.wait()
    for layer in range(layers):
        small_part = (
            dot(given.out[layer].astype(bf16), place[0:108])
            + dot_tn(given.first[:, layer, :].astype(bf16), place[108:162])
            + dot_tn(given.bias[layer].astype(bf16), place[162:164])
        )
        wmid[layer, block(me_w)] = given.mid[layer].astype(bf16)
        wsmall[layer, block(me_w)] = small_part.astype(bf16)

    class Spread:
        def __init__(self, weights, sems):
            self.weights, self.sems = weights, sems

        def to_chip(self, d, coming=False):
            index = 2 * (behind(chips, chip, d) if coming else chip) + core
            rows = self.weights.at[0, block(index)]
            return remote(rows, rows, self.sems, d, {WIDE: 2 * ahead(chips, chip, d) + core})

        def to_core(self, d, coming=False):
            index = 2 * behind(chips, chip, d) + (1 - core if coming else core)
            rows = self.weights.at[0, block(index)]
            return remote(rows, rows, self.sems, chips + d, {WIDE: me_w + 1 - 2 * core})

        def start(self):
            each(1, chips, lambda d: self.to_chip(d).start())
            each(0, 1, lambda d: self.to_core(d).start())

        def pass_on(self):
            def one(d):
                self.to_chip(d).wait_send()
                self.to_chip(d, True).wait_recv()
                self.to_core(d).start()

            each(1, chips, one)

        def finish(self):
            def one(d):
                self.to_core(d).wait_send()
                self.to_core(d, True).wait_recv()

            each(0, chips, one)

    spread_small, spread_mid = Spread(wsmall, at.spread[0]), Spread(wmid, at.spread[1])

    def to_all(weights, sems, layer, d):
        rows = weights.at[layer, block(me_w)]
        return remote(rows, rows, sems[layer], 0, {WIDE: ahead(wide, me_w, d)})

    later = ((wsmall, at.later[0]), (wmid, at.later[1]))

    if wide > 1:
        pl.semaphore_wait(barrier, wide * narrow - 1)
        spread_small.start()
        spread_mid.start()

    fill_masks(at.masks)
    loads.small.wait()
    to_slots = spread_rows(16, 12)
    reverse = jnp.where(slot(11 - iota((16, 12), 1)) == iota((16, 12), 0), 1.0, 0.0)
    for layer in range(layers):
        small = given.small[:, layer, :]
        lower, upper = mixing_parts(small[:, 0:12])
        scale = jnp.exp(small[:, 13:14])
        mixed = dot(reverse, dot(lower, upper, highest), highest) * as_row(scale)
        const = jnp.sum(mixed * as_row(small[:, 12:13]), axis=1, keepdims=True)
        cb = jnp.sum(to_slots * as_row(small[:, 14:15]), axis=1, keepdims=True)
        for c in range(12):
            mixes[layer, c] = jnp.broadcast_to(mixed[:, c : c + 1], (16, 128))
        mixes[layer, 12] = jnp.broadcast_to(const, (16, 128))
        mixes[layer, 13] = jnp.broadcast_to(cb, (16, 128))
        if layer:
            back = dot_nt(to_slots, mixed, highest)
            for c in range(12):
                s = c + 2 * (c // 6)
                mixes_back[layer, c] = jnp.broadcast_to(back[:, s : s + 1], (16, 128))

    def by_lanes(v):
        parts = [v[:, 128 * k : 128 * k + 128] for k in range(v.shape[1] // 128)]
        while len(parts) > 1:
            parts = [a + b for a, b in zip(parts[0::2], parts[1::2])]
        return parts[0]

    real = jnp.where(iota((8, 128), 0) < 6, 1.0, 0.0)
    first_row = jnp.where(iota((8, TILE), 0) == 0, 1.0, 0.0)

    def enter(layer, here, x):
        at.x[layer][:, here] = x
        y = wide_rows(mixes[layer, 12], TILE)
        for c in range(12):
            s = c + 2 * (c // 6)
            y = y + wide_rows(mixes[layer, c], TILE) * x[s : s + 1, :]
        taps = jnp.concatenate(shifts.taps(y[0:8]) + [first_row], axis=0)
        at.taps[layer][:, here] = taps.astype(bf16)
        at.x[layer + 1][0:8, here] = y[0:8]
        at.keep[layer][0:8, here] = y[8:16]

    def pixels_in(t, carry):
        images = TILE // 256
        blank = jnp.zeros((2, 256), f32)
        chunks = []
        for k in range(images):
            coarse = given.depth[t * images + k] == 5
            by = jnp.where(coarse, 3, 0)
            level = jnp.where(coarse, 1.0 / 32.0, 1.0 / 256.0).astype(f32)
            at_image = pl.ds(pl.multiple_of(t * TILE + k * 256, 256), 256)
            quant = lax.shift_right_logical(given.pixels[:, at_image], jnp.broadcast_to(by, (12, 256)))
            x = (quant.astype(f32) + given.noise[:, at_image]) * level - 0.5
            chunks.append(jnp.concatenate([x[0:6], blank, x[6:12], blank], axis=0))
        enter(0, tile_at(t), jnp.concatenate(chunks, axis=1))
        return carry

    tiles = count // TILE
    half = tiles // 2

    def run(first, end, body):
        lax.fori_loop(first, end, lambda t, c: (body(t), c)[1], 0)

    def piped(first, end, lead, follow):
        lead(first)

        def both(t):
            follow(t - 1)
            lead(t)

        run(first + 1, end, both)
        follow(end - 1)

    for copy in (loads.depth, loads.pixels, loads.noise, loads.prior):
        copy.wait()
    lax.fori_loop(0, tiles, pixels_in, 0)
    spread_small.pass_on()

    prior = given.prior[...]
    s = iota((55, 256), 0)
    lane = iota((55, 256), 1)
    hit = (slot(s) == lane) | (slot(s) + 72 == lane)
    to_taps = jnp.where(((s < 54) & hit) | ((s == 54) & (lane == 144)), 1.0, 0.0)
    prior_slots = dot(to_slots, prior, highest)
    parts = split_two(dot(prior_slots, to_taps, highest))
    at.prior_fwd[...] = jnp.concatenate(parts, axis=0).astype(bf16)
    turned = dot_nt(spread_rows(72, 55), prior_slots, highest)
    stacked = jnp.concatenate(split_two(turned), axis=0)
    again = jnp.where((iota((16, 32), 1) & 15) == iota((16, 32), 0), 1.0, 0.0)
    at.prior_back[...] = dot(stacked.astype(bf16), again.astype(bf16)).astype(bf16)

    whole = [group.full for group in mid + out]
    sums = [at.stat_acc, at.like_acc, at.prior_acc, at.small_acc, at.sum_acc, at.acc_in]
    for ref in whole + sums + at.bone_acc + at.acc_rest:
        ref[...] = jnp.zeros_like(ref)

    pick = jnp.where(iota((SMALL, 128), 0) == iota((SMALL, 128), 1) + OUT, 1.0, 0.0).astype(bf16)

    def derive(layer):
        w = wsmall[layer]
        win[layer] = dot(w, pick).astype(bf16)
        wst[layer] = w.T
        bone[layer] = jnp.broadcast_to(w[:, 217:218].astype(f32), (hid, 128))

    def hidden_first(layer, t):
        here = tile_at(t)
        first = dot(win[layer, :, 0:80], at.taps[layer][:, here]).astype(bf16)
        h1 = jnp.maximum(first, jnp.zeros_like(first))
        at.one[layer][:, here] = h1
        return h1

    def forward_products(layer, t):
        here = tile_at(t)
        h1 = hidden_first(layer, t) if layer else at.one[0][:, here]
        second = dot(wmid[layer], h1) + wide_rows(bone[layer], TILE)
        h2 = jnp.maximum(second, 0.0).astype(bf16)
        at.two[layer][:, here] = h2
        tbuf[...] = dot(wst[layer, 0:OUT, :], h2)

    def forward_rest(layer, t):
        here = tile_at(t)
        o = shifts.fold([tbuf[16 * k : 16 * k + 16] for k in range(9)])
        o = o + wide_rows(mixes[layer, 13], TILE)
        v = at.keep[layer][0:8, here] + o[0:8]
        decay = 1.0 + jnp.exp(-(o[8:16] + 2.0))
        q = 1.0 / decay
        at.like_acc[...] -= by_lanes(jnp.log(decay)) * real
        at.keep[layer][0:8, here] = v
        at.keep[layer][8:16, here] = q
        x = jnp.concatenate([at.x[layer + 1][0:8, here], v * q], axis=0)
        if layer < layers - 1:
            enter(layer + 1, here, x)
        else:
            at.x[layer + 1][8:16, here] = x[8:16]
            at.stat_acc[0] += by_lanes(x)
            at.stat_acc[1] += by_lanes(x * x)

    spread_small.finish()
    for layer in range(1, layers):
        for weights, sems in later:
            each(1, wide, lambda d: to_all(weights, sems, layer, d).start())
    derive(0)
    run(0, half, functools.partial(hidden_first, 0))
    spread_mid.pass_on()
    run(half, tiles, functools.partial(hidden_first, 0))
    spread_mid.finish()
    for layer in range(layers):
        if layer:
            for weights, sems in later:

                if wide > 1:
                    for sem in sems[layer]:
                        drain(weights.at[layer, 0 : (wide - 1) * share], sem)
            derive(layer)
        piped(0, tiles, functools.partial(forward_products, layer), functools.partial(forward_rest, layer))

    lane = iota((16, 128), 1)

    line = iota((16, 128), 0)
    row = jnp.where(lane == line, jnp.sum(at.stat_acc[0], axis=1, keepdims=True), 0.0)
    row = row + jnp.where(lane == line + 16, jnp.sum(at.stat_acc[1], axis=1, keepdims=True), 0.0)
    stat.start(jnp.sum(row, axis=0, keepdims=True))

    def prior_tile(t):
        here = tile_at(t)
        z1 = at.x[layers][0:8, here]
        z2 = at.x[layers][8:16, here]
        pieces = [split_two(v) for v in shifts.taps(z1)]
        tz = jnp.concatenate(
            [p[0] for p in pieces] + [p[1] for p in pieces] + [first_row, jnp.zeros_like(first_row)], axis=0
        ).astype(bf16)
        both = dot(at.prior_fwd[:, 0:160], tz)
        value = both[0:16] + both[16:32]
        centre, log_sd = value[0:8], value[8:16]
        inverse = jnp.exp(-log_sd)
        ratio = (z2 - centre) * inverse
        at.like_acc[...] += by_lanes(-0.5 * z1 * z1 - 0.5 * ratio * ratio - log_sd)
        d_centre = ratio * inverse
        d_stat = jnp.concatenate([d_centre, ratio * ratio - 1.0], axis=0)
        ds = jnp.concatenate(split_two(d_stat), axis=0).astype(bf16)
        at.prior_acc[:, 0:160] += dot_nt(ds, tz)
        dt = dot(at.prior_back[...], ds)
        dt = dt[0:72] + dt[72:144]
        folded = shifts.fold([dt[8 * k : 8 * k + 8] for k in range(9)], -1)
        gz[0:8, here] = coeff * (folded - z1)
        gz[8:16, here] = -coeff * d_centre

    run(0, tiles, prior_tile)
    for layer in range(layers):
        wmt[layer] = wmid[layer].T
    stats = stat.finish()
    mean = jnp.sum(jnp.where(lane == line, stats, 0.0), axis=1, keepdims=True) / total
    square = jnp.sum(jnp.where(lane == line + 16, stats, 0.0), axis=1, keepdims=True) / total
    var = square - mean * mean
    from_first = penalty_weight * (2.0 * mean - 4.0 * (var - 1.0) * mean) / total
    from_square = penalty_weight * 2.0 * (var - 1.0) / total
    ones_rows = jnp.where((iota((16, 1), 0) & 7) < 6, 1.0, 0.0)
    penalty = penalty_weight * jnp.sum(
        ones_rows * (mean * mean + (var - 1.0) * (var - 1.0)), axis=0, keepdims=True
    )

    def prepare_back(layer, here, g):
        v = at.keep[layer][0:8, here]
        q = at.keep[layer][8:16, here]
        gbq = g[8:16] * q
        gy_ref[0:8, here] = g[0:8]
        gy_ref[8:16, here] = gbq
        do = jnp.concatenate([gbq, (gbq * v + coeff) * (1.0 - q)], axis=0)
        at.sum_acc[layer, 1] += by_lanes(do)
        rounded = do.astype(bf16).astype(f32)
        d3[:, here] = jnp.concatenate(shifts.taps(rounded, -1), axis=0).astype(bf16)

    def last_gradient(t):
        here = tile_at(t)
        g = gz[:, here] + from_first + 2.0 * at.x[layers][:, here] * from_square
        prepare_back(layers - 1, here, g)

    def back_a(layer, t):
        here = tile_at(t)
        h2 = at.two[layer][:, here]
        taps = d3[:, here]
        grad = dot_nt(h2, taps)
        out[layer].add(grad[:, 0:128])
        at.acc_rest[layer][:, 0:16] += grad[:, 128:OUT]
        dd2 = dot(wsmall[layer, :, 0:OUT], taps).astype(bf16)
        at.two[layer][:, here] = jnp.where(h2 > 0, dd2, jnp.zeros_like(dd2))

    def back_b(layer, t):
        here = tile_at(t)
        d2 = at.two[layer][:, here]
        mid[layer].add(dot_nt(d2, at.one[layer][:, here]))
        at.bone_acc[layer][...] += by_lanes(d2.astype(f32))

    def back_c(layer, t):
        here = tile_at(t)
        dd1 = dot(wmt[layer], at.two[layer][:, here]).astype(bf16)
        h1 = at.one[layer][:, here]
        at.one[layer][:, here] = jnp.where(h1 > 0, dd1, jnp.zeros_like(dd1))

    def back_in(layer, t):
        here = tile_at(t)
        at.acc_in[:, 0:80] += dot_nt(at.one[layer][:, here], at.taps[layer][:, here])

    def back_taps(layer, t):
        tbuf[0:80] = dot(wst[layer, OUT : OUT + 80, :], at.one[layer][:, tile_at(t)])

    def back_rest(layer, t):
        here = tile_at(t)
        gya = gy_ref[0:8, here] + shifts.fold([tbuf[8 * k : 8 * k + 8] for k in range(9)], -1)
        gy = jnp.concatenate([gya, gy_ref[8:16, here]], axis=0)
        at.sum_acc[layer, 0] += by_lanes(gy)
        left = jnp.concatenate(split_two(gy), axis=0).astype(bf16)
        right = jnp.concatenate(split_two(at.x[layer][:, here]), axis=0).astype(bf16)
        at.small_acc[layer, :, 0:32] += dot_nt(left, right)
        if layer:
            gx = wide_rows(mixes_back[layer, 0], TILE) * gy[0:1, :]
            for c in range(1, 12):
                s = c + 2 * (c // 6)
                gx = gx + wide_rows(mixes_back[layer, c], TILE) * gy[s : s + 1, :]
            prepare_back(layer - 1, here, gx)

    def inner_gradient(layer):
        column = jnp.sum(at.bone_acc[layer][...], axis=1, keepdims=True)
        grad = at.acc_rest[layer][...] + pltpu.roll(at.acc_in[...], 16, 1)
        inn[layer].put(grad + jnp.where(iota((hid, 128), 1) == 217 - 128, column, 0.0))
        if layer:
            at.acc_in[...] = jnp.zeros_like(at.acc_in)

    def moments(layer):
        acc = at.small_acc[layer]
        part = acc[0:16] + acc[16:32]
        moment = jnp.where(lane < 16, part + pltpu.roll(part, 112, 1), 0.0)
        for k in range(2):
            line = jnp.sum(at.sum_acc[layer, k], axis=1, keepdims=True)
            moment = moment + jnp.where(lane == 16 + k, line, 0.0)
        return moment

    def early_sums():
        acc = at.prior_acc[0:16] + at.prior_acc[16:32]
        taps_part = (acc + pltpu.roll(acc, 256 - 72, 1))[:, 0:128]
        last = pltpu.roll(acc, 256 - 72, 1)[:, 0:128]
        pieces = [moments(layer) for layer in range(1, layers)]
        pieces.append(jnp.where(lane < 72, taps_part, 0.0) + jnp.where(lane == 72, last, 0.0))
        depths = lax.fori_loop(0, given.depth.shape[0], lambda k, c: c + given.depth[k], jnp.int32(0))
        depths = jnp.broadcast_to(depths, (8, 128)).astype(f32)
        row8 = iota((8, 128), 0)
        logs = jnp.sum(at.like_acc[...], axis=0, keepdims=True)
        pieces.append(jnp.where(row8 == 0, logs, 0.0) + jnp.where(row8 == 1, depths, 0.0))
        return jnp.concatenate(pieces, axis=0)

    def go(*which):
        for group in which:
            group.advance()

    def loop(body, layer, first=0, end=tiles):
        run(first, end, functools.partial(body, layer))

    def rest_loop(layer, first, end):
        piped(first, end, functools.partial(back_taps, layer), functools.partial(back_rest, layer))

    def inner(layer):
        inner_gradient(layer)
        inn[layer].start()

    def packed(moment):
        value = jnp.zeros((2, 128), f32)
        for k in range(6):
            pair = jnp.concatenate([moment[k : k + 1], moment[8 + k : 9 + k]], axis=0)
            value = value + (pltpu.roll(pair, 20 * k, 1) if k else pair)
        return value

    def unpacked(value):
        blank = jnp.zeros((2, 128), f32)
        turns = [pltpu.roll(value, 128 - 20 * k, 1) if k else value for k in range(6)]
        rows = [turn[0:1] for turn in turns] + [blank] + [turn[1:2] for turn in turns] + [blank]
        return jnp.where(lane < 18, jnp.concatenate(rows, axis=0), 0.0)

    run(0, tiles, last_gradient)
    loop(back_a, 1)
    out[1].start()
    loop(back_b, 1)
    mid[1].start()
    go(out[1])
    loop(back_c, 1, 0, half)
    go(mid[1])
    loop(back_c, 1, half, tiles)
    go(out[1])
    rest_loop(1, 0, tiles)
    early.start(0, early_sums())
    loop(back_a, 0)
    out[0].start()
    go(mid[1], out[1])
    early.hop()
    loop(back_b, 0)
    mid[0].start()
    go(out[0], out[1])
    loop(back_in, 1, 0, half)
    go(mid[0])
    loop(back_in, 1, half, tiles)
    inner(1)
    go(mid[1])
    early_total = early.finish(1)
    loop(back_c, 0, 0, half)
    go(inn[1], out[0])
    loop(back_c, 0, half, tiles)
    loop(back_in, 0, 0, half)
    go(mid[0], inn[1])
    loop(back_in, 0, half, tiles)
    inner(0)
    go(mid[1], out[0])
    rest_loop(0, 0, half)
    go(inn[0])
    rest_loop(0, half, tiles)
    late.start(packed(moments(0)))
    go(mid[0], inn[1], inn[0], out[0])
    go(inn[1])
    late_total = unpacked(late.finish())
    whole = jnp.concatenate([late_total, early_total], axis=0)
    rows = whole.shape[0]
    grads.sums[...] = whole + jnp.where(iota((rows, 128), 0) == rows - 8 + 2, penalty, 0.0)

    def write(group, layer, first):
        ref = group[layer].out
        grads.found[layer, :, first : first + ref.shape[1]] = ref[...]

    write(mid, 1, 0)
    write(out, 0, hid)
    write(out, 1, hid)
    write(inn, 1, hid + 128)
    go(mid[0], inn[0])
    write(mid, 0, 0)
    write(inn, 0, hid + 128)


def adamw(weight, grad, first, second, fixes):
    first_new = beta_one * first + (1.0 - beta_one) * grad
    second_new = beta_two * second + (1.0 - beta_two) * grad * grad
    update = first_new * fixes[0] / (jnp.sqrt(second_new * fixes[1]) + epsilon) + decay_rate * weight
    return (weight - learn_rate * update, first_new, second_new)


def update_kernel(total, images, step_ref, grad_ref, sums_ref, *refs):
    weights, firsts, seconds, loss_ref, outs = refs[0:6], refs[6:12], refs[12:18], refs[18], refs[19:]
    layers, share, _ = grad_ref.shape
    hid = weights[1].shape[2]
    coeff = -1.0 / (total * 12 * math.log(2.0))
    power = iota((8, 128), 1)
    used = power < jnp.broadcast_to(step_ref[0], (8, 128))
    fixes = tuple(
        1.0
        / (
            (1.0 - beta)
            * jnp.sum(
                jnp.where(used, jnp.exp(power.astype(f32) * math.log(beta)), 0.0), axis=1, keepdims=True
            )[0:1]
        )
        for beta in (beta_one, beta_two)
    )

    def write(which, at, grad):
        new = adamw(weights[which][at], grad, firsts[which][at], seconds[which][at], fixes)
        for k in range(3):
            outs[3 * which + k][at] = new[k]

    def column(layer):
        return (slice(None), layer, slice(None))

    place = spread(164, SMALL)
    to_slots = spread_rows(16, 12)
    reverse = jnp.where(slot(11 - iota((16, 12), 1)) == iota((16, 12), 0), 1.0, 0.0)
    row, col = iota((12, 12), 0), iota((12, 12), 1)
    eye = row == col
    logdet = jnp.zeros((1, 1), f32)
    for layer in range(layers):
        write(1, layer, grad_ref[layer, :, 0:hid])
        part = grad_ref[layer, :, hid : hid + SMALL]
        write(0, column(layer), dot_nt(place[108:162], part, highest))
        write(2, layer, dot_nt(part, place[0:108], highest))
        write(3, layer, dot_nt(place[162:164], part, highest))
        small = weights[4][column(layer)]
        lu = small[:, 0:12]
        lower, upper = mixing_parts(lu)
        scale = jnp.exp(small[:, 13:14])
        scale_row = as_row(scale)
        sums = sums_ref[16 * layer : 16 * layer + 16]
        turned = dot_tn(reverse, sums, highest)
        moment = dot(turned[:, 0:16], to_slots, highest)
        ones = turned[:, 16:17]
        g_mix = (moment + ones * as_row(small[:, 12:13])) * scale_row
        mix = dot(lower, upper, highest)
        g_bias = scale * dot_tn(mix, ones, highest)
        g_scale = as_column(jnp.sum(mix * g_mix, axis=0, keepdims=True)) + coeff * total
        g_lower = dot_nt(g_mix, upper, highest)
        g_upper = dot_tn(lower, g_mix, highest)
        g_lu = jnp.where(row > col, g_lower, jnp.where(eye, g_upper * jnp.exp(lu) + coeff * total, g_upper))
        g_cb = dot_tn(to_slots, sums, highest)[:, 17:18]
        wide15 = iota((12, 15), 1)
        grad = dot(g_lu, jnp.where(iota((12, 15), 0) == wide15, 1.0, 0.0), highest)
        grad = jnp.where(wide15 == 12, g_bias, grad)
        grad = jnp.where(wide15 == 13, g_scale, grad)
        grad = jnp.where(wide15 == 14, g_cb, grad)
        write(4, column(layer), grad)
        diag = jnp.sum(jnp.where(eye, lu, 0.0), axis=0, keepdims=True) + as_row(small[:, 13:14])
        logdet = logdet + jnp.sum(diag, axis=1, keepdims=True)
    sums = sums_ref[16 * layers : 16 * layers + 16]
    grad = coeff * dot_nt(
        dot_tn(to_slots, sums, highest), spread(55, 128), highest
    )
    write(5, Ellipsis, grad)
    tail = sums_ref[16 * layers + 16 :]
    likely = jnp.sum(tail[0:1], axis=1, keepdims=True)
    likely = likely - total * 6.0 * math.log(2.0 * math.pi) + total * logdet
    loss_ref[...] = coeff * likely + tail[1:2, 0:1] / images + tail[2:3, 0:1]


def turn(arrays, back=False):
    orders = ((1, 2, 0) if back else (2, 0, 1), None, (0, 2, 1), None, (1, 0, 2), None)
    return tuple(a if o is None else jnp.transpose(a, o) for a, o in zip(arrays, orders))


def shards(*args, wide, narrow):
    pixels, noise, depth, step_count = args[0:4]
    params, firsts, seconds = turn(args[4:10]), turn(args[10:16]), turn(args[16:22])
    layers, share, hid = params[1].shape
    count = pixels.shape[1]
    chips = max(wide // 2, 1)
    vmem = pltpu.VMEM

    def sems(*shape):
        return [pltpu.SemaphoreType.DMA(shape) for _ in range(2)]

    def group(across, scatter=True):
        piece = share // narrow if scatter and share % (8 * narrow) == 0 else share
        return [
            vmem((chips, hid // share // chips, share, across), f32),
            vmem((chips, share, across), f32),
            vmem((chips, share, across), f32),
            vmem((narrow, piece, across), f32),
            vmem((share, across), f32),
            [sems(1) for _ in range(4)],
        ]

    def both(height, dtype, times=layers):
        return [vmem((height, count), dtype) for _ in range(times)]

    first, middle, outer, bias, small, prior = params
    inputs = dict(
        mid=middle, first=first, out=outer, bias=bias, small=small, depth=depth, pixels=pixels, noise=noise, prior=prior
    )
    given = {
        name: pltpu.SMEM(a.shape, a.dtype) if a is depth else vmem(a.shape, a.dtype) for name, a in inputs.items()
    }
    early = 16 * layers + 8
    scratch = dict(
        given=given,
        load=pltpu.SemaphoreType.DMA((len(inputs),)),
        wmid=vmem((layers, hid, hid), bf16),
        wsmall=vmem((layers, hid, SMALL), bf16),
        wmt=vmem((layers, hid, hid), bf16),
        wst=vmem((layers, SMALL, hid), bf16),
        win=vmem((layers, hid, 128), bf16),
        bone=vmem((layers, hid, 128), f32),
        mixes=vmem((layers, 14, 16, 128), f32),
        mixes_back=vmem((layers, 12, 16, 128), f32),
        prior_fwd=vmem((32, 256), bf16),
        prior_back=vmem((144, 32), bf16),
        masks=vmem((4, 8, TILE), f32),
        gz=vmem((16, count), f32),
        gy=vmem((16, count), f32),
        d3=vmem((OUT, count), bf16),
        tbuf=vmem((OUT, TILE), f32),
        stat_acc=vmem((2, 16, 128), f32),
        like_acc=vmem((8, 128), f32),
        prior_acc=vmem((32, 256), f32),
        small_acc=vmem((layers, 32, 128), f32),
        sum_acc=vmem((layers, 2, 16, 128), f32),
        acc_in=vmem((hid, 128), f32),
        bone_acc=[vmem((hid, 128), f32) for _ in range(layers)],
        acc_rest=[vmem((hid, 128), f32) for _ in range(layers)],
        x=both(16, f32, layers + 1),
        keep=both(16, f32),
        taps=both(80, bf16),
        one=both(hid, bf16),
        two=both(hid, bf16),
        stat=[vmem((wide * narrow, 1, 128), f32), sems(1)],
        late=[vmem((wide * narrow, 2, 128), f32), sems(1)],
        early=[
            [vmem((size, early, 128), f32) for size in (wide, narrow)],
            [sems(1) for _ in range(2)],
        ],
        mid=[group(hid) for _ in range(layers)],
        out=[group(128) for _ in range(layers)],
        inn=[group(128, layer > 0) for layer in range(layers)],
        spread=[sems(2 * chips) for _ in range(2)],
        later=[[sems(1) for _ in range(layers)] for _ in range(2)],
    )
    like = jax.ShapeDtypeStruct
    grads = dict(
        found=like((layers, share, hid + SMALL), f32),
        sums=like((early + 16, 128), f32),
    )
    order = jax.tree.structure((inputs, grads, scratch))
    remote = dict(collective_id=0, has_side_effects=True) if wide > 1 else {}
    given_leaves, grad_leaves = jax.tree.leaves(inputs), jax.tree.leaves(grads)
    found = pl.pallas_call(
        functools.partial(flow_kernel, wide, narrow, order),
        out_shape=tuple(grad_leaves),
        in_specs=[HBM] * len(given_leaves),
        out_specs=(VMEM,) * len(grad_leaves),
        scratch_shapes=jax.tree.leaves(scratch),
        compiler_params=pltpu.CompilerParams(vmem_limit_bytes=FLOW_VMEM, **remote),
        name="flow",
    )(*given_leaves)
    found = SimpleNamespace(**jax.tree.unflatten(jax.tree.structure(grads), found))
    total = count * wide * narrow
    shapes = [like((1, 1), f32)] + [like(p.shape, f32) for p in params for _ in range(3)]
    results = pl.pallas_call(
        functools.partial(update_kernel, total, total // 256),
        out_shape=tuple(shapes),
        in_specs=[SMEM] + [VMEM] * 20,
        out_specs=(VMEM,) * 19,
        compiler_params=pltpu.CompilerParams(vmem_limit_bytes=UPDATE_VMEM),
        name="update",
    )(step_count.reshape(1), found.found, found.sums, *params, *firsts, *seconds)
    updated = [turn(results[1 + k :: 3], True) for k in range(3)]
    return (results[0].reshape(()),) + tuple(updated[k][p] for p in range(6) for k in range(3))


def solution(mesh):
    pixels = P(None, (NARROW, WIDE))
    rows, columns = P(None, WIDE, None), P(None, None, WIDE)
    weights = (rows, rows, columns, columns, P(), P())
    return jax.shard_map(
        functools.partial(shards, wide=mesh.shape[WIDE], narrow=mesh.shape[NARROW]),
        mesh=mesh,
        in_specs=(pixels, pixels, P((NARROW, WIDE)), P()) + weights * 3,
        out_specs=(P(),) + tuple(w for w in weights for _ in range(3)),
        check_vma=False,
    )
```

```python
import functools
import math
from types import SimpleNamespace

import jax
import jax.numpy as jnp
from jax import lax
from jax.experimental import pallas as pl
from jax.experimental.pallas import tpu as pltpu
from jax.sharding import PartitionSpec as P

f32 = jnp.float32
bf16 = jnp.bfloat16
highest = lax.Precision.HIGHEST
MESH = pl.DeviceIdType.MESH
learn_rate = 0.02
beta_one = 0.9
beta_two = 0.999
epsilon = 1e-08
decay_rate = 0.01
penalty_weight = 0.5
tap_offsets = [(r, c) for r in (-1, 0, 1) for c in (-1, 0, 1)]
TILE = 2048
FLOW_VMEM = 62 * 1024 * 1024
UPDATE_VMEM = 60 * 1024 * 1024
OUT = 144
SMALL = 256
VMEM = pl.BlockSpec(memory_space=pltpu.VMEM)
SMEM = pl.BlockSpec(memory_space=pltpu.SMEM)
HBM = pl.BlockSpec(memory_space=pl.ANY)
WIDE, NARROW = "wide", "narrow"


def dot(a, b, precision=None):
    return lax.dot_general(
        a, b, (((1,), (0,)), ((), ())), preferred_element_type=f32, precision=precision
    )


def dot_nt(a, b, precision=None):
    return lax.dot_general(
        a, b, (((1,), (1,)), ((), ())), preferred_element_type=f32, precision=precision
    )


def dot_tn(a, b, precision=None):
    return lax.dot_general(
        a, b, (((0,), (0,)), ((), ())), preferred_element_type=f32, precision=precision
    )


def iota(shape, axis):
    return lax.broadcasted_iota(jnp.int32, shape, axis)


def slot(s):
    return s + 2 * ((s * 10923) >> 16)


def spread(count, width, first=0):
    return jnp.where(slot(iota((count, width), 0) + first) == iota((count, width), 1), 1.0, 0.0)


def spread_rows(height, count):
    return jnp.where(slot(iota((height, count), 1)) == iota((height, count), 0), 1.0, 0.0)


def split_two(v):
    high = v.astype(bf16).astype(f32)
    return high, v - high


def as_row(column):
    n = column.shape[0]
    eye = iota((n, n), 0) == iota((n, n), 1)
    return jnp.sum(jnp.where(eye, column, 0.0), axis=0, keepdims=True)


def as_column(row):
    n = row.shape[1]
    eye = iota((n, n), 0) == iota((n, n), 1)
    return jnp.sum(jnp.where(eye, row, 0.0), axis=1, keepdims=True)


def mixing_parts(lu):
    n = lu.shape[0]
    row, col = iota((n, n), 0), iota((n, n), 1)
    lower = jnp.where(row > col, lu, 0.0) + jnp.where(row == col, 1.0, 0.0)
    upper = jnp.where(row < col, lu, 0.0) + jnp.where(row == col, jnp.exp(lu), 0.0)
    return lower, upper


def wide_rows(v, lanes):
    return jnp.concatenate([v] * (lanes // 128), axis=1)


class Shifts:
    def __init__(self, mask_ref, lanes):
        self.lanes = lanes
        self.masks = mask_ref

    def mask(self, which, rows):
        m = self.masks[which, :, 0 : self.lanes]
        return jnp.concatenate([m] * (rows // 8), axis=0) if rows > 8 else m

    def col(self, v, c):
        if c == 0:
            return v
        moved = pltpu.roll(v, (-c) % self.lanes, 1)
        return moved * self.mask(0 if c > 0 else 1, v.shape[0])

    def row(self, v, r):
        if r == 0:
            return v
        moved = pltpu.roll(v, (-16 * r) % self.lanes, 1)
        return moved * self.mask(2 if r > 0 else 3, v.shape[0])

    def taps(self, v, sign=1):
        by_col = {c: self.col(v, c) for c in (-1, 0, 1)}
        return [self.row(by_col[sign * c], sign * r) for r, c in tap_offsets]

    def fold(self, pieces, sign=1):
        total = None
        for c in (-1, 0, 1):
            part = None
            for r in (-1, 0, 1):
                piece = self.row(pieces[3 * (r + 1) + (c + 1)], sign * r)
                part = piece if part is None else part + piece
            part = self.col(part, sign * c)
            total = part if total is None else total + part
        return total


def fill_masks(mask_ref):
    lanes = mask_ref.shape[2]
    pos = iota((8, lanes), 1)
    row, col = (pos >> 4) & 15, pos & 15
    for which, keep in enumerate((col < 15, col > 0, row < 15, row > 0)):
        mask_ref[which] = jnp.where(keep, 1.0, 0.0)


def flow_kernel(wide, narrow, tree, *refs):
    hbm, grads, at = (SimpleNamespace(**part) for part in jax.tree.unflatten(tree, refs))
    wmid, wsmall, wmt, wst, win = at.wmid, at.wsmall, at.wmt, at.wst, at.win
    bone, mixes, mixes_back = at.bone, at.mixes, at.mixes_back
    gz, gy_ref, d3, tbuf = at.gz, at.gy, at.d3, at.tbuf
    given = SimpleNamespace(**at.given)
    layers, share, hid = given.mid.shape
    count = given.pixels.shape[1]
    total = count * wide * narrow
    coeff = -1.0 / (total * 12 * math.log(2.0))
    chips = max(wide // 2, 1)
    me_w = lax.axis_index(WIDE) if wide > 1 else 0
    me_n = lax.axis_index(NARROW) if narrow > 1 else 0
    chip, core = (me_w // 2, lax.rem(me_w, 2)) if wide > 1 else (0, 0)
    shifts = Shifts(at.masks, TILE)

    def block(index):
        return pl.ds(pl.multiple_of(index * share, share), share)

    def tile_at(t):
        return pl.ds(pl.multiple_of(t * TILE, TILE), TILE)

    def ahead(size, me, d):
        return lax.rem(me + d, size)

    def behind(size, me, d):
        return lax.rem(me + size - d, size)

    def each(first, size, fn):
        if wide > 1 and size > first:
            lax.fori_loop(first, size, lambda d, c: (fn(d), c)[1], 0)

    def remote(src, dst, sems, index, device):
        return pltpu.make_async_remote_copy(
            src_ref=src,
            dst_ref=dst,
            send_sem=sems[0].at[index],
            recv_sem=sems[1].at[index],
            device_id=device,
            device_id_type=MESH,
        )

    def drain(ref, sem):
        if wide > 1:
            pltpu.make_async_copy(ref, ref, sem.at[0]).wait()

    class Exchange:
        def __init__(self, bufs, sems):
            self.bufs, self.sems = bufs, sems

        def copy(self, phase, d):
            axis, size, me = ((WIDE, wide, me_w), (NARROW, narrow, me_n))[phase]
            row = self.bufs[phase].at[me]
            return remote(row, row, self.sems[phase], 0, {axis: ahead(size, me, d)})

        def start(self, phase, value):
            me, size = ((me_w, wide), (me_n, narrow))[phase]
            self.bufs[phase][me] = value
            each(1, size, lambda d: self.copy(phase, d).start())

        def finish(self, phase):
            size = (wide, narrow)[phase]
            if size > 1:
                for sem in self.sems[phase]:
                    drain(self.bufs[phase].at[1:size], sem)
            value = self.bufs[phase][0]
            for k in range(1, size):
                value = value + self.bufs[phase][k]
            return value

        def hop(self):
            self.start(1, self.finish(0))

    class OneShot:
        def __init__(self, rows, sems):
            self.rows, self.sems = rows, sems

        def copy(self, d):
            by_n, by_w = d // wide, lax.rem(d, wide)
            row = self.rows.at[me_n * wide + me_w]
            device = {NARROW: ahead(narrow, me_n, by_n), WIDE: ahead(wide, me_w, by_w)}
            return remote(row, row, self.sems, 0, device)

        def start(self, value):
            self.rows[me_n * wide + me_w] = value
            each(1, wide * narrow, lambda d: self.copy(d).start())

        def finish(self):
            if wide > 1:
                for sem in self.sems:
                    drain(self.rows.at[1 : wide * narrow], sem)
            return lax.fori_loop(
                0, wide * narrow, lambda k, c: c + self.rows[k], jnp.zeros(self.rows.shape[1:], f32)
            )

    stat, late = OneShot(*at.stat), OneShot(*at.late)
    early = Exchange(*at.early)

    class Group:
        def __init__(self, refs):
            self.full, self.pair, self.chip, self.part, self.out = refs[0:5]
            self.sems = refs[5]
            self.piece = self.part.shape[1]
            self.scatter = self.piece < share
            self.stage = 0
            self.last = 3 if self.scatter else 2

        def mine(self, index):
            return pl.ds(pl.multiple_of(index * self.piece, 8), self.piece)

        def start(self):
            sems = self.sems[self.stage]
            if self.stage == 0:
                if wide > 1:
                    theirs = self.full.at[:, 1 - core]
                    remote(theirs, self.pair, sems, 0, {WIDE: me_w + 1 - 2 * core}).start()
                return

            def go(d):
                if self.stage == 1:
                    to = ahead(chips, chip, d)
                    remote(self.full.at[to, core], self.chip.at[d - 1], sems, 0, {WIDE: 2 * to + core}).start()
                    return
                to = ahead(narrow, me_n, d)
                if self.stage == 2 and self.scatter:
                    rows = self.full.at[chip, core, self.mine(to)]
                    remote(rows, self.part.at[d - 1], sems, 0, {NARROW: to}).start()
                    return
                ref = self.part.at[me_n] if self.stage == 2 else self.out.at[self.mine(me_n)]
                remote(ref, ref, sems, 0, {NARROW: to}).start()

            each(1, chips if self.stage == 1 else narrow, go)

        def finish(self):
            if self.stage == 0:
                come = self.pair
            elif self.stage == 1:
                come = self.chip.at[0 : chips - 1] if chips > 1 else None
            elif self.stage == 2:
                come = self.part.at[0 : narrow - 1] if narrow > 1 else None
            else:
                come = self.out.at[0 : (narrow - 1) * self.piece] if narrow > 1 else None
            if come is not None:
                for sem in self.sems[self.stage]:
                    drain(come, sem)
            own = (chip, core)
            if self.stage == 0:

                def add(d):
                    self.full[d, core] += self.pair[d]

                each(0, chips, add)
            if self.stage == 1:
                value = self.full[own]
                for d in range(chips - 1):
                    value = value + self.chip[d]
                if self.scatter:
                    self.full[own] = value
                else:
                    self.part[me_n] = value
            if self.stage == 2:
                value = self.full[chip, core, self.mine(me_n)] if self.scatter else self.part[0]
                for d in range(0 if self.scatter else 1, narrow - 1 if self.scatter else narrow):
                    value = value + self.part[d]
                self.out[self.mine(me_n) if self.scatter else slice(None)] = value
            self.stage += 1

        def put(self, value):
            self.full[...] = value.reshape(self.full.shape)

        def add(self, value):
            self.full[...] += value.reshape(self.full.shape)

        def advance(self):
            self.finish()
            if self.stage <= self.last:
                self.start()

    mid, out, inn = ([Group(refs) for refs in kind] for kind in (at.mid, at.out, at.inn))

    if wide > 1:
        barrier = pltpu.get_barrier_semaphore()
        each(
            1,
            wide * narrow,
            lambda d: pl.semaphore_signal(
                barrier,
                inc=1,
                device_id={
                    NARROW: ahead(narrow, me_n, d // wide),
                    WIDE: ahead(wide, me_w, lax.rem(d, wide)),
                },
                device_id_type=MESH,
            ),
        )
    loads = {
        name: pltpu.make_async_copy(source_ref, at.given[name], at.load.at[k])
        for k, (name, source_ref) in enumerate(vars(hbm).items())
    }
    for copy in loads.values():
        copy.start()
    loads = SimpleNamespace(**loads)

    place = spread(164, SMALL).astype(bf16)
    for copy in (loads.mid, loads.first, loads.out, loads.bias):
        copy.wait()
    for layer in range(layers):
        small_part = (
            dot(given.out[layer].astype(bf16), place[0:108])
            + dot_tn(given.first[:, layer, :].astype(bf16), place[108:162])
            + dot_tn(given.bias[layer].astype(bf16), place[162:164])
        )
        wmid[layer, block(me_w)] = given.mid[layer].astype(bf16)
        wsmall[layer, block(me_w)] = small_part.astype(bf16)

    class Spread:
        def __init__(self, weights, sems):
            self.weights, self.sems = weights, sems

        def to_chip(self, d, coming=False):
            index = 2 * (behind(chips, chip, d) if coming else chip) + core
            rows = self.weights.at[0, block(index)]
            return remote(rows, rows, self.sems, d, {WIDE: 2 * ahead(chips, chip, d) + core})

        def to_core(self, d, coming=False):
            index = 2 * behind(chips, chip, d) + (1 - core if coming else core)
            rows = self.weights.at[0, block(index)]
            return remote(rows, rows, self.sems, chips + d, {WIDE: me_w + 1 - 2 * core})

        def start(self):
            each(1, chips, lambda d: self.to_chip(d).start())
            each(0, 1, lambda d: self.to_core(d).start())

        def pass_on(self):
            def one(d):
                self.to_chip(d).wait_send()
                self.to_chip(d, True).wait_recv()
                self.to_core(d).start()

            each(1, chips, one)

        def finish(self):
            def one(d):
                self.to_core(d).wait_send()
                self.to_core(d, True).wait_recv()

            each(0, chips, one)

    spread_small, spread_mid = Spread(wsmall, at.spread[0]), Spread(wmid, at.spread[1])

    def to_all(weights, sems, layer, d):
        rows = weights.at[layer, block(me_w)]
        return remote(rows, rows, sems[layer], 0, {WIDE: ahead(wide, me_w, d)})

    later = ((wsmall, at.later[0]), (wmid, at.later[1]))

    if wide > 1:
        pl.semaphore_wait(barrier, wide * narrow - 1)
        spread_small.start()
        spread_mid.start()

    fill_masks(at.masks)
    loads.small.wait()
    to_slots = spread_rows(16, 12)
    reverse = jnp.where(slot(11 - iota((16, 12), 1)) == iota((16, 12), 0), 1.0, 0.0)
    for layer in range(layers):
        small = given.small[:, layer, :]
        lower, upper = mixing_parts(small[:, 0:12])
        scale = jnp.exp(small[:, 13:14])
        mixed = dot(reverse, dot(lower, upper, highest), highest) * as_row(scale)
        const = jnp.sum(mixed * as_row(small[:, 12:13]), axis=1, keepdims=True)
        cb = jnp.sum(to_slots * as_row(small[:, 14:15]), axis=1, keepdims=True)
        for c in range(12):
            mixes[layer, c] = jnp.broadcast_to(mixed[:, c : c + 1], (16, 128))
        mixes[layer, 12] = jnp.broadcast_to(const, (16, 128))
        mixes[layer, 13] = jnp.broadcast_to(cb, (16, 128))
        if layer:
            back = dot_nt(to_slots, mixed, highest)
            for c in range(12):
                s = c + 2 * (c // 6)
                mixes_back[layer, c] = jnp.broadcast_to(back[:, s : s + 1], (16, 128))

    def by_lanes(v):
        parts = [v[:, 128 * k : 128 * k + 128] for k in range(v.shape[1] // 128)]
        while len(parts) > 1:
            parts = [a + b for a, b in zip(parts[0::2], parts[1::2])]
        return parts[0]

    real = jnp.where(iota((8, 128), 0) < 6, 1.0, 0.0)
    first_row = jnp.where(iota((8, TILE), 0) == 0, 1.0, 0.0)

    def enter(layer, here, x):
        at.x[layer][:, here] = x
        y = wide_rows(mixes[layer, 12], TILE)
        for c in range(12):
            s = c + 2 * (c // 6)
            y = y + wide_rows(mixes[layer, c], TILE) * x[s : s + 1, :]
        taps = jnp.concatenate(shifts.taps(y[0:8]) + [first_row], axis=0)
        at.taps[layer][:, here] = taps.astype(bf16)
        at.x[layer + 1][0:8, here] = y[0:8]
        at.keep[layer][0:8, here] = y[8:16]

    def pixels_in(t, carry):
        images = TILE // 256
        blank = jnp.zeros((2, 256), f32)
        chunks = []
        for k in range(images):
            coarse = given.depth[t * images + k] == 5
            by = jnp.where(coarse, 3, 0)
            level = jnp.where(coarse, 1.0 / 32.0, 1.0 / 256.0).astype(f32)
            at_image = pl.ds(pl.multiple_of(t * TILE + k * 256, 256), 256)
            quant = lax.shift_right_logical(given.pixels[:, at_image], jnp.broadcast_to(by, (12, 256)))
            x = (quant.astype(f32) + given.noise[:, at_image]) * level - 0.5
            chunks.append(jnp.concatenate([x[0:6], blank, x[6:12], blank], axis=0))
        enter(0, tile_at(t), jnp.concatenate(chunks, axis=1))
        return carry

    tiles = count // TILE
    half = tiles // 2

    def run(first, end, body):
        lax.fori_loop(first, end, lambda t, c: (body(t), c)[1], 0)

    def piped(first, end, lead, follow):
        lead(first)

        def both(t):
            follow(t - 1)
            lead(t)

        run(first + 1, end, both)
        follow(end - 1)

    for copy in (loads.depth, loads.pixels, loads.noise, loads.prior):
        copy.wait()
    lax.fori_loop(0, tiles, pixels_in, 0)
    spread_small.pass_on()

    prior = given.prior[...]
    s = iota((55, 256), 0)
    lane = iota((55, 256), 1)
    hit = (slot(s) == lane) | (slot(s) + 72 == lane)
    to_taps = jnp.where(((s < 54) & hit) | ((s == 54) & (lane == 144)), 1.0, 0.0)
    prior_slots = dot(to_slots, prior, highest)
    parts = split_two(dot(prior_slots, to_taps, highest))
    at.prior_fwd[...] = jnp.concatenate(parts, axis=0).astype(bf16)
    turned = dot_nt(spread_rows(72, 55), prior_slots, highest)
    stacked = jnp.concatenate(split_two(turned), axis=0)
    again = jnp.where((iota((16, 32), 1) & 15) == iota((16, 32), 0), 1.0, 0.0)
    at.prior_back[...] = dot(stacked.astype(bf16), again.astype(bf16)).astype(bf16)

    whole = [group.full for group in mid + out]
    sums = [at.stat_acc, at.like_acc, at.prior_acc, at.small_acc, at.sum_acc, at.acc_in]
    for ref in whole + sums + at.bone_acc + at.acc_rest:
        ref[...] = jnp.zeros_like(ref)

    pick = jnp.where(iota((SMALL, 128), 0) == iota((SMALL, 128), 1) + OUT, 1.0, 0.0).astype(bf16)

    def derive(layer):
        w = wsmall[layer]
        win[layer] = dot(w, pick).astype(bf16)
        wst[layer] = w.T
        bone[layer] = jnp.broadcast_to(w[:, 217:218].astype(f32), (hid, 128))

    def hidden_first(layer, t):
        here = tile_at(t)
        first = dot(win[layer, :, 0:80], at.taps[layer][:, here]).astype(bf16)
        h1 = jnp.maximum(first, jnp.zeros_like(first))
        at.one[layer][:, here] = h1
        return h1

    def forward_products(layer, t):
        here = tile_at(t)
        h1 = hidden_first(layer, t) if layer else at.one[0][:, here]
        second = dot(wmid[layer], h1) + wide_rows(bone[layer], TILE)
        h2 = jnp.maximum(second, 0.0).astype(bf16)
        at.two[layer][:, here] = h2
        tbuf[...] = dot(wst[layer, 0:OUT, :], h2)

    def forward_rest(layer, t):
        here = tile_at(t)
        o = shifts.fold([tbuf[16 * k : 16 * k + 16] for k in range(9)])
        o = o + wide_rows(mixes[layer, 13], TILE)
        v = at.keep[layer][0:8, here] + o[0:8]
        decay = 1.0 + jnp.exp(-(o[8:16] + 2.0))
        q = 1.0 / decay
        at.like_acc[...] -= by_lanes(jnp.log(decay)) * real
        at.keep[layer][0:8, here] = v
        at.keep[layer][8:16, here] = q
        x = jnp.concatenate([at.x[layer + 1][0:8, here], v * q], axis=0)
        if layer < layers - 1:
            enter(layer + 1, here, x)
        else:
            at.x[layer + 1][8:16, here] = x[8:16]
            at.stat_acc[0] += by_lanes(x)
            at.stat_acc[1] += by_lanes(x * x)

    spread_small.finish()
    for layer in range(1, layers):
        for weights, sems in later:
            each(1, wide, lambda d: to_all(weights, sems, layer, d).start())
    derive(0)
    run(0, half, functools.partial(hidden_first, 0))
    spread_mid.pass_on()
    run(half, tiles, functools.partial(hidden_first, 0))
    spread_mid.finish()
    for layer in range(layers):
        if layer:
            for weights, sems in later:

                if wide > 1:
                    for sem in sems[layer]:
                        drain(weights.at[layer, 0 : (wide - 1) * share], sem)
            derive(layer)
        piped(0, tiles, functools.partial(forward_products, layer), functools.partial(forward_rest, layer))

    lane = iota((16, 128), 1)

    line = iota((16, 128), 0)
    row = jnp.where(lane == line, jnp.sum(at.stat_acc[0], axis=1, keepdims=True), 0.0)
    row = row + jnp.where(lane == line + 16, jnp.sum(at.stat_acc[1], axis=1, keepdims=True), 0.0)
    stat.start(jnp.sum(row, axis=0, keepdims=True))

    def prior_tile(t):
        here = tile_at(t)
        z1 = at.x[layers][0:8, here]
        z2 = at.x[layers][8:16, here]
        pieces = [split_two(v) for v in shifts.taps(z1)]
        tz = jnp.concatenate(
            [p[0] for p in pieces] + [p[1] for p in pieces] + [first_row, jnp.zeros_like(first_row)], axis=0
        ).astype(bf16)
        both = dot(at.prior_fwd[:, 0:160], tz)
        value = both[0:16] + both[16:32]
        centre, log_sd = value[0:8], value[8:16]
        inverse = jnp.exp(-log_sd)
        ratio = (z2 - centre) * inverse
        at.like_acc[...] += by_lanes(-0.5 * z1 * z1 - 0.5 * ratio * ratio - log_sd)
        d_centre = ratio * inverse
        d_stat = jnp.concatenate([d_centre, ratio * ratio - 1.0], axis=0)
        ds = jnp.concatenate(split_two(d_stat), axis=0).astype(bf16)
        at.prior_acc[:, 0:160] += dot_nt(ds, tz)
        dt = dot(at.prior_back[...], ds)
        dt = dt[0:72] + dt[72:144]
        folded = shifts.fold([dt[8 * k : 8 * k + 8] for k in range(9)], -1)
        gz[0:8, here] = coeff * (folded - z1)
        gz[8:16, here] = -coeff * d_centre

    run(0, tiles, prior_tile)
    for layer in range(layers):
        wmt[layer] = wmid[layer].T
    stats = stat.finish()
    mean = jnp.sum(jnp.where(lane == line, stats, 0.0), axis=1, keepdims=True) / total
    square = jnp.sum(jnp.where(lane == line + 16, stats, 0.0), axis=1, keepdims=True) / total
    var = square - mean * mean
    from_first = penalty_weight * (2.0 * mean - 4.0 * (var - 1.0) * mean) / total
    from_square = penalty_weight * 2.0 * (var - 1.0) / total
    ones_rows = jnp.where((iota((16, 1), 0) & 7) < 6, 1.0, 0.0)
    penalty = penalty_weight * jnp.sum(
        ones_rows * (mean * mean + (var - 1.0) * (var - 1.0)), axis=0, keepdims=True
    )

    def prepare_back(layer, here, g):
        v = at.keep[layer][0:8, here]
        q = at.keep[layer][8:16, here]
        gbq = g[8:16] * q
        gy_ref[0:8, here] = g[0:8]
        gy_ref[8:16, here] = gbq
        do = jnp.concatenate([gbq, (gbq * v + coeff) * (1.0 - q)], axis=0)
        at.sum_acc[layer, 1] += by_lanes(do)
        rounded = do.astype(bf16).astype(f32)
        d3[:, here] = jnp.concatenate(shifts.taps(rounded, -1), axis=0).astype(bf16)

    def last_gradient(t):
        here = tile_at(t)
        g = gz[:, here] + from_first + 2.0 * at.x[layers][:, here] * from_square
        prepare_back(layers - 1, here, g)

    def back_a(layer, t):
        here = tile_at(t)
        h2 = at.two[layer][:, here]
        taps = d3[:, here]
        grad = dot_nt(h2, taps)
        out[layer].add(grad[:, 0:128])
        at.acc_rest[layer][:, 0:16] += grad[:, 128:OUT]
        dd2 = dot(wsmall[layer, :, 0:OUT], taps).astype(bf16)
        at.two[layer][:, here] = jnp.where(h2 > 0, dd2, jnp.zeros_like(dd2))

    def back_b(layer, t):
        here = tile_at(t)
        d2 = at.two[layer][:, here]
        mid[layer].add(dot_nt(d2, at.one[layer][:, here]))
        at.bone_acc[layer][...] += by_lanes(d2.astype(f32))

    def back_c(layer, t):
        here = tile_at(t)
        dd1 = dot(wmt[layer], at.two[layer][:, here]).astype(bf16)
        h1 = at.one[layer][:, here]
        at.one[layer][:, here] = jnp.where(h1 > 0, dd1, jnp.zeros_like(dd1))

    def back_in(layer, t):
        here = tile_at(t)
        at.acc_in[:, 0:80] += dot_nt(at.one[layer][:, here], at.taps[layer][:, here])

    def back_taps(layer, t):
        tbuf[0:80] = dot(wst[layer, OUT : OUT + 80, :], at.one[layer][:, tile_at(t)])

    def back_rest(layer, t):
        here = tile_at(t)
        gya = gy_ref[0:8, here] + shifts.fold([tbuf[8 * k : 8 * k + 8] for k in range(9)], -1)
        gy = jnp.concatenate([gya, gy_ref[8:16, here]], axis=0)
        at.sum_acc[layer, 0] += by_lanes(gy)
        left = jnp.concatenate(split_two(gy), axis=0).astype(bf16)
        right = jnp.concatenate(split_two(at.x[layer][:, here]), axis=0).astype(bf16)
        at.small_acc[layer, :, 0:32] += dot_nt(left, right)
        if layer:
            gx = wide_rows(mixes_back[layer, 0], TILE) * gy[0:1, :]
            for c in range(1, 12):
                s = c + 2 * (c // 6)
                gx = gx + wide_rows(mixes_back[layer, c], TILE) * gy[s : s + 1, :]
            prepare_back(layer - 1, here, gx)

    def inner_gradient(layer):
        column = jnp.sum(at.bone_acc[layer][...], axis=1, keepdims=True)
        grad = at.acc_rest[layer][...] + pltpu.roll(at.acc_in[...], 16, 1)
        inn[layer].put(grad + jnp.where(iota((hid, 128), 1) == 217 - 128, column, 0.0))
        if layer:
            at.acc_in[...] = jnp.zeros_like(at.acc_in)

    def moments(layer):
        acc = at.small_acc[layer]
        part = acc[0:16] + acc[16:32]
        moment = jnp.where(lane < 16, part + pltpu.roll(part, 112, 1), 0.0)
        for k in range(2):
            line = jnp.sum(at.sum_acc[layer, k], axis=1, keepdims=True)
            moment = moment + jnp.where(lane == 16 + k, line, 0.0)
        return moment

    def early_sums():
        acc = at.prior_acc[0:16] + at.prior_acc[16:32]
        taps_part = (acc + pltpu.roll(acc, 256 - 72, 1))[:, 0:128]
        last = pltpu.roll(acc, 256 - 72, 1)[:, 0:128]
        pieces = [moments(layer) for layer in range(1, layers)]
        pieces.append(jnp.where(lane < 72, taps_part, 0.0) + jnp.where(lane == 72, last, 0.0))
        depths = lax.fori_loop(0, given.depth.shape[0], lambda k, c: c + given.depth[k], jnp.int32(0))
        depths = jnp.broadcast_to(depths, (8, 128)).astype(f32)
        row8 = iota((8, 128), 0)
        logs = jnp.sum(at.like_acc[...], axis=0, keepdims=True)
        pieces.append(jnp.where(row8 == 0, logs, 0.0) + jnp.where(row8 == 1, depths, 0.0))
        return jnp.concatenate(pieces, axis=0)

    def go(*which):
        for group in which:
            group.advance()

    def loop(body, layer, first=0, end=tiles):
        run(first, end, functools.partial(body, layer))

    def rest_loop(layer, first, end):
        piped(first, end, functools.partial(back_taps, layer), functools.partial(back_rest, layer))

    def inner(layer):
        inner_gradient(layer)
        inn[layer].start()

    def packed(moment):
        value = jnp.zeros((2, 128), f32)
        for k in range(6):
            pair = jnp.concatenate([moment[k : k + 1], moment[8 + k : 9 + k]], axis=0)
            value = value + (pltpu.roll(pair, 20 * k, 1) if k else pair)
        return value

    def unpacked(value):
        blank = jnp.zeros((2, 128), f32)
        turns = [pltpu.roll(value, 128 - 20 * k, 1) if k else value for k in range(6)]
        rows = [turn[0:1] for turn in turns] + [blank] + [turn[1:2] for turn in turns] + [blank]
        return jnp.where(lane < 18, jnp.concatenate(rows, axis=0), 0.0)

    piped(0, tiles, last_gradient, functools.partial(back_a, 1))
    out[1].start()
    def lead(t):
        back_b(1, t)
        back_c(1, t)

    def follow(t):
        back_taps(1, t)
        back_rest(1, t)

    piped(0, tiles, lead, follow)
    mid[1].start()
    go(out[1])
    early.start(0, early_sums())
    loop(back_a, 0, 0, half)
    go(mid[1])
    loop(back_a, 0, half, tiles)
    out[0].start()
    go(out[1])
    early.hop()
    loop(back_b, 0)
    mid[0].start()
    go(mid[1], out[0], out[1])
    loop(back_in, 1, 0, half)
    go(mid[0])
    loop(back_in, 1, half, tiles)
    inner(1)
    early_total = early.finish(1)
    loop(back_c, 0, 0, half)
    go(inn[1], out[0], out[1])
    loop(back_c, 0, half, tiles)
    go(mid[1])
    loop(back_in, 0, 0, half)
    go(mid[0], inn[1])
    loop(back_in, 0, half, tiles)
    inner(0)
    go(out[0])
    rest_loop(0, 0, half)
    go(inn[0], mid[1])
    rest_loop(0, half, tiles)
    late.start(packed(moments(0)))
    go(mid[0], inn[1], inn[0], out[0])
    go(inn[1])
    late_total = unpacked(late.finish())
    whole = jnp.concatenate([late_total, early_total], axis=0)
    rows = whole.shape[0]
    grads.sums[...] = whole + jnp.where(iota((rows, 128), 0) == rows - 8 + 2, penalty, 0.0)

    def write(group, layer, first):
        ref = group[layer].out
        grads.found[layer, :, first : first + ref.shape[1]] = ref[...]

    write(mid, 1, 0)
    write(out, 0, hid)
    write(out, 1, hid)
    write(inn, 1, hid + 128)
    go(mid[0], inn[0])
    write(mid, 0, 0)
    write(inn, 0, hid + 128)


def adamw(weight, grad, first, second, fixes):
    first_new = beta_one * first + (1.0 - beta_one) * grad
    second_new = beta_two * second + (1.0 - beta_two) * grad * grad
    update = first_new * fixes[0] / (jnp.sqrt(second_new * fixes[1]) + epsilon) + decay_rate * weight
    return (weight - learn_rate * update, first_new, second_new)


def update_kernel(total, images, step_ref, grad_ref, sums_ref, *refs):
    weights, firsts, seconds, loss_ref, outs = refs[0:6], refs[6:12], refs[12:18], refs[18], refs[19:]
    layers, share, _ = grad_ref.shape
    hid = weights[1].shape[2]
    coeff = -1.0 / (total * 12 * math.log(2.0))
    power = iota((8, 128), 1)
    used = power < jnp.broadcast_to(step_ref[0], (8, 128))
    fixes = tuple(
        1.0
        / (
            (1.0 - beta)
            * jnp.sum(
                jnp.where(used, jnp.exp(power.astype(f32) * math.log(beta)), 0.0), axis=1, keepdims=True
            )[0:1]
        )
        for beta in (beta_one, beta_two)
    )

    def write(which, at, grad):
        new = adamw(weights[which][at], grad, firsts[which][at], seconds[which][at], fixes)
        for k in range(3):
            outs[3 * which + k][at] = new[k]

    def column(layer):
        return (slice(None), layer, slice(None))

    place = spread(164, SMALL)
    to_slots = spread_rows(16, 12)
    reverse = jnp.where(slot(11 - iota((16, 12), 1)) == iota((16, 12), 0), 1.0, 0.0)
    row, col = iota((12, 12), 0), iota((12, 12), 1)
    eye = row == col
    logdet = jnp.zeros((1, 1), f32)
    for layer in range(layers):
        write(1, layer, grad_ref[layer, :, 0:hid])
        part = grad_ref[layer, :, hid : hid + SMALL]
        write(0, column(layer), dot_nt(place[108:162], part, highest))
        write(2, layer, dot_nt(part, place[0:108], highest))
        write(3, layer, dot_nt(place[162:164], part, highest))
        small = weights[4][column(layer)]
        lu = small[:, 0:12]
        lower, upper = mixing_parts(lu)
        scale = jnp.exp(small[:, 13:14])
        scale_row = as_row(scale)
        sums = sums_ref[16 * layer : 16 * layer + 16]
        turned = dot_tn(reverse, sums, highest)
        moment = dot(turned[:, 0:16], to_slots, highest)
        ones = turned[:, 16:17]
        g_mix = (moment + ones * as_row(small[:, 12:13])) * scale_row
        mix = dot(lower, upper, highest)
        g_bias = scale * dot_tn(mix, ones, highest)
        g_scale = as_column(jnp.sum(mix * g_mix, axis=0, keepdims=True)) + coeff * total
        g_lower = dot_nt(g_mix, upper, highest)
        g_upper = dot_tn(lower, g_mix, highest)
        g_lu = jnp.where(row > col, g_lower, jnp.where(eye, g_upper * jnp.exp(lu) + coeff * total, g_upper))
        g_cb = dot_tn(to_slots, sums, highest)[:, 17:18]
        wide15 = iota((12, 15), 1)
        grad = dot(g_lu, jnp.where(iota((12, 15), 0) == wide15, 1.0, 0.0), highest)
        grad = jnp.where(wide15 == 12, g_bias, grad)
        grad = jnp.where(wide15 == 13, g_scale, grad)
        grad = jnp.where(wide15 == 14, g_cb, grad)
        write(4, column(layer), grad)
        diag = jnp.sum(jnp.where(eye, lu, 0.0), axis=0, keepdims=True) + as_row(small[:, 13:14])
        logdet = logdet + jnp.sum(diag, axis=1, keepdims=True)
    sums = sums_ref[16 * layers : 16 * layers + 16]
    grad = coeff * dot_nt(
        dot_tn(to_slots, sums, highest), spread(55, 128), highest
    )
    write(5, Ellipsis, grad)
    tail = sums_ref[16 * layers + 16 :]
    likely = jnp.sum(tail[0:1], axis=1, keepdims=True)
    likely = likely - total * 6.0 * math.log(2.0 * math.pi) + total * logdet
    loss_ref[...] = coeff * likely + tail[1:2, 0:1] / images + tail[2:3, 0:1]


def turn(arrays, back=False):
    orders = ((1, 2, 0) if back else (2, 0, 1), None, (0, 2, 1), None, (1, 0, 2), None)
    return tuple(a if o is None else jnp.transpose(a, o) for a, o in zip(arrays, orders))


def shards(*args, wide, narrow):
    pixels, noise, depth, step_count = args[0:4]
    params, firsts, seconds = turn(args[4:10]), turn(args[10:16]), turn(args[16:22])
    layers, share, hid = params[1].shape
    count = pixels.shape[1]
    chips = max(wide // 2, 1)
    vmem = pltpu.VMEM

    def sems(*shape):
        return [pltpu.SemaphoreType.DMA(shape) for _ in range(2)]

    def group(across, scatter=True):
        piece = share // narrow if scatter and share % (8 * narrow) == 0 else share
        return [
            vmem((chips, hid // share // chips, share, across), f32),
            vmem((chips, share, across), f32),
            vmem((chips, share, across), f32),
            vmem((narrow, piece, across), f32),
            vmem((share, across), f32),
            [sems(1) for _ in range(4)],
        ]

    def both(height, dtype, times=layers):
        return [vmem((height, count), dtype) for _ in range(times)]

    first, middle, outer, bias, small, prior = params
    inputs = dict(
        mid=middle, first=first, out=outer, bias=bias, small=small, depth=depth, pixels=pixels, noise=noise, prior=prior
    )
    given = {
        name: pltpu.SMEM(a.shape, a.dtype) if a is depth else vmem(a.shape, a.dtype) for name, a in inputs.items()
    }
    early = 16 * layers + 8
    scratch = dict(
        given=given,
        load=pltpu.SemaphoreType.DMA((len(inputs),)),
        wmid=vmem((layers, hid, hid), bf16),
        wsmall=vmem((layers, hid, SMALL), bf16),
        wmt=vmem((layers, hid, hid), bf16),
        wst=vmem((layers, SMALL, hid), bf16),
        win=vmem((layers, hid, 128), bf16),
        bone=vmem((layers, hid, 128), f32),
        mixes=vmem((layers, 14, 16, 128), f32),
        mixes_back=vmem((layers, 12, 16, 128), f32),
        prior_fwd=vmem((32, 256), bf16),
        prior_back=vmem((144, 32), bf16),
        masks=vmem((4, 8, TILE), f32),
        gz=vmem((16, count), f32),
        gy=vmem((16, count), f32),
        d3=vmem((OUT, count), bf16),
        tbuf=vmem((OUT, TILE), f32),
        stat_acc=vmem((2, 16, 128), f32),
        like_acc=vmem((8, 128), f32),
        prior_acc=vmem((32, 256), f32),
        small_acc=vmem((layers, 32, 128), f32),
        sum_acc=vmem((layers, 2, 16, 128), f32),
        acc_in=vmem((hid, 128), f32),
        bone_acc=[vmem((hid, 128), f32) for _ in range(layers)],
        acc_rest=[vmem((hid, 128), f32) for _ in range(layers)],
        x=both(16, f32, layers + 1),
        keep=both(16, f32),
        taps=both(80, bf16),
        one=both(hid, bf16),
        two=both(hid, bf16),
        stat=[vmem((wide * narrow, 1, 128), f32), sems(1)],
        late=[vmem((wide * narrow, 2, 128), f32), sems(1)],
        early=[
            [vmem((size, early, 128), f32) for size in (wide, narrow)],
            [sems(1) for _ in range(2)],
        ],
        mid=[group(hid) for _ in range(layers)],
        out=[group(128) for _ in range(layers)],
        inn=[group(128, layer > 0) for layer in range(layers)],
        spread=[sems(2 * chips) for _ in range(2)],
        later=[[sems(1) for _ in range(layers)] for _ in range(2)],
    )
    like = jax.ShapeDtypeStruct
    grads = dict(
        found=like((layers, share, hid + SMALL), f32),
        sums=like((early + 16, 128), f32),
    )
    order = jax.tree.structure((inputs, grads, scratch))
    remote = dict(collective_id=0, has_side_effects=True) if wide > 1 else {}
    given_leaves, grad_leaves = jax.tree.leaves(inputs), jax.tree.leaves(grads)
    found = pl.pallas_call(
        functools.partial(flow_kernel, wide, narrow, order),
        out_shape=tuple(grad_leaves),
        in_specs=[HBM] * len(given_leaves),
        out_specs=(VMEM,) * len(grad_leaves),
        scratch_shapes=jax.tree.leaves(scratch),
        compiler_params=pltpu.CompilerParams(vmem_limit_bytes=FLOW_VMEM, **remote),
        name="flow",
    )(*given_leaves)
    found = SimpleNamespace(**jax.tree.unflatten(jax.tree.structure(grads), found))
    total = count * wide * narrow
    shapes = [like((1, 1), f32)] + [like(p.shape, f32) for p in params for _ in range(3)]
    results = pl.pallas_call(
        functools.partial(update_kernel, total, total // 256),
        out_shape=tuple(shapes),
        in_specs=[SMEM] + [VMEM] * 20,
        out_specs=(VMEM,) * 19,
        compiler_params=pltpu.CompilerParams(vmem_limit_bytes=UPDATE_VMEM),
        name="update",
    )(step_count.reshape(1), found.found, found.sums, *params, *firsts, *seconds)
    updated = [turn(results[1 + k :: 3], True) for k in range(3)]
    return (results[0].reshape(()),) + tuple(updated[k][p] for p in range(6) for k in range(3))


def solution(mesh):
    pixels = P(None, (NARROW, WIDE))
    rows, columns = P(None, WIDE, None), P(None, None, WIDE)
    weights = (rows, rows, columns, columns, P(), P())
    return jax.shard_map(
        functools.partial(shards, wide=mesh.shape[WIDE], narrow=mesh.shape[NARROW]),
        mesh=mesh,
        in_specs=(pixels, pixels, P((NARROW, WIDE)), P()) + weights * 3,
        out_specs=(P(),) + tuple(w for w in weights for _ in range(3)),
        check_vma=False,
    )
```

```python
import functools
import math
from types import SimpleNamespace

import jax
import jax.numpy as jnp
from jax import lax
from jax.experimental import pallas as pl
from jax.experimental.pallas import tpu as pltpu
from jax.sharding import PartitionSpec as P

f32 = jnp.float32
bf16 = jnp.bfloat16
highest = lax.Precision.HIGHEST
MESH = pl.DeviceIdType.MESH
learn_rate = 0.02
beta_one = 0.9
beta_two = 0.999
epsilon = 1e-08
decay_rate = 0.01
penalty_weight = 0.5
tap_offsets = [(r, c) for r in (-1, 0, 1) for c in (-1, 0, 1)]
TILE = 2048
FLOW_VMEM = 62 * 1024 * 1024
UPDATE_VMEM = 60 * 1024 * 1024
OUT = 144
SMALL = 256
VMEM = pl.BlockSpec(memory_space=pltpu.VMEM)
SMEM = pl.BlockSpec(memory_space=pltpu.SMEM)
HBM = pl.BlockSpec(memory_space=pl.ANY)
WIDE, NARROW = "wide", "narrow"


def dot(a, b, precision=None):
    return lax.dot_general(
        a, b, (((1,), (0,)), ((), ())), preferred_element_type=f32, precision=precision
    )


def dot_nt(a, b, precision=None):
    return lax.dot_general(
        a, b, (((1,), (1,)), ((), ())), preferred_element_type=f32, precision=precision
    )


def dot_tn(a, b, precision=None):
    return lax.dot_general(
        a, b, (((0,), (0,)), ((), ())), preferred_element_type=f32, precision=precision
    )


def iota(shape, axis):
    return lax.broadcasted_iota(jnp.int32, shape, axis)


def slot(s):
    return s + 2 * ((s * 10923) >> 16)


def spread(count, width, first=0):
    return jnp.where(slot(iota((count, width), 0) + first) == iota((count, width), 1), 1.0, 0.0)


def spread_rows(height, count):
    return jnp.where(slot(iota((height, count), 1)) == iota((height, count), 0), 1.0, 0.0)


def split_two(v):
    high = v.astype(bf16).astype(f32)
    return high, v - high


def as_row(column):
    n = column.shape[0]
    eye = iota((n, n), 0) == iota((n, n), 1)
    return jnp.sum(jnp.where(eye, column, 0.0), axis=0, keepdims=True)


def as_column(row):
    n = row.shape[1]
    eye = iota((n, n), 0) == iota((n, n), 1)
    return jnp.sum(jnp.where(eye, row, 0.0), axis=1, keepdims=True)


def mixing_parts(lu):
    n = lu.shape[0]
    row, col = iota((n, n), 0), iota((n, n), 1)
    lower = jnp.where(row > col, lu, 0.0) + jnp.where(row == col, 1.0, 0.0)
    upper = jnp.where(row < col, lu, 0.0) + jnp.where(row == col, jnp.exp(lu), 0.0)
    return lower, upper


def wide_rows(v, lanes):
    return jnp.concatenate([v] * (lanes // 128), axis=1)


class Shifts:
    def __init__(self, mask_ref, lanes):
        self.lanes = lanes
        self.masks = mask_ref

    def mask(self, which, rows):
        m = self.masks[which, :, 0 : self.lanes]
        return jnp.concatenate([m] * (rows // 8), axis=0) if rows > 8 else m

    def col(self, v, c):
        if c == 0:
            return v
        moved = pltpu.roll(v, (-c) % self.lanes, 1)
        return moved * self.mask(0 if c > 0 else 1, v.shape[0])

    def row(self, v, r):
        if r == 0:
            return v
        moved = pltpu.roll(v, (-16 * r) % self.lanes, 1)
        return moved * self.mask(2 if r > 0 else 3, v.shape[0])

    def taps(self, v, sign=1):
        by_col = {c: self.col(v, c) for c in (-1, 0, 1)}
        return [self.row(by_col[sign * c], sign * r) for r, c in tap_offsets]

    def fold(self, pieces, sign=1):
        total = None
        for c in (-1, 0, 1):
            part = None
            for r in (-1, 0, 1):
                piece = self.row(pieces[3 * (r + 1) + (c + 1)], sign * r)
                part = piece if part is None else part + piece
            part = self.col(part, sign * c)
            total = part if total is None else total + part
        return total


def fill_masks(mask_ref):
    lanes = mask_ref.shape[2]
    pos = iota((8, lanes), 1)
    row, col = (pos >> 4) & 15, pos & 15
    for which, keep in enumerate((col < 15, col > 0, row < 15, row > 0)):
        mask_ref[which] = jnp.where(keep, 1.0, 0.0)


def flow_kernel(wide, narrow, tree, *refs):
    hbm, grads, at = (SimpleNamespace(**part) for part in jax.tree.unflatten(tree, refs))
    wmid, wsmall, wmt, wst, win = at.wmid, at.wsmall, at.wmt, at.wst, at.win
    bone, mixes, mixes_back = at.bone, at.mixes, at.mixes_back
    gz, gy_ref, d3, tbuf = at.gz, at.gy, at.d3, at.tbuf
    given = SimpleNamespace(**at.given)
    layers, share, hid = given.mid.shape
    count = given.pixels.shape[1]
    total = count * wide * narrow
    coeff = -1.0 / (total * 12 * math.log(2.0))
    chips = max(wide // 2, 1)
    me_w = lax.axis_index(WIDE) if wide > 1 else 0
    me_n = lax.axis_index(NARROW) if narrow > 1 else 0
    chip, core = (me_w // 2, lax.rem(me_w, 2)) if wide > 1 else (0, 0)
    shifts = Shifts(at.masks, TILE)

    def block(index):
        return pl.ds(pl.multiple_of(index * share, share), share)

    def tile_at(t):
        return pl.ds(pl.multiple_of(t * TILE, TILE), TILE)

    def ahead(size, me, d):
        return lax.rem(me + d, size)

    def behind(size, me, d):
        return lax.rem(me + size - d, size)

    def each(first, size, fn):
        if wide > 1 and size > first:
            lax.fori_loop(first, size, lambda d, c: (fn(d), c)[1], 0)

    def remote(src, dst, sems, index, device):
        return pltpu.make_async_remote_copy(
            src_ref=src,
            dst_ref=dst,
            send_sem=sems[0].at[index],
            recv_sem=sems[1].at[index],
            device_id=device,
            device_id_type=MESH,
        )

    def drain(ref, sem):
        if wide > 1:
            pltpu.make_async_copy(ref, ref, sem.at[0]).wait()

    class Exchange:
        def __init__(self, bufs, sems):
            self.bufs, self.sems = bufs, sems

        def copy(self, phase, d):
            axis, size, me = ((WIDE, wide, me_w), (NARROW, narrow, me_n))[phase]
            row = self.bufs[phase].at[me]
            return remote(row, row, self.sems[phase], 0, {axis: ahead(size, me, d)})

        def start(self, phase, value):
            me, size = ((me_w, wide), (me_n, narrow))[phase]
            self.bufs[phase][me] = value
            each(1, size, lambda d: self.copy(phase, d).start())

        def finish(self, phase):
            size = (wide, narrow)[phase]
            if size > 1:
                for sem in self.sems[phase]:
                    drain(self.bufs[phase].at[1:size], sem)
            value = self.bufs[phase][0]
            for k in range(1, size):
                value = value + self.bufs[phase][k]
            return value

        def hop(self):
            self.start(1, self.finish(0))

    class OneShot:
        def __init__(self, rows, sems):
            self.rows, self.sems = rows, sems

        def copy(self, d):
            by_n, by_w = d // wide, lax.rem(d, wide)
            row = self.rows.at[me_n * wide + me_w]
            device = {NARROW: ahead(narrow, me_n, by_n), WIDE: ahead(wide, me_w, by_w)}
            return remote(row, row, self.sems, 0, device)

        def start(self, value):
            self.rows[me_n * wide + me_w] = value
            each(1, wide * narrow, lambda d: self.copy(d).start())

        def finish(self):
            if wide > 1:
                for sem in self.sems:
                    drain(self.rows.at[1 : wide * narrow], sem)
            return lax.fori_loop(
                0, wide * narrow, lambda k, c: c + self.rows[k], jnp.zeros(self.rows.shape[1:], f32)
            )

    stat, late = OneShot(*at.stat), OneShot(*at.late)
    early = Exchange(*at.early)

    class Group:
        def __init__(self, refs):
            self.full, self.pair, self.chip, self.part, self.out = refs[0:5]
            self.sems = refs[5]
            self.piece = self.part.shape[1]
            self.scatter = self.piece < share
            self.stage = 0
            self.last = 3 if self.scatter else 2

        def mine(self, index):
            return pl.ds(pl.multiple_of(index * self.piece, 8), self.piece)

        def start(self):
            sems = self.sems[self.stage]
            if self.stage == 0:
                if wide > 1:
                    theirs = self.full.at[:, 1 - core]
                    remote(theirs, self.pair, sems, 0, {WIDE: me_w + 1 - 2 * core}).start()
                return

            def go(d):
                if self.stage == 1:
                    to = ahead(chips, chip, d)
                    remote(self.full.at[to, core], self.chip.at[d - 1], sems, 0, {WIDE: 2 * to + core}).start()
                    return
                to = ahead(narrow, me_n, d)
                if self.stage == 2 and self.scatter:
                    rows = self.full.at[chip, core, self.mine(to)]
                    remote(rows, self.part.at[d - 1], sems, 0, {NARROW: to}).start()
                    return
                ref = self.part.at[me_n] if self.stage == 2 else self.out.at[self.mine(me_n)]
                remote(ref, ref, sems, 0, {NARROW: to}).start()

            each(1, chips if self.stage == 1 else narrow, go)

        def finish(self):
            if self.stage == 0:
                come = self.pair
            elif self.stage == 1:
                come = self.chip.at[0 : chips - 1] if chips > 1 else None
            elif self.stage == 2:
                come = self.part.at[0 : narrow - 1] if narrow > 1 else None
            else:
                come = self.out.at[0 : (narrow - 1) * self.piece] if narrow > 1 else None
            if come is not None:
                for sem in self.sems[self.stage]:
                    drain(come, sem)
            own = (chip, core)
            if self.stage == 0:

                def add(d):
                    self.full[d, core] += self.pair[d]

                each(0, chips, add)
            if self.stage == 1:
                value = self.full[own]
                for d in range(chips - 1):
                    value = value + self.chip[d]
                if self.scatter:
                    self.full[own] = value
                else:
                    self.part[me_n] = value
            if self.stage == 2:
                value = self.full[chip, core, self.mine(me_n)] if self.scatter else self.part[0]
                for d in range(0 if self.scatter else 1, narrow - 1 if self.scatter else narrow):
                    value = value + self.part[d]
                self.out[self.mine(me_n) if self.scatter else slice(None)] = value
            self.stage += 1

        def put(self, value):
            self.full[...] = value.reshape(self.full.shape)

        def add(self, value):
            self.full[...] += value.reshape(self.full.shape)

        def advance(self):
            self.finish()
            if self.stage <= self.last:
                self.start()

    mid, out, inn = ([Group(refs) for refs in kind] for kind in (at.mid, at.out, at.inn))

    if wide > 1:
        barrier = pltpu.get_barrier_semaphore()
        each(
            1,
            wide * narrow,
            lambda d: pl.semaphore_signal(
                barrier,
                inc=1,
                device_id={
                    NARROW: behind(narrow, me_n, (wide * narrow - d) // wide),
                    WIDE: behind(wide, me_w, lax.rem(wide * narrow - d, wide)),
                },
                device_id_type=MESH,
            ),
        )
    loads = {
        name: pltpu.make_async_copy(source_ref, at.given[name], at.load.at[k])
        for k, (name, source_ref) in enumerate(vars(hbm).items())
    }
    for copy in loads.values():
        copy.start()
    loads = SimpleNamespace(**loads)

    place = spread(164, SMALL).astype(bf16)
    for copy in (loads.mid, loads.first, loads.out, loads.bias):
        copy.wait()
    for layer in range(layers):
        small_part = (
            dot(given.out[layer].astype(bf16), place[0:108])
            + dot_tn(given.first[:, layer, :].astype(bf16), place[108:162])
            + dot_tn(given.bias[layer].astype(bf16), place[162:164])
        )
        wmid[layer, block(me_w)] = given.mid[layer].astype(bf16)
        wsmall[layer, block(me_w)] = small_part.astype(bf16)

    class Spread:
        def __init__(self, weights, sems):
            self.weights, self.sems = weights, sems

        def to_chip(self, d, coming=False):
            index = 2 * (behind(chips, chip, d) if coming else chip) + core
            rows = self.weights.at[0, block(index)]
            return remote(rows, rows, self.sems, d, {WIDE: 2 * ahead(chips, chip, d) + core})

        def to_core(self, d, coming=False):
            index = 2 * behind(chips, chip, d) + (1 - core if coming else core)
            rows = self.weights.at[0, block(index)]
            return remote(rows, rows, self.sems, chips + d, {WIDE: me_w + 1 - 2 * core})

        def start(self):
            each(1, chips, lambda d: self.to_chip(d).start())
            each(0, 1, lambda d: self.to_core(d).start())

        def pass_on(self):
            def one(d):
                self.to_chip(d).wait_send()
                self.to_chip(d, True).wait_recv()
                self.to_core(d).start()

            each(1, chips, one)

        def finish(self):
            def one(d):
                self.to_core(d).wait_send()
                self.to_core(d, True).wait_recv()

            each(0, chips, one)

    spread_small, spread_mid = Spread(wsmall, at.spread[0]), Spread(wmid, at.spread[1])

    def to_all(weights, sems, layer, d):
        rows = weights.at[layer, block(me_w)]
        return remote(rows, rows, sems[layer], 0, {WIDE: ahead(wide, me_w, d)})

    later = ((wsmall, at.later[0]), (wmid, at.later[1]))

    if wide > 1:
        pl.semaphore_wait(barrier, wide * narrow - 1)
        spread_small.start()
        spread_mid.start()

    fill_masks(at.masks)
    loads.small.wait()
    to_slots = spread_rows(16, 12)
    reverse = jnp.where(slot(11 - iota((16, 12), 1)) == iota((16, 12), 0), 1.0, 0.0)
    for layer in range(layers):
        small = given.small[:, layer, :]
        lower, upper = mixing_parts(small[:, 0:12])
        scale = jnp.exp(small[:, 13:14])
        mixed = dot(reverse, dot(lower, upper, highest), highest) * as_row(scale)
        const = jnp.sum(mixed * as_row(small[:, 12:13]), axis=1, keepdims=True)
        cb = jnp.sum(to_slots * as_row(small[:, 14:15]), axis=1, keepdims=True)
        for c in range(12):
            mixes[layer, c] = jnp.broadcast_to(mixed[:, c : c + 1], (16, 128))
        mixes[layer, 12] = jnp.broadcast_to(const, (16, 128))
        mixes[layer, 13] = jnp.broadcast_to(cb, (16, 128))
        if layer:
            back = dot_nt(to_slots, mixed, highest)
            for c in range(12):
                s = c + 2 * (c // 6)
                mixes_back[layer, c] = jnp.broadcast_to(back[:, s : s + 1], (16, 128))

    def by_lanes(v):
        parts = [v[:, 128 * k : 128 * k + 128] for k in range(v.shape[1] // 128)]
        while len(parts) > 1:
            parts = [a + b for a, b in zip(parts[0::2], parts[1::2])]
        return parts[0]

    real = jnp.where(iota((8, 128), 0) < 6, 1.0, 0.0)
    first_row = jnp.where(iota((8, TILE), 0) == 0, 1.0, 0.0)

    def enter(layer, here, x):
        at.x[layer][:, here] = x
        y = wide_rows(mixes[layer, 12], TILE)
        for c in range(12):
            s = c + 2 * (c // 6)
            y = y + wide_rows(mixes[layer, c], TILE) * x[s : s + 1, :]
        taps = jnp.concatenate(shifts.taps(y[0:8]) + [first_row], axis=0)
        at.taps[layer][:, here] = taps.astype(bf16)
        at.x[layer + 1][0:8, here] = y[0:8]
        at.keep[layer][0:8, here] = y[8:16]

    def pixels_in(t, carry):
        images = TILE // 256
        blank = jnp.zeros((2, 256), f32)
        chunks = []
        for k in range(images):
            coarse = given.depth[t * images + k] == 5
            by = jnp.where(coarse, 3, 0)
            level = jnp.where(coarse, 1.0 / 32.0, 1.0 / 256.0).astype(f32)
            at_image = pl.ds(pl.multiple_of(t * TILE + k * 256, 256), 256)
            quant = lax.shift_right_logical(given.pixels[:, at_image], jnp.broadcast_to(by, (12, 256)))
            x = (quant.astype(f32) + given.noise[:, at_image]) * level - 0.5
            chunks.append(jnp.concatenate([x[0:6], blank, x[6:12], blank], axis=0))
        enter(0, tile_at(t), jnp.concatenate(chunks, axis=1))
        return carry

    tiles = count // TILE
    half = tiles // 2

    def run(first, end, body):
        lax.fori_loop(first, end, lambda t, c: (body(t), c)[1], 0)

    def piped(first, end, lead, follow):
        lead(first)

        def both(t):
            follow(t - 1)
            lead(t)

        run(first + 1, end, both)
        follow(end - 1)

    for copy in (loads.depth, loads.pixels, loads.noise, loads.prior):
        copy.wait()
    lax.fori_loop(0, tiles, pixels_in, 0)
    spread_small.pass_on()

    prior = given.prior[...]
    s = iota((55, 256), 0)
    lane = iota((55, 256), 1)
    hit = (slot(s) == lane) | (slot(s) + 72 == lane)
    to_taps = jnp.where(((s < 54) & hit) | ((s == 54) & (lane == 144)), 1.0, 0.0)
    prior_slots = dot(to_slots, prior, highest)
    parts = split_two(dot(prior_slots, to_taps, highest))
    at.prior_fwd[...] = jnp.concatenate(parts, axis=0).astype(bf16)
    turned = dot_nt(spread_rows(72, 55), prior_slots, highest)
    stacked = jnp.concatenate(split_two(turned), axis=0)
    again = jnp.where((iota((16, 32), 1) & 15) == iota((16, 32), 0), 1.0, 0.0)
    at.prior_back[...] = dot(stacked.astype(bf16), again.astype(bf16)).astype(bf16)

    whole = [group.full for group in mid + out]
    sums = [at.stat_acc, at.like_acc, at.prior_acc, at.small_acc, at.sum_acc, at.acc_in]
    for ref in whole + sums + at.bone_acc + at.acc_rest:
        ref[...] = jnp.zeros_like(ref)

    pick = jnp.where(iota((SMALL, 128), 0) == iota((SMALL, 128), 1) + OUT, 1.0, 0.0).astype(bf16)

    def derive(layer):
        w = wsmall[layer]
        win[layer] = dot(w, pick).astype(bf16)
        wst[layer] = w.T
        bone[layer] = jnp.broadcast_to(w[:, 217:218].astype(f32), (hid, 128))

    def hidden_first(layer, t):
        here = tile_at(t)
        first = dot(win[layer, :, 0:80], at.taps[layer][:, here]).astype(bf16)
        h1 = jnp.maximum(first, jnp.zeros_like(first))
        at.one[layer][:, here] = h1
        return h1

    def forward_products(layer, t):
        here = tile_at(t)
        h1 = hidden_first(layer, t) if layer else at.one[0][:, here]
        second = dot(wmid[layer], h1) + wide_rows(bone[layer], TILE)
        h2 = jnp.maximum(second, 0.0).astype(bf16)
        at.two[layer][:, here] = h2
        tbuf[...] = dot(wst[layer, 0:OUT, :], h2)

    def forward_rest(layer, t):
        here = tile_at(t)
        o = shifts.fold([tbuf[16 * k : 16 * k + 16] for k in range(9)])
        o = o + wide_rows(mixes[layer, 13], TILE)
        v = at.keep[layer][0:8, here] + o[0:8]
        u = o[8:16] + 2.0
        decay = jnp.exp(-jnp.abs(u))
        q = jnp.where(u >= 0.0, 1.0, decay) / (1.0 + decay)
        at.like_acc[...] += by_lanes(jnp.minimum(u, 0.0) - jnp.log(1.0 + decay)) * real
        at.keep[layer][0:8, here] = v
        at.keep[layer][8:16, here] = q
        x = jnp.concatenate([at.x[layer + 1][0:8, here], v * q], axis=0)
        if layer < layers - 1:
            enter(layer + 1, here, x)
        else:
            at.x[layer + 1][8:16, here] = x[8:16]
            at.stat_acc[0] += by_lanes(x)
            at.stat_acc[1] += by_lanes(x * x)

    spread_small.finish()
    for layer in range(1, layers):
        for weights, sems in later:
            each(1, wide, lambda d: to_all(weights, sems, layer, d).start())
    derive(0)
    run(0, half, functools.partial(hidden_first, 0))
    spread_mid.pass_on()
    run(half, tiles, functools.partial(hidden_first, 0))
    spread_mid.finish()
    for layer in range(layers):
        if layer:
            for weights, sems in later:

                if wide > 1:
                    for sem in sems[layer]:
                        drain(weights.at[layer, 0 : (wide - 1) * share], sem)
            derive(layer)
        piped(0, tiles, functools.partial(forward_products, layer), functools.partial(forward_rest, layer))

    lane = iota((16, 128), 1)

    line = iota((16, 128), 0)
    row = jnp.where(lane == line, jnp.sum(at.stat_acc[0], axis=1, keepdims=True), 0.0)
    row = row + jnp.where(lane == line + 16, jnp.sum(at.stat_acc[1], axis=1, keepdims=True), 0.0)
    stat.start(jnp.sum(row, axis=0, keepdims=True))

    def prior_tile(t):
        here = tile_at(t)
        z1 = at.x[layers][0:8, here]
        z2 = at.x[layers][8:16, here]
        pieces = [split_two(v) for v in shifts.taps(z1)]
        tz = jnp.concatenate(
            [p[0] for p in pieces] + [p[1] for p in pieces] + [first_row, jnp.zeros_like(first_row)], axis=0
        ).astype(bf16)
        both = dot(at.prior_fwd[:, 0:160], tz)
        value = both[0:16] + both[16:32]
        centre, log_sd = value[0:8], value[8:16]
        inverse = jnp.exp(-log_sd)
        ratio = (z2 - centre) * inverse
        at.like_acc[...] += by_lanes(-0.5 * z1 * z1 - 0.5 * ratio * ratio - log_sd)
        d_centre = ratio * inverse
        d_stat = jnp.concatenate([d_centre, ratio * ratio - 1.0], axis=0)
        ds = jnp.concatenate(split_two(d_stat), axis=0).astype(bf16)
        at.prior_acc[:, 0:160] += dot_nt(ds, tz)
        dt = dot(at.prior_back[...], ds)
        dt = dt[0:72] + dt[72:144]
        folded = shifts.fold([dt[8 * k : 8 * k + 8] for k in range(9)], -1)
        gz[0:8, here] = coeff * (folded - z1)
        gz[8:16, here] = -coeff * d_centre

    run(0, tiles, prior_tile)
    for layer in range(layers):
        wmt[layer] = wmid[layer].T
    stats = stat.finish()
    mean = jnp.sum(jnp.where(lane == line, stats, 0.0), axis=1, keepdims=True) / total
    square = jnp.sum(jnp.where(lane == line + 16, stats, 0.0), axis=1, keepdims=True) / total
    var = square - mean * mean
    from_first = penalty_weight * (2.0 * mean - 4.0 * (var - 1.0) * mean) / total
    from_square = penalty_weight * 2.0 * (var - 1.0) / total
    ones_rows = jnp.where((iota((16, 1), 0) & 7) < 6, 1.0, 0.0)
    penalty = penalty_weight * jnp.sum(
        ones_rows * (mean * mean + (var - 1.0) * (var - 1.0)), axis=0, keepdims=True
    )

    def prepare_back(layer, here, g):
        v = at.keep[layer][0:8, here]
        q = at.keep[layer][8:16, here]
        gbq = g[8:16] * q
        gy_ref[0:8, here] = g[0:8]
        gy_ref[8:16, here] = gbq
        do = jnp.concatenate([gbq, (gbq * v + coeff) * (1.0 - q)], axis=0)
        at.sum_acc[layer, 1] += by_lanes(do)
        rounded = do.astype(bf16).astype(f32)
        d3[:, here] = jnp.concatenate(shifts.taps(rounded, -1), axis=0).astype(bf16)

    def last_gradient(t):
        here = tile_at(t)
        g = gz[:, here] + from_first + 2.0 * at.x[layers][:, here] * from_square
        prepare_back(layers - 1, here, g)

    def back_a(layer, t):
        here = tile_at(t)
        h2 = at.two[layer][:, here]
        taps = d3[:, here]
        grad = dot_nt(h2, taps)
        out[layer].add(grad[:, 0:128])
        at.acc_rest[layer][:, 0:16] += grad[:, 128:OUT]
        dd2 = dot(wsmall[layer, :, 0:OUT], taps).astype(bf16)
        at.two[layer][:, here] = jnp.where(h2 > 0, dd2, jnp.zeros_like(dd2))

    def back_b(layer, t):
        here = tile_at(t)
        d2 = at.two[layer][:, here]
        mid[layer].add(dot_nt(d2, at.one[layer][:, here]))
        at.bone_acc[layer][...] += by_lanes(d2.astype(f32))

    def back_c(layer, t):
        here = tile_at(t)
        dd1 = dot(wmt[layer], at.two[layer][:, here]).astype(bf16)
        h1 = at.one[layer][:, here]
        at.one[layer][:, here] = jnp.where(h1 > 0, dd1, jnp.zeros_like(dd1))

    def back_in(layer, t):
        here = tile_at(t)
        at.acc_in[:, 0:80] += dot_nt(at.one[layer][:, here], at.taps[layer][:, here])

    def back_taps(layer, t):
        tbuf[0:80] = dot(wst[layer, OUT : OUT + 80, :], at.one[layer][:, tile_at(t)])

    def back_rest(layer, t):
        here = tile_at(t)
        gya = gy_ref[0:8, here] + shifts.fold([tbuf[8 * k : 8 * k + 8] for k in range(9)], -1)
        gy = jnp.concatenate([gya, gy_ref[8:16, here]], axis=0)
        at.sum_acc[layer, 0] += by_lanes(gy)
        left = jnp.concatenate(split_two(gy), axis=0).astype(bf16)
        right = jnp.concatenate(split_two(at.x[layer][:, here]), axis=0).astype(bf16)
        at.small_acc[layer, :, 0:32] += dot_nt(left, right)
        if layer:
            gx = wide_rows(mixes_back[layer, 0], TILE) * gy[0:1, :]
            for c in range(1, 12):
                s = c + 2 * (c // 6)
                gx = gx + wide_rows(mixes_back[layer, c], TILE) * gy[s : s + 1, :]
            prepare_back(layer - 1, here, gx)

    def inner_gradient(layer):
        column = jnp.sum(at.bone_acc[layer][...], axis=1, keepdims=True)
        grad = at.acc_rest[layer][...] + pltpu.roll(at.acc_in[...], 16, 1)
        inn[layer].put(grad + jnp.where(iota((hid, 128), 1) == 217 - 128, column, 0.0))
        if layer:
            at.acc_in[...] = jnp.zeros_like(at.acc_in)

    def moments(layer):
        acc = at.small_acc[layer]
        part = acc[0:16] + acc[16:32]
        moment = jnp.where(lane < 16, part + pltpu.roll(part, 112, 1), 0.0)
        for k in range(2):
            line = jnp.sum(at.sum_acc[layer, k], axis=1, keepdims=True)
            moment = moment + jnp.where(lane == 16 + k, line, 0.0)
        return moment

    def early_sums():
        acc = at.prior_acc[0:16] + at.prior_acc[16:32]
        taps_part = (acc + pltpu.roll(acc, 256 - 72, 1))[:, 0:128]
        last = pltpu.roll(acc, 256 - 72, 1)[:, 0:128]
        pieces = [moments(layer) for layer in range(1, layers)]
        pieces.append(jnp.where(lane < 72, taps_part, 0.0) + jnp.where(lane == 72, last, 0.0))
        depths = lax.fori_loop(0, given.depth.shape[0], lambda k, c: c + given.depth[k], jnp.int32(0))
        depths = jnp.broadcast_to(depths, (8, 128)).astype(f32)
        row8 = iota((8, 128), 0)
        logs = jnp.sum(at.like_acc[...], axis=0, keepdims=True)
        pieces.append(jnp.where(row8 == 0, logs, 0.0) + jnp.where(row8 == 1, depths, 0.0))
        return jnp.concatenate(pieces, axis=0)

    def go(*which):
        for group in which:
            group.advance()

    def loop(body, layer, first=0, end=tiles):
        run(first, end, functools.partial(body, layer))

    def rest_loop(layer, first, end):
        piped(first, end, functools.partial(back_taps, layer), functools.partial(back_rest, layer))

    def inner(layer):
        inner_gradient(layer)
        inn[layer].start()

    def packed(moment):
        value = jnp.zeros((2, 128), f32)
        for k in range(6):
            pair = jnp.concatenate([moment[k : k + 1], moment[8 + k : 9 + k]], axis=0)
            value = value + (pltpu.roll(pair, 20 * k, 1) if k else pair)
        return value

    def unpacked(value):
        blank = jnp.zeros((2, 128), f32)
        turns = [pltpu.roll(value, 128 - 20 * k, 1) if k else value for k in range(6)]
        rows = [turn[0:1] for turn in turns] + [blank] + [turn[1:2] for turn in turns] + [blank]
        return jnp.where(lane < 18, jnp.concatenate(rows, axis=0), 0.0)

    piped(0, tiles, last_gradient, functools.partial(back_a, 1))
    out[1].start()
    def lead(t):
        back_b(1, t)
        back_c(1, t)

    def follow(t):
        back_taps(1, t)
        back_rest(1, t)

    piped(0, tiles, lead, follow)
    mid[1].start()
    go(out[1])
    early.start(0, early_sums())
    loop(back_a, 0, 0, half)
    go(mid[1])
    loop(back_a, 0, half, tiles)
    out[0].start()
    go(out[1])
    early.hop()
    loop(back_b, 0)
    mid[0].start()
    go(mid[1], out[0], out[1])
    loop(back_in, 1, 0, half)
    go(mid[0])
    loop(back_in, 1, half, tiles)
    inner(1)
    early_total = early.finish(1)
    loop(back_c, 0, 0, half)
    go(inn[1], out[0], out[1])
    loop(back_c, 0, half, tiles)
    go(mid[1])
    loop(back_in, 0, 0, half)
    go(mid[0], inn[1])
    loop(back_in, 0, half, tiles)
    inner(0)
    go(out[0])
    rest_loop(0, 0, half)
    go(inn[0], mid[1])
    rest_loop(0, half, tiles)
    late.start(packed(moments(0)))
    go(mid[0], inn[1], inn[0], out[0])
    go(inn[1])
    late_total = unpacked(late.finish())
    whole = jnp.concatenate([late_total, early_total], axis=0)
    rows = whole.shape[0]
    grads.sums[...] = whole + jnp.where(iota((rows, 128), 0) == rows - 8 + 2, penalty, 0.0)

    def write(group, layer, first):
        ref = group[layer].out
        grads.found[layer, :, first : first + ref.shape[1]] = ref[...]

    write(mid, 1, 0)
    write(out, 0, hid)
    write(out, 1, hid)
    write(inn, 1, hid + 128)
    go(mid[0], inn[0])
    write(mid, 0, 0)
    write(inn, 0, hid + 128)


def adamw(weight, grad, first, second, fixes):
    first_new = beta_one * first + (1.0 - beta_one) * grad
    second_new = beta_two * second + (1.0 - beta_two) * grad * grad
    update = first_new * fixes[0] / (jnp.sqrt(second_new * fixes[1]) + epsilon) + decay_rate * weight
    return (weight - learn_rate * update, first_new, second_new)


def update_kernel(total, images, step_ref, grad_ref, sums_ref, *refs):
    weights, firsts, seconds, loss_ref, outs = refs[0:6], refs[6:12], refs[12:18], refs[18], refs[19:]
    layers, share, _ = grad_ref.shape
    hid = weights[1].shape[2]
    coeff = -1.0 / (total * 12 * math.log(2.0))
    power = iota((8, 128), 1)
    used = power < jnp.broadcast_to(step_ref[0], (8, 128))
    fixes = tuple(
        1.0
        / (
            (1.0 - beta)
            * jnp.sum(
                jnp.where(used, jnp.exp(power.astype(f32) * math.log(beta)), 0.0), axis=1, keepdims=True
            )[0:1]
        )
        for beta in (beta_one, beta_two)
    )

    def write(which, at, grad):
        new = adamw(weights[which][at], grad, firsts[which][at], seconds[which][at], fixes)
        for k in range(3):
            outs[3 * which + k][at] = new[k]

    def column(layer):
        return (slice(None), layer, slice(None))

    place = spread(164, SMALL)
    to_slots = spread_rows(16, 12)
    reverse = jnp.where(slot(11 - iota((16, 12), 1)) == iota((16, 12), 0), 1.0, 0.0)
    row, col = iota((12, 12), 0), iota((12, 12), 1)
    eye = row == col
    logdet = jnp.zeros((1, 1), f32)
    for layer in range(layers):
        write(1, layer, grad_ref[layer, :, 0:hid])
        part = grad_ref[layer, :, hid : hid + SMALL]
        write(0, column(layer), dot_nt(place[108:162], part, highest))
        write(2, layer, dot_nt(part, place[0:108], highest))
        write(3, layer, dot_nt(place[162:164], part, highest))
        small = weights[4][column(layer)]
        lu = small[:, 0:12]
        lower, upper = mixing_parts(lu)
        scale = jnp.exp(small[:, 13:14])
        scale_row = as_row(scale)
        sums = sums_ref[16 * layer : 16 * layer + 16]
        turned = dot_tn(reverse, sums, highest)
        moment = dot(turned[:, 0:16], to_slots, highest)
        ones = turned[:, 16:17]
        g_mix = (moment + ones * as_row(small[:, 12:13])) * scale_row
        mix = dot(lower, upper, highest)
        g_bias = scale * dot_tn(mix, ones, highest)
        g_scale = as_column(jnp.sum(mix * g_mix, axis=0, keepdims=True)) + coeff * total
        g_lower = dot_nt(g_mix, upper, highest)
        g_upper = dot_tn(lower, g_mix, highest)
        g_lu = jnp.where(row > col, g_lower, jnp.where(eye, g_upper * jnp.exp(lu) + coeff * total, g_upper))
        g_cb = dot_tn(to_slots, sums, highest)[:, 17:18]
        wide15 = iota((12, 15), 1)
        grad = dot(g_lu, jnp.where(iota((12, 15), 0) == wide15, 1.0, 0.0), highest)
        grad = jnp.where(wide15 == 12, g_bias, grad)
        grad = jnp.where(wide15 == 13, g_scale, grad)
        grad = jnp.where(wide15 == 14, g_cb, grad)
        write(4, column(layer), grad)
        diag = jnp.sum(jnp.where(eye, lu, 0.0), axis=0, keepdims=True) + as_row(small[:, 13:14])
        logdet = logdet + jnp.sum(diag, axis=1, keepdims=True)
    sums = sums_ref[16 * layers : 16 * layers + 16]
    grad = coeff * dot_nt(
        dot_tn(to_slots, sums, highest), spread(55, 128), highest
    )
    write(5, Ellipsis, grad)
    tail = sums_ref[16 * layers + 16 :]
    likely = jnp.sum(tail[0:1], axis=1, keepdims=True)
    likely = likely - total * 6.0 * math.log(2.0 * math.pi) + total * logdet
    loss_ref[...] = coeff * likely + tail[1:2, 0:1] / images + tail[2:3, 0:1]


def turn(arrays, back=False):
    orders = ((1, 2, 0) if back else (2, 0, 1), None, (0, 2, 1), None, (1, 0, 2), None)
    return tuple(a if o is None else jnp.transpose(a, o) for a, o in zip(arrays, orders))


def shards(*args, wide, narrow):
    pixels, noise, depth, step_count = args[0:4]
    params, firsts, seconds = turn(args[4:10]), turn(args[10:16]), turn(args[16:22])
    layers, share, hid = params[1].shape
    count = pixels.shape[1]
    chips = max(wide // 2, 1)
    vmem = pltpu.VMEM

    def sems(*shape):
        return [pltpu.SemaphoreType.DMA(shape) for _ in range(2)]

    def group(across, scatter=True):
        piece = share // narrow if scatter and share % (8 * narrow) == 0 else share
        return [
            vmem((chips, hid // share // chips, share, across), f32),
            vmem((chips, share, across), f32),
            vmem((chips, share, across), f32),
            vmem((narrow, piece, across), f32),
            vmem((share, across), f32),
            [sems(1) for _ in range(4)],
        ]

    def both(height, dtype, times=layers):
        return [vmem((height, count), dtype) for _ in range(times)]

    first, middle, outer, bias, small, prior = params
    inputs = dict(
        mid=middle, first=first, out=outer, bias=bias, small=small, depth=depth, pixels=pixels, noise=noise, prior=prior
    )
    given = {
        name: pltpu.SMEM(a.shape, a.dtype) if a is depth else vmem(a.shape, a.dtype) for name, a in inputs.items()
    }
    early = 16 * layers + 8
    scratch = dict(
        given=given,
        load=pltpu.SemaphoreType.DMA((len(inputs),)),
        wmid=vmem((layers, hid, hid), bf16),
        wsmall=vmem((layers, hid, SMALL), bf16),
        wmt=vmem((layers, hid, hid), bf16),
        wst=vmem((layers, SMALL, hid), bf16),
        win=vmem((layers, hid, 128), bf16),
        bone=vmem((layers, hid, 128), f32),
        mixes=vmem((layers, 14, 16, 128), f32),
        mixes_back=vmem((layers, 12, 16, 128), f32),
        prior_fwd=vmem((32, 256), bf16),
        prior_back=vmem((144, 32), bf16),
        masks=vmem((4, 8, TILE), f32),
        gz=vmem((16, count), f32),
        gy=vmem((16, count), f32),
        d3=vmem((OUT, count), bf16),
        tbuf=vmem((OUT, TILE), f32),
        stat_acc=vmem((2, 16, 128), f32),
        like_acc=vmem((8, 128), f32),
        prior_acc=vmem((32, 256), f32),
        small_acc=vmem((layers, 32, 128), f32),
        sum_acc=vmem((layers, 2, 16, 128), f32),
        acc_in=vmem((hid, 128), f32),
        bone_acc=[vmem((hid, 128), f32) for _ in range(layers)],
        acc_rest=[vmem((hid, 128), f32) for _ in range(layers)],
        x=both(16, f32, layers + 1),
        keep=both(16, f32),
        taps=both(80, bf16),
        one=both(hid, bf16),
        two=both(hid, bf16),
        stat=[vmem((wide * narrow, 1, 128), f32), sems(1)],
        late=[vmem((wide * narrow, 2, 128), f32), sems(1)],
        early=[
            [vmem((size, early, 128), f32) for size in (wide, narrow)],
            [sems(1) for _ in range(2)],
        ],
        mid=[group(hid) for _ in range(layers)],
        out=[group(128) for _ in range(layers)],
        inn=[group(128, layer > 0) for layer in range(layers)],
        spread=[sems(2 * chips) for _ in range(2)],
        later=[[sems(1) for _ in range(layers)] for _ in range(2)],
    )
    like = jax.ShapeDtypeStruct
    grads = dict(
        found=like((layers, share, hid + SMALL), f32),
        sums=like((early + 16, 128), f32),
    )
    order = jax.tree.structure((inputs, grads, scratch))
    remote = dict(collective_id=0, has_side_effects=True) if wide > 1 else {}
    given_leaves, grad_leaves = jax.tree.leaves(inputs), jax.tree.leaves(grads)
    found = pl.pallas_call(
        functools.partial(flow_kernel, wide, narrow, order),
        out_shape=tuple(grad_leaves),
        in_specs=[HBM] * len(given_leaves),
        out_specs=(VMEM,) * len(grad_leaves),
        scratch_shapes=jax.tree.leaves(scratch),
        compiler_params=pltpu.CompilerParams(vmem_limit_bytes=FLOW_VMEM, **remote),
        name="flow",
    )(*given_leaves)
    found = SimpleNamespace(**jax.tree.unflatten(jax.tree.structure(grads), found))
    total = count * wide * narrow
    shapes = [like((1, 1), f32)] + [like(p.shape, f32) for p in params for _ in range(3)]
    results = pl.pallas_call(
        functools.partial(update_kernel, total, total // 256),
        out_shape=tuple(shapes),
        in_specs=[SMEM] + [VMEM] * 20,
        out_specs=(VMEM,) * 19,
        compiler_params=pltpu.CompilerParams(vmem_limit_bytes=UPDATE_VMEM),
        name="update",
    )(step_count.reshape(1), found.found, found.sums, *params, *firsts, *seconds)
    updated = [turn(results[1 + k :: 3], True) for k in range(3)]
    return (results[0].reshape(()),) + tuple(updated[k][p] for p in range(6) for k in range(3))


def solution(mesh):
    pixels = P(None, (NARROW, WIDE))
    rows, columns = P(None, WIDE, None), P(None, None, WIDE)
    weights = (rows, rows, columns, columns, P(), P())
    return jax.shard_map(
        functools.partial(shards, wide=mesh.shape[WIDE], narrow=mesh.shape[NARROW]),
        mesh=mesh,
        in_specs=(pixels, pixels, P((NARROW, WIDE)), P()) + weights * 3,
        out_specs=(P(),) + tuple(w for w in weights for _ in range(3)),
        check_vma=False,
    )
```
